32 devices in a mesh: grid: 8 (over y, x, core), dom: 4 (over z).
Axes of the slice: x: 2, y: 2, z: 4, core: 2. Of those that a mesh axis runs over, the one named last changes fastest.
Arguments:
- concentration: float32 [8, 64, 8192], P('grid', 'dom'), may hold values from -6 to 6
- diffusion: float32 [8, 64, 8192], P('grid', 'dom'), may hold values from 0.25 to 1
- velocity: float32 [4], replicated, may hold values from -1 to 1
- levels: int32 [8, 3], P('grid'), may hold values from 3 to 7, as said below
- grid_signs: int32 [8], P('grid'), may hold values from -1 to 1, as said below
- owner_list: int32 [32, 128], P(('grid', 'dom')), may hold values from 0 to 31, as said below
- slot_list: int32 [32, 128], P(('grid', 'dom')), may hold values from 0 to 63
Outputs:
- combined: float32 [8, 64, 8192], P('grid', 'dom')
The draws below stay inside these ranges and needn't reach their ends.
Inputs may be any that keep to these rules, and one draw needn't show every extreme that they name: Each row's three levels sum to 13. `grid_signs`: each is -1 or 1. `owner_list`: at most 8 blocks of one device name the same owner; some owner is named by 8 blocks of every device.
All inputs are finite; a program needn't handle non-finite values.
Results may differ from the reference program's by a relative error of at most 0.0003.
Values sent between devices are 32-bit elements; how exact they have to be, the bound alone decides.
No kernel may reach another device: no remote copies, remote signals or barrier semaphores. Data moves between devices by JAX's collectives and lax.ppermute only.
A program may use at most 192 MiB of HBM per device.

```python
import math
import jax
import jax.numpy as jnp
from jax import lax

LR = 13
LMIN = 3
N4_DEV = 16
TSTEPS = 2
GPD = 1
BLK = 1024
ROWCELLS = 8192
N4 = 64
GRIDS = 8
NBLK = 128
CAP = 8
SLOTS = 64
N_GRID = 8
N_DOM = 4


def draw_levels(key, part):
    spare_levels = LR - 3 * LMIN
    first_key, second_key, third_key = jax.random.split(key, 3)
    first_extra = jax.random.randint(first_key, (GRIDS,), 0, spare_levels + 1)
    second_raw = jax.random.randint(second_key, (GRIDS,), 0, spare_levels + 1)
    second_extra = second_raw % (spare_levels - first_extra + 1)
    third_extra = spare_levels - first_extra - second_extra
    stacked = jnp.stack([first_extra, second_extra, third_extra], axis=1)
    rotation = jax.random.randint(third_key, (GRIDS, 1), 0, 3)
    columns = (jnp.arange(3)[None, :] + rotation) % 3
    rotated = jnp.take_along_axis(stacked, columns, axis=1)
    rotated = rotated.at[0].set(jnp.array([spare_levels, 0, 0], jnp.int32))
    return (rotated + LMIN).astype(jnp.int32)


def draw_grid_signs(key, part):
    picks = jax.random.randint(key, (GRIDS,), 0, 2)
    return (2 * picks - 1).at[0].set(1).at[1].set(-1).astype(jnp.int32)


def draw_owner_list(key, part):
    busy_key, rest_key = jax.random.split(key)
    busiest = jax.random.randint(busy_key, (), 0, N_GRID * N_DOM)

    def one_device(dev_key):
        perm_key, order_key = jax.random.split(dev_key)
        places = jax.random.permutation(perm_key, N_GRID * N_DOM * CAP)
        owners = places // CAP
        is_busy = (owners == busiest).astype(jnp.int32)
        ordering = jnp.argsort(is_busy, stable=True)
        others = owners[ordering][:NBLK - CAP]
        picked = jnp.concatenate([jnp.full((CAP,), busiest, jnp.int32), others.astype(jnp.int32)])
        return jax.random.permutation(order_key, picked)
    return jax.vmap(one_device)(jax.random.split(rest_key, N_GRID * N_DOM)).astype(jnp.int32)


def draw_slot_list(key, part):
    drawn = jax.random.randint(key, (N_GRID * N_DOM, NBLK), 0, SLOTS)
    return drawn.at[0, 0].set(SLOTS - 1).at[0, 1].set(0).astype(jnp.int32)


def level_of(stream_key, extent, cuts, smallest, top_value):
    loudness, own = 1.0, jax.random.fold_in(stream_key, 6)
    for axis_at, blocks in cuts:
        heights = jnp.exp(jax.random.uniform(jax.random.fold_in(own, axis_at), (blocks,), jnp.float32, smallest / len(cuts), top_value / len(cuts)))
        loudness = loudness * jnp.repeat(heights, extent[axis_at] // blocks).reshape([-1 if axis == axis_at else 1 for axis in range(len(extent))])
    return loudness


def scatter_about(rng, extent, width, most, cuts=(), kind=jnp.bfloat16):
    values = width * jax.random.normal(rng, extent, jnp.float32)
    if cuts:
        values = values * level_of(rng, extent, cuts, -0.22, 0.18)
    return jnp.clip(values, -most, most).astype(kind)


def setup_inputs(seed: int = 0) -> dict:
    key_list = jax.random.split(jax.random.key(seed), 8)
    return {
        "concentration": scatter_about(key_list[0], (GRIDS, N4, ROWCELLS), 1.0, 6.0, ((0, 8), (1, 4)), jnp.float32),
        "diffusion": jnp.clip(jnp.exp(math.log(1.0) - 1.3862944 * jax.random.uniform(key_list[1], (GRIDS, N4, ROWCELLS), jnp.float32) ** level_of(key_list[1], (GRIDS, N4, ROWCELLS), ((0, 8), (1, 4)), -0.2, 0.2)), 0.25, 1.0),
        "velocity": jnp.clip(jax.random.uniform(key_list[2], (4,), jnp.float32, -1.0, 1.0), -1.0, 1.0),
        "levels": draw_levels(jax.random.fold_in(key_list[7], 71), 0),
        "grid_signs": draw_grid_signs(jax.random.fold_in(key_list[7], 71), 0),
        "owner_list": draw_owner_list(jax.random.fold_in(key_list[7], 71), 0),
        "slot_list": draw_slot_list(jax.random.fold_in(key_list[7], 71), 0),
    }


def level_table():
    level_rows = []
    for first_level in range(LMIN, LR - 2 * LMIN + 1):
        for second_level in range(LMIN, LR - first_level - LMIN + 1):
            level_rows.append((first_level, second_level, LR - first_level - second_level))
    return level_rows


def branch_index(grid_levels):
    level_rows = jnp.array(level_table(), jnp.int32)
    matching = jnp.all(grid_levels[None, :] == level_rows, axis=1)
    return jnp.sum(jnp.where(matching, jnp.arange(level_rows.shape[0], dtype=jnp.int32), 0)).astype(jnp.int32)


def step_ahead(values, axis_num):
    length = values.shape[axis_num]
    shifted = lax.slice_in_dim(values, 1, length, axis=axis_num)
    return jnp.concatenate([shifted, jnp.zeros_like(lax.slice_in_dim(values, 0, 1, axis=axis_num))], axis=axis_num)


def behind(values, axis_num):
    length = values.shape[axis_num]
    shifted = lax.slice_in_dim(values, 0, length - 1, axis=axis_num)
    return jnp.concatenate([jnp.zeros_like(lax.slice_in_dim(values, 0, 1, axis=axis_num)), shifted], axis=axis_num)


def inner_terms(level_combo):
    def branch_fn(values, velocity):
        shaped = values.reshape(values.shape[0], 2 ** level_combo[2], 2 ** level_combo[1], 2 ** level_combo[0])
        second = jnp.zeros_like(shaped)
        drift = jnp.zeros_like(shaped)
        for direction in range(3):
            axis_num = 3 - direction
            ahead_vals = step_ahead(shaped, axis_num)
            before = behind(shaped, axis_num)
            second = second + (ahead_vals - 2.0 * shaped + before)
            drift = drift + velocity[direction] * (ahead_vals - before)
        return second.reshape(values.shape), drift.reshape(values.shape)
    return branch_fn


def hier_axis(values, axis_num):
    length = values.shape[axis_num]
    result = values
    for level_bit in range(length.bit_length() - 1):
        stride = 2 ** (level_bit + 1)
        before = lax.slice_in_dim(values, 0, length, stride, axis=axis_num)
        ahead_vals = lax.slice_in_dim(values, stride, length, stride, axis=axis_num)
        ahead_vals = jnp.concatenate([ahead_vals, jnp.zeros_like(lax.slice_in_dim(before, 0, 1, axis=axis_num))], axis=axis_num)
        position = [slice(None)] * values.ndim
        position[axis_num] = slice(2 ** level_bit, None, stride)
        result = result.at[tuple(position)].add(-0.5 * (before + ahead_vals))
    return result


def inner_surplus(level_combo):
    def branch_fn(values):
        shaped = values.reshape(values.shape[0], 2 ** level_combo[2], 2 ** level_combo[1], 2 ** level_combo[0])
        for axis_num in (3, 2, 1):
            shaped = hier_axis(shaped, axis_num)
        return shaped.reshape(values.shape)
    return branch_fn


def reference(concentration, diffusion, velocity, levels, grid_signs, owner_list, slot_list):
    level_rows = level_table()
    term_fns = [inner_terms(level_combo) for level_combo in level_rows]
    surplus_fns = [inner_surplus(level_combo) for level_combo in level_rows]

    def one_grid(operands):
        values, coefficient, grid_levels, grid_sign = operands
        branch = branch_index(grid_levels)
        for step_num in range(TSTEPS):
            second, drift = lax.switch(branch, term_fns, values, velocity)
            ahead_vals = step_ahead(values, 0)
            before = behind(values, 0)
            second = second + (ahead_vals - 2.0 * values + before)
            drift = drift + velocity[3] * (ahead_vals - before)
            values = values + 0.1 * coefficient * second - 0.1 * drift
        values = hier_axis(values, 0)
        values = lax.switch(branch, surplus_fns, values)
        return grid_sign.astype(jnp.float32) * values

    signed = lax.map(one_grid, (concentration, diffusion, levels, grid_signs))
    blocks = signed.reshape(N_GRID, GPD, N_DOM, N4_DEV, ROWCELLS).transpose(0, 2, 1, 3, 4).reshape(N_GRID * N_DOM * NBLK, BLK)
    targets = (owner_list * SLOTS + slot_list).reshape(-1).astype(jnp.int32)
    pieces = jax.ops.segment_sum(blocks, targets, num_segments=N_GRID * N_DOM * SLOTS)
    returned = pieces[targets]
    return returned.reshape(N_GRID, N_DOM, GPD, N4_DEV, ROWCELLS).transpose(0, 2, 1, 3, 4).reshape(GRIDS, N4, ROWCELLS)
```

```python
import functools

import jax
import jax.numpy as jnp
from jax import lax
from jax.experimental import pallas as pl
from jax.experimental.pallas import tpu as pltpu
from jax.sharding import PartitionSpec as P

LR = 13
BLK = 1024
SLOTS = 64
LANES = 128
TILES = 2**LR // LANES
PAD = 9
VMEM_LIMIT = 48 * 1024 * 1024


def params():
    return pltpu.CompilerParams(vmem_limit_bytes=VMEM_LIMIT)


VM = pl.BlockSpec(memory_space=pltpu.VMEM)
SM = pl.BlockSpec(memory_space=pltpu.SMEM)


def grid_step(first_bits, second_bits, weights, valid, src, dst, dif, lane_two, lane_three):
    lane = lax.broadcasted_iota(jnp.int32, (1, LANES), 1)
    first_mask = (1 << first_bits) - 1
    stride_two = 1 << first_bits
    stride_three = 1 << (first_bits + second_bits)
    two_mask = stride_three - 1
    up_one = (lane & first_mask) != first_mask
    down_one = (lane & first_mask) != 0

    def rolled(tile, stride):
        return pltpu.roll(tile, LANES - stride, 1), pltpu.roll(tile, stride, 1)

    def neighbours(j, x, nxt, stride, in_lanes, carry):
        if not in_lanes:
            step = stride // LANES
            return src[PAD + j + step], src[PAD + j - step], carry
        up_here, down_here, down_last = carry
        up_next, down_next = rolled(nxt, stride)
        ahead = jnp.where(lane < LANES - stride, up_here, up_next)
        before = jnp.where(lane >= stride, down_here, down_last)
        return ahead, before, (up_next, down_next, down_here)

    def one_tile(j, carry):
        x, carry_two, carry_three = carry
        nxt = src[PAD + j + 1]
        ahead = jnp.where(up_one, pltpu.roll(x, LANES - 1, 1), 0.0)
        before = jnp.where(down_one, pltpu.roll(x, 1, 1), 0.0)
        total = ahead + before
        drift = weights[0] * (ahead - before)
        ahead, before, carry_two = neighbours(j, x, nxt, stride_two, lane_two, carry_two)
        node = (j * LANES + lane) & two_mask
        ahead = jnp.where(node < stride_three - stride_two, ahead, 0.0)
        before = jnp.where(node >= stride_two, before, 0.0)
        total = total + (ahead + before)
        drift = drift + weights[1] * (ahead - before)
        ahead, before, carry_three = neighbours(j, x, nxt, stride_three, lane_three, carry_three)
        total = total + (ahead + before)
        drift = drift + weights[2] * (ahead - before)
        ahead = pltpu.roll(x, 23, 0)
        before = pltpu.roll(x, 1, 0)
        total = total + (ahead + before)
        drift = drift + weights[3] * (ahead - before)
        new = x + dif[j] * (total - 8.0 * x) - drift
        dst[PAD + j] = jnp.where(valid, new, 0.0)
        return nxt, carry_two, carry_three

    def start(stride, in_lanes):
        if not in_lanes:
            return ()
        up_here, down_here = rolled(src[PAD], stride)
        return up_here, down_here, jnp.zeros((24, LANES), jnp.float32)

    def several(k, carry):
        for i in range(4):
            carry = one_tile(4 * k + i, carry)
        return carry

    lax.fori_loop(
        0,
        TILES // 4,
        several,
        (src[PAD], start(stride_two, lane_two), start(stride_three, lane_three)),
    )


def steps_kernel(levels, velocity, conc, dif_in, low, high, out, lead, u_a, u_b, dif):
    place = lax.axis_index("dom")
    count = lax.axis_size("dom")
    zeros = jnp.zeros((PAD, 24, LANES), jnp.float32)
    for ref in (u_a, u_b):
        ref[pl.ds(0, PAD)] = zeros
        ref[pl.ds(PAD + TILES, PAD)] = zeros
    tail = jnp.zeros((8, LANES), jnp.float32)
    for j in range(TILES):
        cols = pl.ds(j * LANES, LANES)
        u_a[PAD + j, 0:16] = conc[:, cols]
        u_a[PAD + j, 16:24] = tail
        dif[j, 0:16] = 0.1 * dif_in[:, cols]
        dif[j, 16:24] = tail
    for i in range(3):
        u_a[PAD : PAD + TILES, 16 + i] = high[i]
    for i in range(2):
        u_a[PAD : PAD + TILES, 22 + i] = low[i]
        dif[:, 16 + i] = 0.1 * high[3 + i]
    dif[:, 23] = 0.1 * low[2]
    row = lax.broadcasted_iota(jnp.int32, (24, LANES), 0)
    valid = (row < 16) | ((row < 20) & (place < count - 1)) | ((row >= 20) & (place > 0))
    weights = [0.1 * velocity[d] for d in range(4)]
    first_bits = levels[0, 0]
    second_bits = levels[0, 1]

    def both(lane_two, lane_three):
        def run():
            for src, dst in ((u_a, u_b), (u_b, u_a)):
                grid_step(
                    first_bits, second_bits, weights, valid, src, dst, dif, lane_two, lane_three
                )

        return run

    small_two = first_bits < 7
    small_three = first_bits + second_bits < 7
    pl.when(small_three)(both(True, True))
    pl.when(small_two & jnp.logical_not(small_three))(both(True, False))
    pl.when(jnp.logical_not(small_two))(both(False, False))
    out[...] = u_a[PAD : PAD + TILES]
    lead[...] = u_a[PAD : PAD + TILES, 0]


def bit_ends(levels, q):
    one = levels[0, 0]
    two = one + levels[0, 1]
    begin = jnp.where(q < one, 0, jnp.where(q < two, one, two))
    end = jnp.where(q < one, one, jnp.where(q < two, two, LR))
    return begin, end


def lane_kernel(levels, out):
    rows = lax.broadcasted_iota(jnp.int32, (LANES, LANES), 0)
    lane = lax.broadcasted_iota(jnp.int32, (LANES, LANES), 1)
    own = (rows == lane).astype(jnp.float32)
    nxt = jnp.zeros((LANES, LANES), jnp.float32)
    for q in range(7):
        begin, end = bit_ends(levels, q)
        below = (1 << q) - (1 << begin)
        above = (1 << jnp.minimum(end, 7)) - (2 << q)
        here = ((lane & below) == 0) & ((lane & (1 << q)) != 0)
        full = (lane & above) == above
        ahead = pltpu.roll(own, LANES - (1 << q), 1)
        before = pltpu.roll(own, 1 << q, 1)
        half = jnp.where(here, -0.5, 0.0)
        nxt = nxt + jnp.where(full & (end > 7), half * ahead, 0.0)
        own = own + half * (before + jnp.where(full, 0.0, ahead))
    out[0:LANES] = own
    out[LANES : 2 * LANES] = nxt


def pack_kernel(levels, sign, places, v_in, coarse, lanes, out, x, y, stage):
    place = lax.axis_index("dom")
    row = lax.broadcasted_iota(jnp.int32, (24, LANES), 0)
    for j in range(TILES):
        tile = v_in[j]
        for p in range(4):
            s = 1 << p
            both = pltpu.roll(tile, 24 - s, 0) + pltpu.roll(tile, s, 0)
            hit = ((row & (2 * s - 1)) == s) & (row < 16)
            tile = tile - 0.5 * jnp.where(hit, both, 0.0)
        x[j] = tile[0:16]
    own_upper = jnp.where((place & 1) == 1, 0.5, 0.0)
    fix = 0.5 * coarse[...] + own_upper * v_in[:, 16]
    x[0:TILES, 0] = x[0:TILES, 0] - fix
    x[TILES] = jnp.zeros((16, LANES), jnp.float32)
    y[pl.ds(0, 32)] = jnp.zeros((32, 16, LANES), jnp.float32)
    y[pl.ds(32 + TILES, 32)] = jnp.zeros((32, 16, LANES), jnp.float32)

    _, end_six = bit_ends(levels, 6)
    mask_six = (1 << (jnp.maximum(end_six, 7) - 7)) - 1
    chunk = 8
    own_mat = lanes[0:LANES]
    next_mat = lanes[LANES : 2 * LANES]

    def lane_pass(k, carry):
        j0 = k * chunk
        own = x[pl.ds(j0, chunk)].reshape(chunk * 16, LANES)
        nxt = jnp.concatenate(
            [
                jnp.where(((j0 + i) & mask_six) == mask_six, 0.0, x[j0 + i + 1])
                for i in range(chunk)
            ],
            axis=0,
        )
        res = jnp.dot(
            own, own_mat, precision=lax.Precision.HIGHEST, preferred_element_type=jnp.float32
        ) + jnp.dot(
            nxt, next_mat, precision=lax.Precision.HIGHEST, preferred_element_type=jnp.float32
        )
        y[pl.ds(32 + j0, chunk)] = res.reshape(chunk, 16, LANES)
        return carry

    lax.fori_loop(0, TILES // chunk, lane_pass, 0)

    lane = lax.broadcasted_iota(jnp.int32, (1, LANES), 1)
    for q in range(7, LR):
        t = 1 << (q - 7)
        begin, end = bit_ends(levels, q)
        low_lane = 128 - (1 << jnp.minimum(begin, 7))
        half = jnp.where((lane & low_lane) == 0, -0.5, 0.0)
        below = t - (1 << (jnp.maximum(begin, 7) - 7))
        above = (1 << (end - 7)) - 2 * t

        def tile_pass(j):
            hit = (j & below) == 0
            mine = jnp.where(hit, half, 0.0)
            ahead_on = jnp.where((j & above) == above, 0.0, 1.0)
            y[32 + j] = y[32 + j] + mine * (y[32 + j - t] + ahead_on * y[32 + j + t])

        for j in range(TILES):
            if j & t:
                tile_pass(j)

    factor = sign[0].astype(jnp.float32)
    for j in range(TILES):
        tile = factor * y[32 + j]
        for i in range(2):
            stage[pl.ds(j + i * 8 * TILES, 8, stride=TILES), :] = tile[8 * i : 8 * i + 8]
    for b in range(16 * TILES // 8):
        out[places[b]] = stage[pl.ds(8 * b, 8), :]


def places_kernel(owners, out, seen, *, devices, capacity):
    def clear(i, carry):
        seen[i] = 0
        return carry

    lax.fori_loop(0, devices, clear, 0)

    def one(b, carry):
        owner = owners[0, b]
        rank = seen[owner]
        seen[owner] = rank + 1
        out[b] = owner * capacity + rank
        return carry

    lax.fori_loop(0, owners.shape[1], one, 0)


def sum_kernel(table, arrived, out, pieces):
    pieces[...] = jnp.zeros_like(pieces)
    devices, capacity = table.shape

    def add(d, carry):
        for i in range(capacity):
            s = table[d, i]
            pieces[s] = pieces[s] + arrived[d * capacity + i]
        return carry

    lax.fori_loop(0, devices, add, 0)

    def give(d, carry):
        for i in range(capacity):
            out[d * capacity + i] = pieces[table[d, i]]
        return carry

    lax.fori_loop(0, devices, give, 0)


def unpack_kernel(places, back, out, stage):
    for b in range(16 * TILES // 8):
        stage[pl.ds(8 * b, 8), :] = back[places[b]]
    for j in range(TILES):
        for i in range(2):
            out[8 * i : 8 * i + 8, j * LANES : (j + 1) * LANES] = stage[
                pl.ds(j + i * 8 * TILES, 8, stride=TILES), :
            ]


def f32(*shape):
    return jax.ShapeDtypeStruct(shape, jnp.float32)


def body(concentration, diffusion, velocity, levels, grid_signs, owner_list, slot_list):
    dom_count = lax.axis_size("dom")
    devices = lax.axis_size("grid") * dom_count
    rows = concentration.shape[1]
    conc = concentration[0]
    dif = diffusion[0]
    blocks = owner_list.shape[1]
    capacity = 2 * blocks // devices

    up = [(i, i + 1) for i in range(dom_count - 1)]
    down = [(i + 1, i) for i in range(dom_count - 1)]
    low_rows = jnp.concatenate([conc[rows - 2 :], dif[rows - 1 :]], axis=0)
    high_rows = jnp.concatenate([conc[:3], dif[:2]], axis=0)
    low = lax.ppermute(low_rows.reshape(3, TILES, LANES), "dom", up)
    high = lax.ppermute(high_rows.reshape(5, TILES, LANES), "dom", down)

    places = pl.pallas_call(
        functools.partial(places_kernel, devices=devices, capacity=capacity),
        out_shape=jax.ShapeDtypeStruct((blocks,), jnp.int32),
        in_specs=[SM],
        out_specs=SM,
        scratch_shapes=[pltpu.SMEM((devices,), jnp.int32)],
        compiler_params=params(),
        name="places",
    )(owner_list)
    lanes = pl.pallas_call(
        lane_kernel,
        out_shape=f32(2 * LANES, LANES),
        in_specs=[SM],
        out_specs=VM,
        compiler_params=params(),
        name="lane_matrix",
    )(levels)

    me = lax.axis_index("grid") * dom_count + lax.axis_index("dom")
    keys = lax.all_gather(owner_list * SLOTS + slot_list, ("grid", "dom"), axis=0, tiled=True)
    mine = (keys // SLOTS) == me
    rank = jnp.cumsum(mine.astype(jnp.int32), axis=1)
    at_rank = mine[:, None, :] & (
        rank[:, None, :] == jnp.arange(1, capacity + 1, dtype=jnp.int32)[None, :, None]
    )
    table = SLOTS + jnp.sum(jnp.where(at_rank, (keys % SLOTS - SLOTS)[:, None, :], 0), axis=2)

    stepped, lead = pl.pallas_call(
        steps_kernel,
        out_shape=(f32(TILES, 24, LANES), f32(TILES, LANES)),
        in_specs=[SM, SM, VM, VM, VM, VM],
        out_specs=(VM, VM),
        scratch_shapes=[
            pltpu.VMEM((TILES + 2 * PAD, 24, LANES), jnp.float32),
            pltpu.VMEM((TILES + 2 * PAD, 24, LANES), jnp.float32),
            pltpu.VMEM((TILES, 24, LANES), jnp.float32),
        ],
        compiler_params=params(),
        name="steps",
    )(levels, velocity, conc, dif, low, high)

    coarse = None
    distance = 1
    while distance < dom_count:
        targets = range(distance, dom_count, 2 * distance)
        pairs = [[(d - distance, d) for d in targets]]
        if distance > 1:
            pairs.append([(d + distance, d) for d in targets if d + distance < dom_count])
        for pair in pairs:
            if pair:
                part = lax.ppermute(lead, "dom", pair)
                coarse = part if coarse is None else coarse + part
        distance *= 2

    outgoing = pl.pallas_call(
        pack_kernel,
        out_shape=f32(devices * capacity, 8, LANES),
        in_specs=[SM, SM, SM, VM, VM, VM],
        out_specs=VM,
        scratch_shapes=[
            pltpu.VMEM((TILES + 1, 16, LANES), jnp.float32),
            pltpu.VMEM((TILES + 64, 16, LANES), jnp.float32),
            pltpu.VMEM((16 * TILES, LANES), jnp.float32),
        ],
        compiler_params=params(),
        name="pack",
    )(levels, grid_signs, places, stepped, coarse, lanes)

    def exchange(x):
        return lax.all_to_all(
            x.reshape(devices, capacity * 8, LANES),
            ("grid", "dom"),
            split_axis=0,
            concat_axis=0,
            tiled=True,
        ).reshape(devices * capacity, 8, LANES)

    arrived = exchange(outgoing)
    returned = pl.pallas_call(
        sum_kernel,
        out_shape=f32(devices * capacity, 8, LANES),
        in_specs=[SM, VM],
        out_specs=VM,
        scratch_shapes=[pltpu.VMEM((SLOTS + 8, 8, LANES), jnp.float32)],
        compiler_params=params(),
        name="sum_pieces",
    )(table, arrived)
    back = exchange(returned)
    combined = pl.pallas_call(
        unpack_kernel,
        out_shape=f32(rows, TILES * LANES),
        in_specs=[SM, VM],
        out_specs=VM,
        scratch_shapes=[pltpu.VMEM((16 * TILES, LANES), jnp.float32)],
        compiler_params=params(),
        name="unpack",
    )(places, back)
    return combined[None]


def solution(mesh):
    return jax.shard_map(
        body,
        mesh=mesh,
        in_specs=(
            P("grid", "dom", None),
            P("grid", "dom", None),
            P(),
            P("grid", None),
            P("grid"),
            P(("grid", "dom"), None),
            P(("grid", "dom"), None),
        ),
        out_specs=P("grid", "dom", None),
        check_vma=False,
    )
```

```python
import functools

import jax
import jax.numpy as jnp
from jax import lax
from jax.experimental import pallas as pl
from jax.experimental.pallas import tpu as pltpu
from jax.sharding import PartitionSpec as P

LR = 13
BLK = 1024
SLOTS = 64
LANES = 128
TILES = 2**LR // LANES
PAD = 9
VMEM_LIMIT = 48 * 1024 * 1024


def params():
    return pltpu.CompilerParams(vmem_limit_bytes=VMEM_LIMIT)


VM = pl.BlockSpec(memory_space=pltpu.VMEM)
SM = pl.BlockSpec(memory_space=pltpu.SMEM)


def grid_step(first_bits, second_bits, weights, valid, src, dst, dif, lane_two, lane_three):
    lane = lax.broadcasted_iota(jnp.int32, (1, LANES), 1)
    first_mask = (1 << first_bits) - 1
    stride_two = 1 << first_bits
    stride_three = 1 << (first_bits + second_bits)
    two_mask = stride_three - 1
    up_one = (lane & first_mask) != first_mask
    down_one = (lane & first_mask) != 0

    def rolled(tile, stride):
        return pltpu.roll(tile, LANES - stride, 1), pltpu.roll(tile, stride, 1)

    def neighbours(j, x, nxt, stride, in_lanes, carry):
        if not in_lanes:
            step = stride // LANES
            return src[PAD + j + step], src[PAD + j - step], carry
        up_here, down_here, down_last = carry
        up_next, down_next = rolled(nxt, stride)
        ahead = jnp.where(lane < LANES - stride, up_here, up_next)
        before = jnp.where(lane >= stride, down_here, down_last)
        return ahead, before, (up_next, down_next, down_here)

    def one_tile(j, carry):
        x, carry_two, carry_three = carry
        nxt = src[PAD + j + 1]
        ahead = jnp.where(up_one, pltpu.roll(x, LANES - 1, 1), 0.0)
        before = jnp.where(down_one, pltpu.roll(x, 1, 1), 0.0)
        total = ahead + before
        drift = weights[0] * (ahead - before)
        ahead, before, carry_two = neighbours(j, x, nxt, stride_two, lane_two, carry_two)
        node = (j * LANES + lane) & two_mask
        ahead = jnp.where(node < stride_three - stride_two, ahead, 0.0)
        before = jnp.where(node >= stride_two, before, 0.0)
        total = total + (ahead + before)
        drift = drift + weights[1] * (ahead - before)
        ahead, before, carry_three = neighbours(j, x, nxt, stride_three, lane_three, carry_three)
        total = total + (ahead + before)
        drift = drift + weights[2] * (ahead - before)
        ahead = pltpu.roll(x, 23, 0)
        before = pltpu.roll(x, 1, 0)
        total = total + (ahead + before)
        drift = drift + weights[3] * (ahead - before)
        new = x + dif[j] * (total - 8.0 * x) - drift
        dst[PAD + j] = jnp.where(valid, new, 0.0)
        return nxt, carry_two, carry_three

    def start(stride, in_lanes):
        if not in_lanes:
            return ()
        up_here, down_here = rolled(src[PAD], stride)
        return up_here, down_here, jnp.zeros((24, LANES), jnp.float32)

    def several(k, carry):
        for i in range(4):
            carry = one_tile(4 * k + i, carry)
        return carry

    lax.fori_loop(
        0,
        TILES // 4,
        several,
        (src[PAD], start(stride_two, lane_two), start(stride_three, lane_three)),
    )


def steps_kernel(levels, velocity, conc, dif_in, low, high, out, lead, u_a, u_b, dif):
    place = lax.axis_index("dom")
    count = lax.axis_size("dom")
    zeros = jnp.zeros((PAD, 24, LANES), jnp.float32)
    for ref in (u_a, u_b):
        ref[pl.ds(0, PAD)] = zeros
        ref[pl.ds(PAD + TILES, PAD)] = zeros
    tail = jnp.zeros((8, LANES), jnp.float32)
    for j in range(TILES):
        cols = pl.ds(j * LANES, LANES)
        u_a[PAD + j, 0:16] = conc[:, cols]
        u_a[PAD + j, 16:24] = tail
        dif[j, 0:16] = 0.1 * dif_in[:, cols]
        dif[j, 16:24] = tail
    for i in range(3):
        u_a[PAD : PAD + TILES, 16 + i] = high[i]
    for i in range(2):
        u_a[PAD : PAD + TILES, 22 + i] = low[i]
        dif[:, 16 + i] = 0.1 * high[3 + i]
    dif[:, 23] = 0.1 * low[2]
    row = lax.broadcasted_iota(jnp.int32, (24, LANES), 0)
    valid = (row < 16) | ((row < 20) & (place < count - 1)) | ((row >= 20) & (place > 0))
    weights = [0.1 * velocity[d] for d in range(4)]
    first_bits = levels[0, 0]
    second_bits = levels[0, 1]

    def both(lane_two, lane_three):
        def run():
            for src, dst in ((u_a, u_b), (u_b, u_a)):
                grid_step(
                    first_bits, second_bits, weights, valid, src, dst, dif, lane_two, lane_three
                )

        return run

    small_two = first_bits < 7
    small_three = first_bits + second_bits < 7
    pl.when(small_three)(both(True, True))
    pl.when(small_two & jnp.logical_not(small_three))(both(True, False))
    pl.when(jnp.logical_not(small_two))(both(False, False))
    out[...] = u_a[PAD : PAD + TILES]
    lead[...] = u_a[PAD : PAD + TILES, 0]


def bit_ends(levels, q):
    one = levels[0, 0]
    two = one + levels[0, 1]
    begin = jnp.where(q < one, 0, jnp.where(q < two, one, two))
    end = jnp.where(q < one, one, jnp.where(q < two, two, LR))
    return begin, end


def lane_kernel(levels, out):
    rows = lax.broadcasted_iota(jnp.int32, (LANES, LANES), 0)
    lane = lax.broadcasted_iota(jnp.int32, (LANES, LANES), 1)
    own = (rows == lane).astype(jnp.float32)
    nxt = jnp.zeros((LANES, LANES), jnp.float32)
    for q in range(7):
        begin, end = bit_ends(levels, q)
        below = (1 << q) - (1 << begin)
        above = (1 << jnp.minimum(end, 7)) - (2 << q)
        here = ((lane & below) == 0) & ((lane & (1 << q)) != 0)
        full = (lane & above) == above
        ahead = pltpu.roll(own, LANES - (1 << q), 1)
        before = pltpu.roll(own, 1 << q, 1)
        half = jnp.where(here, -0.5, 0.0)
        nxt = nxt + jnp.where(full & (end > 7), half * ahead, 0.0)
        own = own + half * (before + jnp.where(full, 0.0, ahead))
    out[0:LANES] = own
    out[LANES : 2 * LANES] = nxt


def pack_kernel(levels, sign, places, v_in, coarse, lanes, out, x, y, stage):
    place = lax.axis_index("dom")
    row = lax.broadcasted_iota(jnp.int32, (24, LANES), 0)
    for j in range(TILES):
        tile = v_in[j]
        for p in range(4):
            s = 1 << p
            both = pltpu.roll(tile, 24 - s, 0) + pltpu.roll(tile, s, 0)
            hit = ((row & (2 * s - 1)) == s) & (row < 16)
            tile = tile - 0.5 * jnp.where(hit, both, 0.0)
        x[j] = tile[0:16]
    own_upper = jnp.where((place & 1) == 1, 0.5, 0.0)
    fix = 0.5 * coarse[...] + own_upper * v_in[:, 16]
    x[0:TILES, 0] = x[0:TILES, 0] - fix
    x[TILES] = jnp.zeros((16, LANES), jnp.float32)
    y[pl.ds(0, 32)] = jnp.zeros((32, 16, LANES), jnp.float32)
    y[pl.ds(32 + TILES, 32)] = jnp.zeros((32, 16, LANES), jnp.float32)

    _, end_six = bit_ends(levels, 6)
    mask_six = (1 << (jnp.maximum(end_six, 7) - 7)) - 1
    chunk = 8
    own_mat = lanes[0:LANES]
    next_mat = lanes[LANES : 2 * LANES]

    def lane_pass(k, carry):
        j0 = k * chunk
        own = x[pl.ds(j0, chunk)].reshape(chunk * 16, LANES)
        nxt = jnp.concatenate(
            [
                jnp.where(((j0 + i) & mask_six) == mask_six, 0.0, x[j0 + i + 1])
                for i in range(chunk)
            ],
            axis=0,
        )
        res = jnp.dot(
            own, own_mat, precision=lax.Precision.HIGHEST, preferred_element_type=jnp.float32
        ) + jnp.dot(
            nxt, next_mat, precision=lax.Precision.HIGHEST, preferred_element_type=jnp.float32
        )
        y[pl.ds(32 + j0, chunk)] = res.reshape(chunk, 16, LANES)
        return carry

    lax.fori_loop(0, TILES // chunk, lane_pass, 0)

    lane = lax.broadcasted_iota(jnp.int32, (1, LANES), 1)
    for q in range(7, LR):
        t = 1 << (q - 7)
        begin, end = bit_ends(levels, q)
        low_lane = 128 - (1 << jnp.minimum(begin, 7))
        half = jnp.where((lane & low_lane) == 0, -0.5, 0.0)
        below = t - (1 << (jnp.maximum(begin, 7) - 7))
        above = (1 << (end - 7)) - 2 * t

        def tile_pass(j):
            hit = (j & below) == 0
            mine = jnp.where(hit, half, 0.0)
            ahead_on = jnp.where((j & above) == above, 0.0, 1.0)
            y[32 + j] = y[32 + j] + mine * (y[32 + j - t] + ahead_on * y[32 + j + t])

        for j in range(TILES):
            if j & t:
                tile_pass(j)

    factor = sign[0].astype(jnp.float32)
    for j in range(TILES):
        tile = factor * y[32 + j]
        for i in range(2):
            stage[pl.ds(j + i * 8 * TILES, 8, stride=TILES), :] = tile[8 * i : 8 * i + 8]
    for b in range(16 * TILES // 8):
        out[places[b]] = stage[pl.ds(8 * b, 8), :]


def places_kernel(owners, out, seen, *, devices, capacity):
    def clear(i, carry):
        seen[i] = 0
        return carry

    lax.fori_loop(0, devices, clear, 0)

    def one(b, carry):
        owner = owners[0, b]
        rank = seen[owner]
        seen[owner] = rank + 1
        out[b] = owner * capacity + rank
        return carry

    lax.fori_loop(0, owners.shape[1], one, 0)


def sum_kernel(table, arrived, out, pieces):
    pieces[...] = jnp.zeros_like(pieces)
    devices, capacity = table.shape

    def add(d, carry):
        for i in range(capacity):
            s = table[d, i]
            pieces[s] = pieces[s] + arrived[d * capacity + i]
        return carry

    lax.fori_loop(0, devices, add, 0)

    def give(d, carry):
        for i in range(capacity):
            out[d * capacity + i] = pieces[table[d, i]]
        return carry

    lax.fori_loop(0, devices, give, 0)


def unpack_kernel(places, back, out, stage):
    for b in range(16 * TILES // 8):
        stage[pl.ds(8 * b, 8), :] = back[places[b]]
    for j in range(TILES):
        for i in range(2):
            out[8 * i : 8 * i + 8, j * LANES : (j + 1) * LANES] = stage[
                pl.ds(j + i * 8 * TILES, 8, stride=TILES), :
            ]


def f32(*shape):
    return jax.ShapeDtypeStruct(shape, jnp.float32)


def body(concentration, diffusion, velocity, levels, grid_signs, owner_list, slot_list):
    dom_count = lax.axis_size("dom")
    devices = lax.axis_size("grid") * dom_count
    rows = concentration.shape[1]
    conc = concentration[0]
    dif = diffusion[0]
    blocks = owner_list.shape[1]
    capacity = 2 * blocks // devices

    up = [(i, i + 1) for i in range(dom_count - 1)]
    down = [(i + 1, i) for i in range(dom_count - 1)]
    low_rows = jnp.concatenate([conc[rows - 2 :], dif[rows - 1 :]], axis=0)
    high_rows = jnp.concatenate([conc[:3], dif[:2]], axis=0)
    low = lax.ppermute(low_rows.reshape(3, TILES, LANES), "dom", up)
    high = lax.ppermute(high_rows.reshape(5, TILES, LANES), "dom", down)

    places = pl.pallas_call(
        functools.partial(places_kernel, devices=devices, capacity=capacity),
        out_shape=jax.ShapeDtypeStruct((blocks,), jnp.int32),
        in_specs=[SM],
        out_specs=SM,
        scratch_shapes=[pltpu.SMEM((devices,), jnp.int32)],
        compiler_params=params(),
        name="places",
    )(owner_list)
    lanes = pl.pallas_call(
        lane_kernel,
        out_shape=f32(2 * LANES, LANES),
        in_specs=[SM],
        out_specs=VM,
        compiler_params=params(),
        name="lane_matrix",
    )(levels)

    me = lax.axis_index("grid") * dom_count + lax.axis_index("dom")
    own_keys = owner_list * SLOTS + slot_list
    keys = lax.all_to_all(
        jnp.broadcast_to(own_keys[:, None], (devices, 1, blocks)),
        ("grid", "dom"),
        split_axis=0,
        concat_axis=0,
        tiled=True,
    )[:, 0]
    mine = (keys // SLOTS) == me
    rank = jnp.cumsum(mine.astype(jnp.int32), axis=1)
    at_rank = mine[:, None, :] & (
        rank[:, None, :] == jnp.arange(1, capacity + 1, dtype=jnp.int32)[None, :, None]
    )
    table = SLOTS + jnp.sum(jnp.where(at_rank, (keys % SLOTS - SLOTS)[:, None, :], 0), axis=2)

    stepped, lead = pl.pallas_call(
        steps_kernel,
        out_shape=(f32(TILES, 24, LANES), f32(TILES, LANES)),
        in_specs=[SM, SM, VM, VM, VM, VM],
        out_specs=(VM, VM),
        scratch_shapes=[
            pltpu.VMEM((TILES + 2 * PAD, 24, LANES), jnp.float32),
            pltpu.VMEM((TILES + 2 * PAD, 24, LANES), jnp.float32),
            pltpu.VMEM((TILES, 24, LANES), jnp.float32),
        ],
        compiler_params=params(),
        name="steps",
    )(levels, velocity, conc, dif, low, high)

    coarse = None
    distance = 1
    while distance < dom_count:
        targets = range(distance, dom_count, 2 * distance)
        pairs = [[(d - distance, d) for d in targets]]
        if distance > 1:
            pairs.append([(d + distance, d) for d in targets if d + distance < dom_count])
        for pair in pairs:
            if pair:
                part = lax.ppermute(lead, "dom", pair)
                coarse = part if coarse is None else coarse + part
        distance *= 2

    outgoing = pl.pallas_call(
        pack_kernel,
        out_shape=f32(devices * capacity, 8, LANES),
        in_specs=[SM, SM, SM, VM, VM, VM],
        out_specs=VM,
        scratch_shapes=[
            pltpu.VMEM((TILES + 1, 16, LANES), jnp.float32),
            pltpu.VMEM((TILES + 64, 16, LANES), jnp.float32),
            pltpu.VMEM((16 * TILES, LANES), jnp.float32),
        ],
        compiler_params=params(),
        name="pack",
    )(levels, grid_signs, places, stepped, coarse, lanes)

    def exchange(x):
        return lax.all_to_all(
            x.reshape(devices, capacity * 8, LANES),
            ("grid", "dom"),
            split_axis=0,
            concat_axis=0,
            tiled=True,
        ).reshape(devices * capacity, 8, LANES)

    arrived = exchange(outgoing)
    returned = pl.pallas_call(
        sum_kernel,
        out_shape=f32(devices * capacity, 8, LANES),
        in_specs=[SM, VM],
        out_specs=VM,
        scratch_shapes=[pltpu.VMEM((SLOTS + 8, 8, LANES), jnp.float32)],
        compiler_params=params(),
        name="sum_pieces",
    )(table, arrived)
    back = exchange(returned)
    combined = pl.pallas_call(
        unpack_kernel,
        out_shape=f32(rows, TILES * LANES),
        in_specs=[SM, VM],
        out_specs=VM,
        scratch_shapes=[pltpu.VMEM((16 * TILES, LANES), jnp.float32)],
        compiler_params=params(),
        name="unpack",
    )(places, back)
    return combined[None]


def solution(mesh):
    return jax.shard_map(
        body,
        mesh=mesh,
        in_specs=(
            P("grid", "dom", None),
            P("grid", "dom", None),
            P(),
            P("grid", None),
            P("grid"),
            P(("grid", "dom"), None),
            P(("grid", "dom"), None),
        ),
        out_specs=P("grid", "dom", None),
        check_vma=False,
    )
```

```python
import functools

import jax
import jax.numpy as jnp
from jax import lax
from jax.experimental import pallas as pl
from jax.experimental.pallas import tpu as pltpu
from jax.sharding import PartitionSpec as P

LR = 13
BLK = 1024
SLOTS = 64
LANES = 128
TILES = 2**LR // LANES
PAD = 9
VMEM_LIMIT = 48 * 1024 * 1024


def params():
    return pltpu.CompilerParams(vmem_limit_bytes=VMEM_LIMIT)


VM = pl.BlockSpec(memory_space=pltpu.VMEM)
SM = pl.BlockSpec(memory_space=pltpu.SMEM)


def grid_step(first_bits, second_bits, weights, valid, src, dst, dif, lane_two, lane_three):
    lane = lax.broadcasted_iota(jnp.int32, (1, LANES), 1)
    first_mask = (1 << first_bits) - 1
    stride_two = 1 << first_bits
    stride_three = 1 << (first_bits + second_bits)
    two_mask = stride_three - 1
    up_one = (lane & first_mask) != first_mask
    down_one = (lane & first_mask) != 0

    def rolled(tile, stride):
        return pltpu.roll(tile, LANES - stride, 1), pltpu.roll(tile, stride, 1)

    def neighbours(j, x, nxt, stride, in_lanes, carry):
        if not in_lanes:
            step = stride // LANES
            return src[PAD + j + step], src[PAD + j - step], carry
        up_here, down_here, down_last = carry
        up_next, down_next = rolled(nxt, stride)
        ahead = jnp.where(lane < LANES - stride, up_here, up_next)
        before = jnp.where(lane >= stride, down_here, down_last)
        return ahead, before, (up_next, down_next, down_here)

    def one_tile(j, carry):
        x, carry_two, carry_three = carry
        nxt = src[PAD + j + 1]
        ahead = jnp.where(up_one, pltpu.roll(x, LANES - 1, 1), 0.0)
        before = jnp.where(down_one, pltpu.roll(x, 1, 1), 0.0)
        total = ahead + before
        drift = weights[0] * (ahead - before)
        ahead, before, carry_two = neighbours(j, x, nxt, stride_two, lane_two, carry_two)
        node = (j * LANES + lane) & two_mask
        ahead = jnp.where(node < stride_three - stride_two, ahead, 0.0)
        before = jnp.where(node >= stride_two, before, 0.0)
        total = total + (ahead + before)
        drift = drift + weights[1] * (ahead - before)
        ahead, before, carry_three = neighbours(j, x, nxt, stride_three, lane_three, carry_three)
        total = total + (ahead + before)
        drift = drift + weights[2] * (ahead - before)
        ahead = pltpu.roll(x, 23, 0)
        before = pltpu.roll(x, 1, 0)
        total = total + (ahead + before)
        drift = drift + weights[3] * (ahead - before)
        new = x + dif[j] * (total - 8.0 * x) - drift
        dst[PAD + j] = jnp.where(valid, new, 0.0)
        return nxt, carry_two, carry_three

    def start(stride, in_lanes):
        if not in_lanes:
            return ()
        up_here, down_here = rolled(src[PAD], stride)
        return up_here, down_here, jnp.zeros((24, LANES), jnp.float32)

    def several(k, carry):
        for i in range(4):
            carry = one_tile(4 * k + i, carry)
        return carry

    lax.fori_loop(
        0,
        TILES // 4,
        several,
        (src[PAD], start(stride_two, lane_two), start(stride_three, lane_three)),
    )


def steps_kernel(levels, velocity, conc, dif_in, low, high, out, lead, u_a, u_b, dif):
    place = lax.axis_index("dom")
    count = lax.axis_size("dom")
    zeros = jnp.zeros((PAD, 24, LANES), jnp.float32)
    for ref in (u_a, u_b):
        ref[pl.ds(0, PAD)] = zeros
        ref[pl.ds(PAD + TILES, PAD)] = zeros
    tail = jnp.zeros((8, LANES), jnp.float32)
    for j in range(TILES):
        cols = pl.ds(j * LANES, LANES)
        u_a[PAD + j, 0:16] = conc[:, cols]
        u_a[PAD + j, 16:24] = tail
        dif[j, 0:16] = 0.1 * dif_in[:, cols]
        dif[j, 16:24] = tail
    for i in range(3):
        u_a[PAD : PAD + TILES, 16 + i] = high[i]
    for i in range(2):
        u_a[PAD : PAD + TILES, 22 + i] = low[i]
        dif[:, 16 + i] = 0.1 * high[3 + i]
    dif[:, 23] = 0.1 * low[2]
    row = lax.broadcasted_iota(jnp.int32, (24, LANES), 0)
    valid = (row < 16) | ((row < 20) & (place < count - 1)) | ((row >= 20) & (place > 0))
    weights = [0.1 * velocity[d] for d in range(4)]
    first_bits = levels[0, 0]
    second_bits = levels[0, 1]

    def both(lane_two, lane_three):
        def run():
            for src, dst in ((u_a, u_b), (u_b, u_a)):
                grid_step(
                    first_bits, second_bits, weights, valid, src, dst, dif, lane_two, lane_three
                )

        return run

    small_two = first_bits < 7
    small_three = first_bits + second_bits < 7
    pl.when(small_three)(both(True, True))
    pl.when(small_two & jnp.logical_not(small_three))(both(True, False))
    pl.when(jnp.logical_not(small_two))(both(False, False))
    out[...] = u_a[PAD : PAD + TILES]
    lead[...] = u_a[PAD : PAD + TILES, 0]


def bit_ends(levels, q):
    one = levels[0, 0]
    two = one + levels[0, 1]
    begin = jnp.where(q < one, 0, jnp.where(q < two, one, two))
    end = jnp.where(q < one, one, jnp.where(q < two, two, LR))
    return begin, end


def lane_kernel(levels, out):
    rows = lax.broadcasted_iota(jnp.int32, (LANES, LANES), 0)
    lane = lax.broadcasted_iota(jnp.int32, (LANES, LANES), 1)
    own = (rows == lane).astype(jnp.float32)
    nxt = jnp.zeros((LANES, LANES), jnp.float32)
    for q in range(7):
        begin, end = bit_ends(levels, q)
        below = (1 << q) - (1 << begin)
        above = (1 << jnp.minimum(end, 7)) - (2 << q)
        here = ((lane & below) == 0) & ((lane & (1 << q)) != 0)
        full = (lane & above) == above
        ahead = pltpu.roll(own, LANES - (1 << q), 1)
        before = pltpu.roll(own, 1 << q, 1)
        half = jnp.where(here, -0.5, 0.0)
        nxt = nxt + jnp.where(full & (end > 7), half * ahead, 0.0)
        own = own + half * (before + jnp.where(full, 0.0, ahead))
    out[0:LANES] = own
    out[LANES : 2 * LANES] = nxt


def pack_kernel(levels, sign, info, v_in, coarse, lanes, out, blocks, x, y, stage):
    place = lax.axis_index("dom")
    row = lax.broadcasted_iota(jnp.int32, (24, LANES), 0)
    for j in range(TILES):
        tile = v_in[j]
        for p in range(4):
            s = 1 << p
            both = pltpu.roll(tile, 24 - s, 0) + pltpu.roll(tile, s, 0)
            hit = ((row & (2 * s - 1)) == s) & (row < 16)
            tile = tile - 0.5 * jnp.where(hit, both, 0.0)
        x[j] = tile[0:16]
    own_upper = jnp.where((place & 1) == 1, 0.5, 0.0)
    fix = 0.5 * coarse[...] + own_upper * v_in[:, 16]
    x[0:TILES, 0] = x[0:TILES, 0] - fix
    x[TILES] = jnp.zeros((16, LANES), jnp.float32)
    y[pl.ds(0, 32)] = jnp.zeros((32, 16, LANES), jnp.float32)
    y[pl.ds(32 + TILES, 32)] = jnp.zeros((32, 16, LANES), jnp.float32)

    _, end_six = bit_ends(levels, 6)
    mask_six = (1 << (jnp.maximum(end_six, 7) - 7)) - 1
    chunk = 8
    own_mat = lanes[0:LANES]
    next_mat = lanes[LANES : 2 * LANES]

    def lane_pass(k, carry):
        j0 = k * chunk
        own = x[pl.ds(j0, chunk)].reshape(chunk * 16, LANES)
        nxt = jnp.concatenate(
            [
                jnp.where(((j0 + i) & mask_six) == mask_six, 0.0, x[j0 + i + 1])
                for i in range(chunk)
            ],
            axis=0,
        )
        res = jnp.dot(
            own, own_mat, precision=lax.Precision.HIGHEST, preferred_element_type=jnp.float32
        ) + jnp.dot(
            nxt, next_mat, precision=lax.Precision.HIGHEST, preferred_element_type=jnp.float32
        )
        y[pl.ds(32 + j0, chunk)] = res.reshape(chunk, 16, LANES)
        return carry

    lax.fori_loop(0, TILES // chunk, lane_pass, 0)

    lane = lax.broadcasted_iota(jnp.int32, (1, LANES), 1)
    for q in range(7, LR):
        t = 1 << (q - 7)
        begin, end = bit_ends(levels, q)
        low_lane = 128 - (1 << jnp.minimum(begin, 7))
        half = jnp.where((lane & low_lane) == 0, -0.5, 0.0)
        below = t - (1 << (jnp.maximum(begin, 7) - 7))
        above = (1 << (end - 7)) - 2 * t

        def tile_pass(j):
            hit = (j & below) == 0
            mine = jnp.where(hit, half, 0.0)
            ahead_on = jnp.where((j & above) == above, 0.0, 1.0)
            y[32 + j] = y[32 + j] + mine * (y[32 + j - t] + ahead_on * y[32 + j + t])

        for j in range(TILES):
            if j & t:
                tile_pass(j)

    factor = sign[0].astype(jnp.float32)
    for j in range(TILES):
        tile = factor * y[32 + j]
        for i in range(2):
            stage[pl.ds(j + i * 8 * TILES, 8, stride=TILES), :] = tile[8 * i : 8 * i + 8]
    for b in range(16 * TILES // 8):
        block = stage[pl.ds(8 * b, 8), :]
        blocks[b] = block
        out[info[0, b]] = block


def key_parts(keys, rows):
    owner = keys // SLOTS
    slot = keys % SLOTS
    row = owner % rows
    lane = slot + SLOTS * (owner // rows)
    return owner, slot, lane, row, (row + slot) % rows


def hot(index, count):
    which = lax.broadcasted_iota(jnp.int32, (count, index.shape[1]), 0)
    return jnp.where(which == index, 1.0, 0.0)


def dot_rows(left, right):
    return lax.dot_general(
        left.astype(jnp.bfloat16),
        right.astype(jnp.bfloat16),
        (((1,), (1,)), ((), ())),
        preferred_element_type=jnp.float32,
    )


def dot_plain(left, right):
    return jnp.dot(
        left.astype(jnp.bfloat16), right.astype(jnp.bfloat16), preferred_element_type=jnp.float32
    )


def mixed(handler, lane, row):
    x = (handler * 40503 + lane * 30011 + row * 52711) & 0xFFFF
    x = ((x ^ (x >> 7)) * 9973) & 0xFFFF
    x = ((x ^ (x >> 5)) * 12347) & 0xFFFF
    return (x >> 8).astype(jnp.float32) * (1.0 / 256.0)


def handlers_of(assigned, lane, row):
    return jnp.sum(
        hot(row, assigned.shape[0]) * dot_plain(assigned, hot(lane, LANES)), axis=0, keepdims=True
    )


def device_number():
    return lax.axis_index("grid") * lax.axis_size("dom") + lax.axis_index("dom")


def write_places(info, handler, ok, me, devices, capacity):
    taken = hot(handler.astype(jnp.int32), devices)
    size = handler.shape[1]
    first = lax.broadcasted_iota(jnp.int32, (size, size), 0)
    second = lax.broadcasted_iota(jnp.int32, (size, size), 1)
    before = dot_plain(taken, jnp.where(first < second, 1.0, 0.0))
    rank = jnp.sum(taken * before, axis=0, keepdims=True)
    place = handler.astype(jnp.int32) * capacity + rank.astype(jnp.int32)
    stays = handler == me.astype(jnp.float32)
    send = jnp.where(stays, devices * capacity, place)
    get = jnp.where(stays, 0, place)
    kept = jnp.where(stays, 1, 0)
    flag = jnp.broadcast_to(ok, kept.shape).astype(jnp.int32)
    rows = [send, get, kept, flag, flag, flag, flag, flag]
    info[...] = jnp.concatenate(rows, axis=0)


def owner_places_kernel(keys, info, *, devices, capacity):
    me = device_number()
    owner = (keys[pl.ds(me, 1), :] // SLOTS).astype(jnp.float32)
    write_places(info, owner, jnp.int32(0), me, devices, capacity)


def balance_kernel(keys, assigned, info, one, two, table, *, devices, capacity, full):
    rows = devices * SLOTS // LANES
    keys_all = keys[...]
    _, _, lane_all, row_one, row_two = key_parts(keys_all, rows)
    for d in range(devices):
        pick = slice(d, d + 1)
        both = jnp.concatenate([hot(row_one[pick], rows), hot(row_two[pick], rows)], axis=0)
        counts = dot_rows(both, hot(lane_all[pick], LANES))
        one[pl.ds(d, rows, stride=devices), :] = counts[:rows]
        two[pl.ds(d, rows, stride=devices), :] = counts[rows:]

    square = (devices, devices)
    own = lax.broadcasted_iota(jnp.int32, square, 0) == lax.broadcasted_iota(jnp.int32, square, 1)

    def price(load, steep):
        value = jnp.exp2(load * 0.3785) + steep * jnp.maximum(load - (capacity - 1), 0.0)
        return jnp.where(own, 0.0, value)

    def settle(counts_ref, group, first, load, number):
        base = number * group
        counts = jnp.concatenate(
            [
                counts_ref[pl.ds(pl.multiple_of((base + i) * devices, devices), devices), :]
                for i in range(group)
            ],
            axis=1,
        )
        shape = (devices, group * LANES)
        handler = lax.broadcasted_iota(jnp.int32, shape, 0)
        column = lax.broadcasted_iota(jnp.int32, shape, 1)
        handler_f = handler.astype(jnp.float32)
        cost = dot_plain(price(load, 4.0 if first else 8.0), counts)
        was = None
        if not first:
            old = jnp.concatenate([table[pl.ds(base + i, 1), :] for i in range(group)], axis=1)
            was = handler_f == old
            cost = jnp.where(was, dot_plain(price(load - 1.0, 8.0), counts) - 1.0, cost)
        noise = 0.5 * mixed(handler, column % LANES, base + column // LANES)
        ranked = jnp.floor((jnp.minimum(cost, 4000.0) + noise) * 64.0) * devices + handler_f
        least = jnp.min(ranked, axis=0, keepdims=True)
        chosen = least - jnp.floor(least * (1.0 / devices)) * devices
        for i in range(group):
            table[pl.ds(base + i, 1), :] = chosen[:, i * LANES : (i + 1) * LANES]
        change = jnp.where(handler_f == chosen, 1.0, 0.0)
        if not first:
            change = change - jnp.where(was, 1.0, 0.0)
        return load + dot_rows(change, counts)

    load = jnp.zeros(square, jnp.float32)
    load = lax.fori_loop(0, rows // 2, lambda i, x: settle(one, 2, True, x, i), load)
    spot = lax.broadcasted_iota(jnp.int32, (rows, LANES), 0)
    lane = lax.broadcasted_iota(jnp.int32, (rows, LANES), 1)
    from_row = (spot + rows - (lane % SLOTS) % rows) % rows
    moved = jnp.zeros((rows, LANES), jnp.float32)
    for r in range(rows):
        moved = jnp.where(from_row == r, table[r : r + 1, :], moved)
    table[...] = moved
    load = lax.fori_loop(0, rows // 2, lambda i, x: settle(two, 2, False, x, i), load)
    load = lax.fori_loop(0, rows // 4, lambda i, x: settle(two, 4, False, x, i), load)

    ok = jnp.max(jnp.where(own, 0.0, load)) <= capacity
    owner = (from_row + rows * (lane // SLOTS)).astype(jnp.float32)
    final = jnp.where(ok, table[...], owner)
    assigned[...] = final
    me = device_number()
    _, _, my_lane, _, my_row = key_parts(keys[pl.ds(me, 1), :], rows)
    handler = handlers_of(final, my_lane, my_row)
    size = jnp.where(ok, capacity, full)
    write_places(info, handler, ok.astype(jnp.int32), me, devices, size)


def table_kernel(*refs, devices, capacity, pieces, balanced):
    if balanced:
        keys, assigned, out, handlers = refs
        rows = devices * SLOTS // LANES
        table = assigned[...]
        _, _, lane_all, _, row_all = key_parts(keys[...], rows)
        for d in range(devices):
            handlers[d : d + 1, :] = handlers_of(table, lane_all[d : d + 1], row_all[d : d + 1])
        piece = keys[...]
    else:
        keys, out, handlers = refs
        handlers[...] = (keys[...] // SLOTS).astype(jnp.float32)
        piece = keys[...] % SLOTS
    me = device_number()
    size = keys.shape[1]
    mine = handlers[...] == me.astype(jnp.float32)
    sender = lax.broadcasted_iota(jnp.int32, (devices, size), 0)
    first = lax.broadcasted_iota(jnp.int32, (size, size), 0)
    second = lax.broadcasted_iota(jnp.int32, (size, size), 1)
    rank = dot_plain(jnp.where(mine, 1.0, 0.0), jnp.where(first <= second, 1.0, 0.0))
    comes = mine & (sender != me)
    column = lax.broadcasted_iota(jnp.int32, (devices, size), 1)
    found = jnp.full((devices, size), pieces, jnp.int32)
    for r in range(capacity):
        hit = comes & (rank == r + 1.0)
        at = jnp.sum(jnp.where(hit, piece - pieces, 0), axis=1, keepdims=True)
        found = jnp.where(column == r, pieces + at, found)
    out[0:devices, :] = found
    kept = jnp.sum(
        jnp.where(mine & (sender == me), piece - pieces, 0), axis=0, keepdims=True
    )
    out[devices : devices + 8, :] = jnp.broadcast_to(kept + pieces, (8, size))


def sum_kernel(table, arrived, own, out, own_out, pieces, *, devices, capacity):
    blocks = own.shape[0]
    zero = jnp.zeros((8, LANES), jnp.float32)

    def over_senders(act):
        def one(d, carry):
            for i in range(capacity):
                act(table[d, i], d * capacity + i)
            return carry

        lax.fori_loop(0, devices, one, 0, unroll=2)

    def over_kept(act):
        def one(k, carry):
            for i in range(8):
                act(table[devices, 8 * k + i], 8 * k + i)
            return carry

        lax.fori_loop(0, blocks // 8, one, 0)

    def clear(piece, at):
        pieces[piece] = zero

    def add(piece, at):
        pieces[piece] = pieces[piece] + arrived[at]

    def add_own(piece, at):
        pieces[piece] = pieces[piece] + own[at]

    def give(piece, at):
        out[at] = pieces[piece]

    def give_own(piece, at):
        own_out[at] = pieces[piece]

    over_senders(clear)
    over_kept(clear)
    over_senders(add)
    over_kept(add_own)
    over_senders(give)
    over_kept(give_own)


def unpack_kernel(info, back, own, out, stage):
    for b in range(16 * TILES // 8):
        stage[pl.ds(8 * b, 8), :] = jnp.where(info[2, b] != 0, own[b], back[info[1, b]])
    for j in range(TILES):
        for i in range(2):
            out[8 * i : 8 * i + 8, j * LANES : (j + 1) * LANES] = stage[
                pl.ds(j + i * 8 * TILES, 8, stride=TILES), :
            ]


def f32(*shape):
    return jax.ShapeDtypeStruct(shape, jnp.float32)


def body(concentration, diffusion, velocity, levels, grid_signs, owner_list, slot_list):
    dom_count = lax.axis_size("dom")
    devices = lax.axis_size("grid") * dom_count
    rows = concentration.shape[1]
    conc = concentration[0]
    dif = diffusion[0]
    blocks = owner_list.shape[1]
    capacity = 2 * blocks // devices

    own_keys = owner_list * SLOTS + slot_list
    keys = lax.all_to_all(
        jnp.broadcast_to(own_keys[:, None], (devices, 1, blocks)),
        ("grid", "dom"),
        split_axis=0,
        concat_axis=0,
        tiled=True,
    )[:, 0]

    up = [(i, i + 1) for i in range(dom_count - 1)]
    down = [(i + 1, i) for i in range(dom_count - 1)]
    low_rows = jnp.concatenate([conc[rows - 2 :], dif[rows - 1 :]], axis=0)
    high_rows = jnp.concatenate([conc[:3], dif[:2]], axis=0)
    low = lax.ppermute(low_rows.reshape(3, TILES, LANES), "dom", up)
    high = lax.ppermute(high_rows.reshape(5, TILES, LANES), "dom", down)

    lanes = pl.pallas_call(
        lane_kernel,
        out_shape=f32(2 * LANES, LANES),
        in_specs=[SM],
        out_specs=VM,
        compiler_params=params(),
        name="lane_matrix",
    )(levels)

    stepped, lead = pl.pallas_call(
        steps_kernel,
        out_shape=(f32(TILES, 24, LANES), f32(TILES, LANES)),
        in_specs=[SM, SM, VM, VM, VM, VM],
        out_specs=(VM, VM),
        scratch_shapes=[
            pltpu.VMEM((TILES + 2 * PAD, 24, LANES), jnp.float32),
            pltpu.VMEM((TILES + 2 * PAD, 24, LANES), jnp.float32),
            pltpu.VMEM((TILES, 24, LANES), jnp.float32),
        ],
        compiler_params=params(),
        name="steps",
    )(levels, velocity, conc, dif, low, high)

    balanced = capacity >= 8 and devices * SLOTS % LANES == 0 and devices <= 64
    info_shape = jax.ShapeDtypeStruct((8, blocks), jnp.int32)
    if balanced:
        key_rows = devices * SLOTS // LANES
        assigned, info = pl.pallas_call(
            functools.partial(
                balance_kernel, devices=devices, capacity=capacity // 2, full=capacity
            ),
            out_shape=(f32(key_rows, LANES), info_shape),
            in_specs=[VM],
            out_specs=(VM, VM),
            scratch_shapes=[
                pltpu.VMEM((key_rows * devices, LANES), jnp.float32),
                pltpu.VMEM((key_rows * devices, LANES), jnp.float32),
                pltpu.VMEM((key_rows, LANES), jnp.float32),
            ],
            compiler_params=params(),
            name="balance",
        )(keys)
    else:
        info = pl.pallas_call(
            functools.partial(owner_places_kernel, devices=devices, capacity=capacity),
            out_shape=info_shape,
            in_specs=[VM],
            out_specs=VM,
            compiler_params=params(),
            name="places",
        )(keys)

    coarse = None
    distance = 1
    while distance < dom_count:
        targets = range(distance, dom_count, 2 * distance)
        pairs = [[(d - distance, d) for d in targets]]
        if distance > 1:
            pairs.append([(d + distance, d) for d in targets if d + distance < dom_count])
        for pair in pairs:
            if pair:
                part = lax.ppermute(lead, "dom", pair)
                coarse = part if coarse is None else coarse + part
        distance *= 2

    def route(slots, balanced, tables):
        pieces = devices * SLOTS if balanced else SLOTS

        def exchange(x):
            return lax.all_to_all(
                x.reshape(devices, slots * 8, LANES),
                ("grid", "dom"),
                split_axis=0,
                concat_axis=0,
                tiled=True,
            ).reshape(devices * slots, 8, LANES)

        outgoing, own = pl.pallas_call(
            pack_kernel,
            out_shape=(f32(devices * slots + 1, 8, LANES), f32(blocks, 8, LANES)),
            in_specs=[SM, SM, SM, VM, VM, VM],
            out_specs=(VM, VM),
            scratch_shapes=[
                pltpu.VMEM((TILES + 1, 16, LANES), jnp.float32),
                pltpu.VMEM((TILES + 64, 16, LANES), jnp.float32),
                pltpu.VMEM((16 * TILES, LANES), jnp.float32),
            ],
            compiler_params=params(),
            name="pack",
        )(levels, grid_signs, info, stepped, coarse, lanes)
        arrived = exchange(outgoing[: devices * slots])
        table = pl.pallas_call(
            functools.partial(
                table_kernel, devices=devices, capacity=slots, pieces=pieces, balanced=balanced
            ),
            out_shape=jax.ShapeDtypeStruct((devices + 8, blocks), jnp.int32),
            in_specs=[VM] * len(tables),
            out_specs=VM,
            scratch_shapes=[pltpu.VMEM((devices, blocks), jnp.float32)],
            compiler_params=params(),
            name="piece_table",
        )(*tables)
        returned, own_back = pl.pallas_call(
            functools.partial(sum_kernel, devices=devices, capacity=slots),
            out_shape=(f32(devices * slots, 8, LANES), f32(blocks, 8, LANES)),
            in_specs=[SM, VM, VM],
            out_specs=(VM, VM),
            scratch_shapes=[pltpu.VMEM((pieces + 8, 8, LANES), jnp.float32)],
            compiler_params=params(),
            name="sum_pieces",
        )(table, arrived, own)
        back = exchange(returned)
        return pl.pallas_call(
            unpack_kernel,
            out_shape=f32(rows, TILES * LANES),
            in_specs=[SM, VM, VM],
            out_specs=VM,
            scratch_shapes=[pltpu.VMEM((16 * TILES, LANES), jnp.float32)],
            compiler_params=params(),
            name="unpack",
        )(info, back, own_back)

    if balanced:
        combined = lax.cond(
            info[3, 0] != 0,
            lambda: route(capacity // 2, True, (keys, assigned)),
            lambda: route(capacity, True, (keys, assigned)),
        )
    else:
        combined = route(capacity, False, (keys,))
    return combined[None]


def solution(mesh):
    return jax.shard_map(
        body,
        mesh=mesh,
        in_specs=(
            P("grid", "dom", None),
            P("grid", "dom", None),
            P(),
            P("grid", None),
            P("grid"),
            P(("grid", "dom"), None),
            P(("grid", "dom"), None),
        ),
        out_specs=P("grid", "dom", None),
        check_vma=False,
    )
```

```python
import functools

import jax
import jax.numpy as jnp
from jax import lax
from jax.experimental import pallas as pl
from jax.experimental.pallas import tpu as pltpu
from jax.sharding import PartitionSpec as P

LR = 13
BLK = 1024
SLOTS = 64
LANES = 128
TILES = 2**LR // LANES
PAD = 9
VMEM_LIMIT = 48 * 1024 * 1024


def params():
    return pltpu.CompilerParams(vmem_limit_bytes=VMEM_LIMIT)


VM = pl.BlockSpec(memory_space=pltpu.VMEM)
SM = pl.BlockSpec(memory_space=pltpu.SMEM)


def grid_step(first_bits, second_bits, weights, valid, src, dst, dif, lane_two, lane_three):
    lane = lax.broadcasted_iota(jnp.int32, (1, LANES), 1)
    first_mask = (1 << first_bits) - 1
    stride_two = 1 << first_bits
    stride_three = 1 << (first_bits + second_bits)
    two_mask = stride_three - 1
    up_one = (lane & first_mask) != first_mask
    down_one = (lane & first_mask) != 0

    def rolled(tile, stride):
        return pltpu.roll(tile, LANES - stride, 1), pltpu.roll(tile, stride, 1)

    def neighbours(j, x, nxt, stride, in_lanes, carry):
        if not in_lanes:
            step = stride // LANES
            return src[PAD + j + step], src[PAD + j - step], carry
        up_here, down_here, down_last = carry
        up_next, down_next = rolled(nxt, stride)
        ahead = jnp.where(lane < LANES - stride, up_here, up_next)
        before = jnp.where(lane >= stride, down_here, down_last)
        return ahead, before, (up_next, down_next, down_here)

    def one_tile(j, carry):
        x, carry_two, carry_three = carry
        nxt = src[PAD + j + 1]
        ahead = jnp.where(up_one, pltpu.roll(x, LANES - 1, 1), 0.0)
        before = jnp.where(down_one, pltpu.roll(x, 1, 1), 0.0)
        total = ahead + before
        drift = weights[0] * (ahead - before)
        ahead, before, carry_two = neighbours(j, x, nxt, stride_two, lane_two, carry_two)
        node = (j * LANES + lane) & two_mask
        ahead = jnp.where(node < stride_three - stride_two, ahead, 0.0)
        before = jnp.where(node >= stride_two, before, 0.0)
        total = total + (ahead + before)
        drift = drift + weights[1] * (ahead - before)
        ahead, before, carry_three = neighbours(j, x, nxt, stride_three, lane_three, carry_three)
        total = total + (ahead + before)
        drift = drift + weights[2] * (ahead - before)
        ahead = pltpu.roll(x, 23, 0)
        before = pltpu.roll(x, 1, 0)
        total = total + (ahead + before)
        drift = drift + weights[3] * (ahead - before)
        new = x + dif[j] * (total - 8.0 * x) - drift
        dst[PAD + j] = jnp.where(valid, new, 0.0)
        return nxt, carry_two, carry_three

    def start(stride, in_lanes):
        if not in_lanes:
            return ()
        up_here, down_here = rolled(src[PAD], stride)
        return up_here, down_here, jnp.zeros((24, LANES), jnp.float32)

    def several(k, carry):
        for i in range(4):
            carry = one_tile(4 * k + i, carry)
        return carry

    lax.fori_loop(
        0,
        TILES // 4,
        several,
        (src[PAD], start(stride_two, lane_two), start(stride_three, lane_three)),
    )


def steps_kernel(levels, velocity, conc, dif_in, low, high, out, lead, u_a, u_b, dif):
    place = lax.axis_index("dom")
    count = lax.axis_size("dom")
    zeros = jnp.zeros((PAD, 24, LANES), jnp.float32)
    for ref in (u_a, u_b):
        ref[pl.ds(0, PAD)] = zeros
        ref[pl.ds(PAD + TILES, PAD)] = zeros
    tail = jnp.zeros((8, LANES), jnp.float32)
    for j in range(TILES):
        cols = pl.ds(j * LANES, LANES)
        u_a[PAD + j, 0:16] = conc[:, cols]
        u_a[PAD + j, 16:24] = tail
        dif[j, 0:16] = 0.1 * dif_in[:, cols]
        dif[j, 16:24] = tail
    for i in range(3):
        u_a[PAD : PAD + TILES, 16 + i] = high[i]
    for i in range(2):
        u_a[PAD : PAD + TILES, 22 + i] = low[i]
        dif[:, 16 + i] = 0.1 * high[3 + i]
    dif[:, 23] = 0.1 * low[2]
    row = lax.broadcasted_iota(jnp.int32, (24, LANES), 0)
    valid = (row < 16) | ((row < 20) & (place < count - 1)) | ((row >= 20) & (place > 0))
    weights = [0.1 * velocity[d] for d in range(4)]
    first_bits = levels[0, 0]
    second_bits = levels[0, 1]

    def both(lane_two, lane_three):
        def run():
            for src, dst in ((u_a, u_b), (u_b, u_a)):
                grid_step(
                    first_bits, second_bits, weights, valid, src, dst, dif, lane_two, lane_three
                )

        return run

    small_two = first_bits < 7
    small_three = first_bits + second_bits < 7
    pl.when(small_three)(both(True, True))
    pl.when(small_two & jnp.logical_not(small_three))(both(True, False))
    pl.when(jnp.logical_not(small_two))(both(False, False))
    out[...] = u_a[PAD : PAD + TILES]
    lead[...] = u_a[PAD : PAD + TILES, 0]


def bit_ends(levels, q):
    one = levels[0, 0]
    two = one + levels[0, 1]
    begin = jnp.where(q < one, 0, jnp.where(q < two, one, two))
    end = jnp.where(q < one, one, jnp.where(q < two, two, LR))
    return begin, end


def lane_kernel(levels, out):
    rows = lax.broadcasted_iota(jnp.int32, (LANES, LANES), 0)
    lane = lax.broadcasted_iota(jnp.int32, (LANES, LANES), 1)
    own = (rows == lane).astype(jnp.float32)
    nxt = jnp.zeros((LANES, LANES), jnp.float32)
    for q in range(7):
        begin, end = bit_ends(levels, q)
        below = (1 << q) - (1 << begin)
        above = (1 << jnp.minimum(end, 7)) - (2 << q)
        here = ((lane & below) == 0) & ((lane & (1 << q)) != 0)
        full = (lane & above) == above
        ahead = pltpu.roll(own, LANES - (1 << q), 1)
        before = pltpu.roll(own, 1 << q, 1)
        half = jnp.where(here, -0.5, 0.0)
        nxt = nxt + jnp.where(full & (end > 7), half * ahead, 0.0)
        own = own + half * (before + jnp.where(full, 0.0, ahead))
    out[0:LANES] = own
    out[LANES : 2 * LANES] = nxt


def surplus_rows(levels, sign, x, y, lanes, stage):
    x[TILES] = jnp.zeros((8, LANES), jnp.float32)
    y[pl.ds(0, 32)] = jnp.zeros((32, 8, LANES), jnp.float32)
    y[pl.ds(32 + TILES, 32)] = jnp.zeros((32, 8, LANES), jnp.float32)

    _, end_six = bit_ends(levels, 6)
    mask_six = (1 << (jnp.maximum(end_six, 7) - 7)) - 1
    chunk = 16
    matrix = lanes[...]
    for j0 in range(0, TILES, chunk):
        own = x[pl.ds(j0, chunk)].reshape(chunk * 8, LANES)
        nxt = jnp.concatenate(
            [
                jnp.where(((j0 + i) & mask_six) == mask_six, 0.0, x[j0 + i + 1])
                for i in range(chunk)
            ],
            axis=0,
        )
        res = jnp.dot(
            jnp.concatenate([own, nxt], axis=1),
            matrix,
            precision=lax.Precision.HIGHEST,
            preferred_element_type=jnp.float32,
        )
        y[pl.ds(32 + j0, chunk)] = res.reshape(chunk, 8, LANES)

    lane = lax.broadcasted_iota(jnp.int32, (1, LANES), 1)
    for q in range(7, LR):
        t = 1 << (q - 7)
        begin, end = bit_ends(levels, q)
        low_lane = 128 - (1 << jnp.minimum(begin, 7))
        half = jnp.where((lane & low_lane) == 0, -0.5, 0.0)
        below = t - (1 << (jnp.maximum(begin, 7) - 7))
        above = (1 << (end - 7)) - 2 * t
        for j in range(TILES):
            if j & t:
                mine = jnp.where((j & below) == 0, half, 0.0)
                ahead_on = jnp.where((j & above) == above, 0.0, 1.0)
                y[32 + j] = y[32 + j] + mine * (y[32 + j - t] + ahead_on * y[32 + j + t])

    factor = sign[0].astype(jnp.float32)
    for j in range(TILES):
        stage[pl.ds(j, 8, stride=TILES), :] = factor * y[32 + j]


def upper_rows_kernel(levels, sign, v_in, lanes, low_out, out, x, y, stage):
    place = lax.axis_index("dom")
    row = lax.broadcasted_iota(jnp.int32, (24, LANES), 0)
    for j in range(TILES):
        tile = v_in[j]
        for p in range(4):
            s = 1 << p
            both = pltpu.roll(tile, 24 - s, 0) + pltpu.roll(tile, s, 0)
            hit = ((row & (2 * s - 1)) == s) & (row < 16)
            tile = tile - 0.5 * jnp.where(hit, both, 0.0)
        low_out[j] = tile[0:8]
        x[j] = tile[8:16]
    own_upper = jnp.where((place & 1) == 1, 0.5, 0.0)
    low_out[:, 0] = low_out[:, 0] - own_upper * v_in[:, 16]
    surplus_rows(levels, sign, x, y, lanes, stage)
    for b in range(TILES):
        out[b] = stage[pl.ds(8 * b, 8), :]


def pack_kernel(levels, sign, info, low, coarse, lanes, upper, out, blocks, x, y, stage):
    x[0:TILES] = low[...]
    x[0:TILES, 0] = x[0:TILES, 0] - 0.5 * coarse[...]
    surplus_rows(levels, sign, x, y, lanes, stage)
    for b in range(TILES):
        block = stage[pl.ds(8 * b, 8), :]
        blocks[b] = block
        out[info[0, b]] = block
    for b in range(TILES):
        block = upper[b]
        blocks[TILES + b] = block
        out[info[0, TILES + b]] = block


def key_parts(keys, rows):
    owner = keys // SLOTS
    slot = keys % SLOTS
    row = owner % rows
    lane = slot + SLOTS * (owner // rows)
    return owner, slot, lane, row, (row + slot) % rows


def hot(index, count):
    which = lax.broadcasted_iota(jnp.int32, (count, index.shape[1]), 0)
    return jnp.where(which == index, 1.0, 0.0)


def dot_rows(left, right):
    return lax.dot_general(
        left.astype(jnp.bfloat16),
        right.astype(jnp.bfloat16),
        (((1,), (1,)), ((), ())),
        preferred_element_type=jnp.float32,
    )


def dot_plain(left, right):
    return jnp.dot(
        left.astype(jnp.bfloat16), right.astype(jnp.bfloat16), preferred_element_type=jnp.float32
    )


def mixed(handler, lane, row):
    x = (handler * 40503 + lane * 30011 + row * 52711) & 0xFFFF
    x = ((x ^ (x >> 7)) * 9973) & 0xFFFF
    x = ((x ^ (x >> 5)) * 12347) & 0xFFFF
    return (x >> 8).astype(jnp.float32) * (1.0 / 256.0)


def handlers_of(assigned, lane, row):
    return jnp.sum(
        hot(row, assigned.shape[0]) * dot_plain(assigned, hot(lane, LANES)), axis=0, keepdims=True
    )


def device_number():
    return lax.axis_index("grid") * lax.axis_size("dom") + lax.axis_index("dom")


def write_places(info, handler, ok, me, devices, capacity):
    taken = hot(handler.astype(jnp.int32), devices)
    size = handler.shape[1]
    first = lax.broadcasted_iota(jnp.int32, (size, size), 0)
    second = lax.broadcasted_iota(jnp.int32, (size, size), 1)
    before = dot_plain(taken, jnp.where(first < second, 1.0, 0.0))
    rank = jnp.sum(taken * before, axis=0, keepdims=True)
    place = handler.astype(jnp.int32) * capacity + rank.astype(jnp.int32)
    stays = handler == me.astype(jnp.float32)
    send = jnp.where(stays, me * capacity, place)
    get = jnp.where(stays, 0, place)
    kept = jnp.where(stays, 1, 0)
    flag = jnp.broadcast_to(ok, kept.shape).astype(jnp.int32)
    rows = [send, get, kept, flag, flag, flag, flag, flag]
    info[...] = jnp.concatenate(rows, axis=0)


def owner_places_kernel(keys, info, *, devices, capacity):
    me = device_number()
    owner = (keys[pl.ds(me, 1), :] // SLOTS).astype(jnp.float32)
    write_places(info, owner, jnp.int32(0), me, devices, capacity)


def balance_kernel(keys, assigned, info, one, two, table, *, devices, capacity, full):
    rows = devices * SLOTS // LANES
    keys_all = keys[...]
    _, _, lane_all, row_one, row_two = key_parts(keys_all, rows)
    for d in range(devices):
        pick = slice(d, d + 1)
        both = jnp.concatenate([hot(row_one[pick], rows), hot(row_two[pick], rows)], axis=0)
        counts = dot_rows(both, hot(lane_all[pick], LANES))
        one[pl.ds(d, rows, stride=devices), :] = counts[:rows]
        two[pl.ds(d, rows, stride=devices), :] = counts[rows:]

    square = (devices, devices)
    own = lax.broadcasted_iota(jnp.int32, square, 0) == lax.broadcasted_iota(jnp.int32, square, 1)

    def price(load, steep):
        value = jnp.exp2(load * 0.3785) + steep * jnp.maximum(load - (capacity - 1), 0.0)
        return jnp.where(own, 0.0, value)

    def settle(counts_ref, group, first, load, number):
        base = number * group
        counts = jnp.concatenate(
            [
                counts_ref[pl.ds(pl.multiple_of((base + i) * devices, devices), devices), :]
                for i in range(group)
            ],
            axis=1,
        )
        shape = (devices, group * LANES)
        handler = lax.broadcasted_iota(jnp.int32, shape, 0)
        column = lax.broadcasted_iota(jnp.int32, shape, 1)
        handler_f = handler.astype(jnp.float32)
        cost = dot_plain(price(load, 4.0 if first else 8.0), counts)
        was = None
        if not first:
            old = jnp.concatenate([table[pl.ds(base + i, 1), :] for i in range(group)], axis=1)
            was = handler_f == old
            cost = jnp.where(was, dot_plain(price(load - 1.0, 8.0), counts) - 1.0, cost)
        noise = 0.5 * mixed(handler, column % LANES, base + column // LANES)
        ranked = jnp.floor((jnp.minimum(cost, 4000.0) + noise) * 64.0) * devices + handler_f
        least = jnp.min(ranked, axis=0, keepdims=True)
        chosen = least - jnp.floor(least * (1.0 / devices)) * devices
        for i in range(group):
            table[pl.ds(base + i, 1), :] = chosen[:, i * LANES : (i + 1) * LANES]
        change = jnp.where(handler_f == chosen, 1.0, 0.0)
        if not first:
            change = change - jnp.where(was, 1.0, 0.0)
        return load + dot_rows(change, counts)

    load = jnp.zeros(square, jnp.float32)
    load = lax.fori_loop(0, rows // 2, lambda i, x: settle(one, 2, True, x, i), load)
    spot = lax.broadcasted_iota(jnp.int32, (rows, LANES), 0)
    lane = lax.broadcasted_iota(jnp.int32, (rows, LANES), 1)
    from_row = (spot + rows - (lane % SLOTS) % rows) % rows
    moved = jnp.zeros((rows, LANES), jnp.float32)
    for r in range(rows):
        moved = jnp.where(from_row == r, table[r : r + 1, :], moved)
    table[...] = moved
    load = lax.fori_loop(0, rows // 2, lambda i, x: settle(two, 2, False, x, i), load)
    load = lax.fori_loop(0, rows // 4, lambda i, x: settle(two, 4, False, x, i), load)

    ok = jnp.max(jnp.where(own, 0.0, load)) <= capacity
    owner = (from_row + rows * (lane // SLOTS)).astype(jnp.float32)
    final = jnp.where(ok, table[...], owner)
    assigned[...] = final
    me = device_number()
    _, _, my_lane, _, my_row = key_parts(keys[pl.ds(me, 1), :], rows)
    handler = handlers_of(final, my_lane, my_row)
    size = jnp.where(ok, capacity, full)
    write_places(info, handler, ok.astype(jnp.int32), me, devices, size)


def table_kernel(*refs, devices, capacity, pieces, balanced):
    if balanced:
        keys, assigned, out, handlers = refs
        rows = devices * SLOTS // LANES
        table = assigned[...]
        _, _, lane_all, _, row_all = key_parts(keys[...], rows)
        for d in range(devices):
            handlers[d : d + 1, :] = handlers_of(table, lane_all[d : d + 1], row_all[d : d + 1])
        piece = keys[...]
    else:
        keys, out, handlers = refs
        handlers[...] = (keys[...] // SLOTS).astype(jnp.float32)
        piece = keys[...] % SLOTS
    me = device_number()
    size = keys.shape[1]
    mine = handlers[...] == me.astype(jnp.float32)
    sender = lax.broadcasted_iota(jnp.int32, (devices, size), 0)
    first = lax.broadcasted_iota(jnp.int32, (size, size), 0)
    second = lax.broadcasted_iota(jnp.int32, (size, size), 1)
    rank = dot_plain(jnp.where(mine, 1.0, 0.0), jnp.where(first <= second, 1.0, 0.0))
    comes = mine & (sender != me)
    column = lax.broadcasted_iota(jnp.int32, (devices, size), 1)
    found = jnp.full((devices, size), pieces, jnp.int32)
    for r in range(capacity):
        hit = comes & (rank == r + 1.0)
        at = jnp.sum(jnp.where(hit, piece - pieces, 0), axis=1, keepdims=True)
        found = jnp.where(column == r, pieces + at, found)
    out[0:devices, :] = found
    kept = jnp.sum(
        jnp.where(mine & (sender == me), piece - pieces, 0), axis=0, keepdims=True
    )
    out[devices : devices + 8, :] = jnp.broadcast_to(kept + pieces, (8, size))


def sum_kernel(table, arrived, own, out, own_out, pieces, *, devices, capacity):
    blocks = own.shape[0]
    zero = jnp.zeros((8, LANES), jnp.float32)

    def over_senders(act):
        def one(d, carry):
            for i in range(capacity):
                act(table[d, i], d * capacity + i)
            return carry

        lax.fori_loop(0, devices, one, 0, unroll=2)

    def over_kept(act):
        def one(k, carry):
            for i in range(8):
                act(table[devices, 8 * k + i], 8 * k + i)
            return carry

        lax.fori_loop(0, blocks // 8, one, 0)

    def clear(piece, at):
        pieces[piece] = zero

    def add(piece, at):
        pieces[piece] = pieces[piece] + arrived[at]

    def add_own(piece, at):
        pieces[piece] = pieces[piece] + own[at]

    def give(piece, at):
        out[at] = pieces[piece]

    def give_own(piece, at):
        own_out[at] = pieces[piece]

    over_senders(clear)
    over_kept(clear)
    over_senders(add)
    over_kept(add_own)
    over_senders(give)
    over_kept(give_own)


def unpack_kernel(info, back, own, out, stage):
    for b in range(16 * TILES // 8):
        stage[pl.ds(8 * b, 8), :] = jnp.where(info[2, b] != 0, own[b], back[info[1, b]])
    for j in range(TILES):
        for i in range(2):
            out[8 * i : 8 * i + 8, j * LANES : (j + 1) * LANES] = stage[
                pl.ds(j + i * 8 * TILES, 8, stride=TILES), :
            ]


def f32(*shape):
    return jax.ShapeDtypeStruct(shape, jnp.float32)


def body(concentration, diffusion, velocity, levels, grid_signs, owner_list, slot_list):
    dom_count = lax.axis_size("dom")
    devices = lax.axis_size("grid") * dom_count
    rows = concentration.shape[1]
    conc = concentration[0]
    dif = diffusion[0]
    blocks = owner_list.shape[1]
    capacity = 2 * blocks // devices

    own_keys = owner_list * SLOTS + slot_list
    keys = lax.all_to_all(
        jnp.broadcast_to(own_keys[:, None], (devices, 1, blocks)),
        ("grid", "dom"),
        split_axis=0,
        concat_axis=0,
        tiled=True,
    )[:, 0]

    up = [(i, i + 1) for i in range(dom_count - 1)]
    down = [(i + 1, i) for i in range(dom_count - 1)]
    low_rows = jnp.concatenate([conc[rows - 2 :], dif[rows - 1 :]], axis=0)
    high_rows = jnp.concatenate([conc[:3], dif[:2]], axis=0)
    low = lax.ppermute(low_rows.reshape(3, TILES, LANES), "dom", up)
    high = lax.ppermute(high_rows.reshape(5, TILES, LANES), "dom", down)

    lanes = pl.pallas_call(
        lane_kernel,
        out_shape=f32(2 * LANES, LANES),
        in_specs=[SM],
        out_specs=VM,
        compiler_params=params(),
        name="lane_matrix",
    )(levels)

    balanced = capacity >= 8 and devices * SLOTS % LANES == 0 and devices <= 64
    info_shape = jax.ShapeDtypeStruct((8, blocks), jnp.int32)
    if balanced:
        key_rows = devices * SLOTS // LANES
        assigned, info = pl.pallas_call(
            functools.partial(
                balance_kernel, devices=devices, capacity=capacity // 2, full=capacity
            ),
            out_shape=(f32(key_rows, LANES), info_shape),
            in_specs=[VM],
            out_specs=(VM, VM),
            scratch_shapes=[
                pltpu.VMEM((key_rows * devices, LANES), jnp.float32),
                pltpu.VMEM((key_rows * devices, LANES), jnp.float32),
                pltpu.VMEM((key_rows, LANES), jnp.float32),
            ],
            compiler_params=params(),
            name="balance",
        )(keys)
    else:
        info = pl.pallas_call(
            functools.partial(owner_places_kernel, devices=devices, capacity=capacity),
            out_shape=info_shape,
            in_specs=[VM],
            out_specs=VM,
            compiler_params=params(),
            name="places",
        )(keys)

    low, high, info = lax.optimization_barrier((low, high, info))

    stepped, lead = pl.pallas_call(
        steps_kernel,
        out_shape=(f32(TILES, 24, LANES), f32(TILES, LANES)),
        in_specs=[SM, SM, VM, VM, VM, VM],
        out_specs=(VM, VM),
        scratch_shapes=[
            pltpu.VMEM((TILES + 2 * PAD, 24, LANES), jnp.float32),
            pltpu.VMEM((TILES + 2 * PAD, 24, LANES), jnp.float32),
            pltpu.VMEM((TILES, 24, LANES), jnp.float32),
        ],
        compiler_params=params(),
        name="steps",
    )(levels, velocity, conc, dif, low, high)

    coarse = None
    distance = 1
    while distance < dom_count:
        targets = range(distance, dom_count, 2 * distance)
        pairs = [[(d - distance, d) for d in targets]]
        if distance > 1:
            pairs.append([(d + distance, d) for d in targets if d + distance < dom_count])
        for pair in pairs:
            if pair:
                part = lax.ppermute(lead, "dom", pair)
                coarse = part if coarse is None else coarse + part
        distance *= 2

    row_scratch = [
        pltpu.VMEM((TILES + 1, 8, LANES), jnp.float32),
        pltpu.VMEM((TILES + 64, 8, LANES), jnp.float32),
        pltpu.VMEM((8 * TILES, LANES), jnp.float32),
    ]
    low_half, high_half = pl.pallas_call(
        upper_rows_kernel,
        out_shape=(f32(TILES, 8, LANES), f32(TILES, 8, LANES)),
        in_specs=[SM, SM, VM, VM],
        out_specs=(VM, VM),
        scratch_shapes=row_scratch,
        compiler_params=params(),
        name="upper_rows",
    )(levels, grid_signs, stepped, lanes)

    def route(slots, balanced, tables):
        pieces = devices * SLOTS if balanced else SLOTS

        def exchange(x):
            return lax.all_to_all(
                x.reshape(devices, slots * 8, LANES),
                ("grid", "dom"),
                split_axis=0,
                concat_axis=0,
                tiled=True,
            ).reshape(devices * slots, 8, LANES)

        outgoing, own = pl.pallas_call(
            pack_kernel,
            out_shape=(f32(devices * slots, 8, LANES), f32(blocks, 8, LANES)),
            in_specs=[SM, SM, SM, VM, VM, VM, VM],
            out_specs=(VM, VM),
            scratch_shapes=row_scratch,
            compiler_params=params(),
            name="pack",
        )(levels, grid_signs, info, low_half, coarse, lanes, high_half)
        arrived = exchange(outgoing)
        table = pl.pallas_call(
            functools.partial(
                table_kernel, devices=devices, capacity=slots, pieces=pieces, balanced=balanced
            ),
            out_shape=jax.ShapeDtypeStruct((devices + 8, blocks), jnp.int32),
            in_specs=[VM] * len(tables),
            out_specs=VM,
            scratch_shapes=[pltpu.VMEM((devices, blocks), jnp.float32)],
            compiler_params=params(),
            name="piece_table",
        )(*tables)
        returned, own_back = pl.pallas_call(
            functools.partial(sum_kernel, devices=devices, capacity=slots),
            out_shape=(f32(devices * slots, 8, LANES), f32(blocks, 8, LANES)),
            in_specs=[SM, VM, VM],
            out_specs=(VM, VM),
            scratch_shapes=[pltpu.VMEM((pieces + 8, 8, LANES), jnp.float32)],
            compiler_params=params(),
            name="sum_pieces",
        )(table, arrived, own)
        back = exchange(returned)
        return pl.pallas_call(
            unpack_kernel,
            out_shape=f32(rows, TILES * LANES),
            in_specs=[SM, VM, VM],
            out_specs=VM,
            scratch_shapes=[pltpu.VMEM((16 * TILES, LANES), jnp.float32)],
            compiler_params=params(),
            name="unpack",
        )(info, back, own_back)

    if balanced:
        combined = lax.cond(
            info[3, 0] != 0,
            lambda: route(capacity // 2, True, (keys, assigned)),
            lambda: route(capacity, True, (keys, assigned)),
        )
    else:
        combined = route(capacity, False, (keys,))
    return combined[None]


def solution(mesh):
    return jax.shard_map(
        body,
        mesh=mesh,
        in_specs=(
            P("grid", "dom", None),
            P("grid", "dom", None),
            P(),
            P("grid", None),
            P("grid"),
            P(("grid", "dom"), None),
            P(("grid", "dom"), None),
        ),
        out_specs=P("grid", "dom", None),
        check_vma=False,
    )
```

```python
import functools

import jax
import jax.numpy as jnp
from jax import lax
from jax.experimental import pallas as pl
from jax.experimental.pallas import tpu as pltpu
from jax.sharding import PartitionSpec as P

LR = 13
BLK = 1024
SLOTS = 64
LANES = 128
TILES = 2**LR // LANES
PAD = 9
VMEM_LIMIT = 48 * 1024 * 1024


def params():
    return pltpu.CompilerParams(vmem_limit_bytes=VMEM_LIMIT)


SMALL = pl.CostEstimate(flops=0, transcendentals=0, bytes_accessed=0)
VM = pl.BlockSpec(memory_space=pltpu.VMEM)
SM = pl.BlockSpec(memory_space=pltpu.SMEM)


def grid_step(first_bits, second_bits, weights, valid, src, dst, dif, lane_two, lane_three):
    lane = lax.broadcasted_iota(jnp.int32, (1, LANES), 1)
    first_mask = (1 << first_bits) - 1
    stride_two = 1 << first_bits
    stride_three = 1 << (first_bits + second_bits)
    two_mask = stride_three - 1
    up_one = (lane & first_mask) != first_mask
    down_one = (lane & first_mask) != 0

    def rolled(tile, stride):
        return pltpu.roll(tile, LANES - stride, 1), pltpu.roll(tile, stride, 1)

    def neighbours(j, x, nxt, stride, in_lanes, carry):
        if not in_lanes:
            step = stride // LANES
            return src[PAD + j + step], src[PAD + j - step], carry
        up_here, down_here, down_last = carry
        up_next, down_next = rolled(nxt, stride)
        ahead = jnp.where(lane < LANES - stride, up_here, up_next)
        before = jnp.where(lane >= stride, down_here, down_last)
        return ahead, before, (up_next, down_next, down_here)

    def one_tile(j, carry):
        x, carry_two, carry_three = carry
        nxt = src[PAD + j + 1]
        ahead = jnp.where(up_one, pltpu.roll(x, LANES - 1, 1), 0.0)
        before = jnp.where(down_one, pltpu.roll(x, 1, 1), 0.0)
        total = ahead + before
        drift = weights[0] * (ahead - before)
        ahead, before, carry_two = neighbours(j, x, nxt, stride_two, lane_two, carry_two)
        node = (j * LANES + lane) & two_mask
        ahead = jnp.where(node < stride_three - stride_two, ahead, 0.0)
        before = jnp.where(node >= stride_two, before, 0.0)
        total = total + (ahead + before)
        drift = drift + weights[1] * (ahead - before)
        ahead, before, carry_three = neighbours(j, x, nxt, stride_three, lane_three, carry_three)
        total = total + (ahead + before)
        drift = drift + weights[2] * (ahead - before)
        ahead = pltpu.roll(x, 23, 0)
        before = pltpu.roll(x, 1, 0)
        total = total + (ahead + before)
        drift = drift + weights[3] * (ahead - before)
        new = x + dif[j] * (total - 8.0 * x) - drift
        dst[PAD + j] = jnp.where(valid, new, 0.0)
        return nxt, carry_two, carry_three

    def start(stride, in_lanes):
        if not in_lanes:
            return ()
        up_here, down_here = rolled(src[PAD], stride)
        return up_here, down_here, jnp.zeros((24, LANES), jnp.float32)

    def several(k, carry):
        for i in range(4):
            carry = one_tile(4 * k + i, carry)
        return carry

    lax.fori_loop(
        0,
        TILES // 4,
        several,
        (src[PAD], start(stride_two, lane_two), start(stride_three, lane_three)),
    )


def bit_ends(levels, q):
    one = levels[0, 0]
    two = one + levels[0, 1]
    begin = jnp.where(q < one, 0, jnp.where(q < two, one, two))
    end = jnp.where(q < one, one, jnp.where(q < two, two, LR))
    return begin, end


def lane_matrix(levels):
    rows = lax.broadcasted_iota(jnp.int32, (LANES, LANES), 0)
    lane = lax.broadcasted_iota(jnp.int32, (LANES, LANES), 1)
    own = (rows == lane).astype(jnp.float32)
    nxt = jnp.zeros((LANES, LANES), jnp.float32)
    for q in range(7):
        begin, end = bit_ends(levels, q)
        below = (1 << q) - (1 << begin)
        above = (1 << jnp.minimum(end, 7)) - (2 << q)
        here = ((lane & below) == 0) & ((lane & (1 << q)) != 0)
        full = (lane & above) == above
        ahead = pltpu.roll(own, LANES - (1 << q), 1)
        before = pltpu.roll(own, 1 << q, 1)
        half = jnp.where(here, -0.5, 0.0)
        nxt = nxt + jnp.where(full & (end > 7), half * ahead, 0.0)
        own = own + half * (before + jnp.where(full, 0.0, ahead))
    return jnp.concatenate([own, nxt], axis=0)


def surplus_rows(levels, sign, x, y, matrix, stage):
    rows = x.shape[1]
    x[TILES] = jnp.zeros((rows, LANES), jnp.float32)
    y[pl.ds(0, 32)] = jnp.zeros((32, rows, LANES), jnp.float32)
    y[pl.ds(32 + TILES, 32)] = jnp.zeros((32, rows, LANES), jnp.float32)

    _, end_six = bit_ends(levels, 6)
    mask_six = (1 << (jnp.maximum(end_six, 7) - 7)) - 1
    chunk = 16
    for j0 in range(0, TILES, chunk):
        own = x[pl.ds(j0, chunk)].reshape(chunk * rows, LANES)
        nxt = jnp.concatenate(
            [
                jnp.where(((j0 + i) & mask_six) == mask_six, 0.0, x[j0 + i + 1])
                for i in range(chunk)
            ],
            axis=0,
        )
        res = jnp.dot(
            jnp.concatenate([own, nxt], axis=1),
            matrix,
            precision=lax.Precision.HIGHEST,
            preferred_element_type=jnp.float32,
        )
        y[pl.ds(32 + j0, chunk)] = res.reshape(chunk, rows, LANES)

    lane = lax.broadcasted_iota(jnp.int32, (1, LANES), 1)
    for q in range(7, LR):
        t = 1 << (q - 7)
        begin, end = bit_ends(levels, q)
        low_lane = 128 - (1 << jnp.minimum(begin, 7))
        half = jnp.where((lane & low_lane) == 0, -0.5, 0.0)
        below = t - (1 << (jnp.maximum(begin, 7) - 7))
        above = (1 << (end - 7)) - 2 * t
        for j in range(TILES):
            if j & t:
                mine = jnp.where((j & below) == 0, half, 0.0)
                ahead_on = jnp.where((j & above) == above, 0.0, 1.0)
                y[32 + j] = y[32 + j] + mine * (y[32 + j - t] + ahead_on * y[32 + j + t])

    factor = sign[0].astype(jnp.float32)
    for j in range(TILES):
        tile = factor * y[32 + j]
        for i in range(0, rows, 8):
            stage[pl.ds(j + i * TILES, 8, stride=TILES), :] = tile[i : i + 8]


def rows_kernel(
    levels, velocity, sign, conc, dif_in, low, high, out, lead, u_a, u_b, dif, x, y
):
    place = lax.axis_index("dom")
    count = lax.axis_size("dom")
    zeros = jnp.zeros((PAD, 24, LANES), jnp.float32)
    for ref in (u_a, u_b):
        ref[pl.ds(0, PAD)] = zeros
        ref[pl.ds(PAD + TILES, PAD)] = zeros
    tail = jnp.zeros((8, LANES), jnp.float32)
    for j in range(TILES):
        cols = pl.ds(j * LANES, LANES)
        u_a[PAD + j, 0:16] = conc[:, cols]
        u_a[PAD + j, 16:24] = tail
        dif[j, 0:16] = 0.1 * dif_in[:, cols]
        dif[j, 16:24] = tail
    for i in range(3):
        u_a[PAD : PAD + TILES, 16 + i] = high[i]
    for i in range(2):
        u_a[PAD : PAD + TILES, 22 + i] = low[i]
        dif[:, 16 + i] = 0.1 * high[3 + i]
    dif[:, 23] = 0.1 * low[2]
    row = lax.broadcasted_iota(jnp.int32, (24, LANES), 0)
    valid = (row < 16) | ((row < 20) & (place < count - 1)) | ((row >= 20) & (place > 0))
    weights = [0.1 * velocity[d] for d in range(4)]
    first_bits = levels[0, 0]
    second_bits = levels[0, 1]

    def both(lane_two, lane_three):
        def run():
            for src, dst in ((u_a, u_b), (u_b, u_a)):
                grid_step(
                    first_bits, second_bits, weights, valid, src, dst, dif, lane_two, lane_three
                )

        return run

    small_two = first_bits < 7
    small_three = first_bits + second_bits < 7
    pl.when(small_three)(both(True, True))
    pl.when(small_two & jnp.logical_not(small_three))(both(True, False))
    pl.when(jnp.logical_not(small_two))(both(False, False))
    lead[...] = u_a[PAD : PAD + TILES, 0]
    for j in range(TILES):
        tile = u_a[PAD + j]
        for p in range(4):
            s = 1 << p
            around = pltpu.roll(tile, 24 - s, 0) + pltpu.roll(tile, s, 0)
            hit = ((row & (2 * s - 1)) == s) & (row < 16)
            tile = tile - 0.5 * jnp.where(hit, around, 0.0)
        x[j] = tile[0:16]
    next_lead = u_a[PAD : PAD + TILES, 16]
    x[0:TILES, 0] = x[0:TILES, 0] - jnp.where((place & 1) == 1, 0.5, 0.0) * next_lead
    surplus_rows(levels, sign, x, y, lane_matrix(levels), out)


def fix_kernel(levels, sign, coarse, blocks, out, x, y, stage):
    x[...] = jnp.zeros_like(x)
    x[0:TILES, 0] = coarse[...]
    surplus_rows(levels, sign, x, y, lane_matrix(levels), stage)
    out[...] = blocks[...]
    out[0:TILES, :] = blocks[0:TILES, :] - 0.5 * stage[0:TILES, :]


def scatter_kernel(info, blocks, out, *, extras):
    for b in range(blocks.shape[0]):
        out[info[0, b]] = blocks[b]
    for i in range(extras):
        out[info[4, i]] = -0.5 * blocks[i % 8]


def row_zero_uses(dom_count):
    uses = []
    distance = 1
    while distance < dom_count:
        uses.append((distance, 2 * distance))
        if distance > 1 and dom_count > 2 * distance:
            uses.append((-distance, 2 * distance))
        distance *= 2
    return uses


def has_use(place, offset, period, dom_count):
    return (place % period == 0) & (place + offset >= 0) & (place + offset < dom_count)


def extra_entries(values, dom_count, fill):
    devices, size = values.shape
    place = lax.broadcasted_iota(jnp.int32, (devices, size), 0) % dom_count
    lane = lax.broadcasted_iota(jnp.int32, (devices, size), 1)
    res = jnp.full((devices, size), fill, values.dtype)
    for t, (offset, period) in enumerate(row_zero_uses(dom_count)):
        cut = offset % devices
        moved = jnp.concatenate([values[cut:], values[:cut]], axis=0)
        moved = pltpu.roll(moved, 8 * t, 1) if t else moved
        hit = (lane >= 8 * t) & (lane < 8 * t + 8) & has_use(place, offset, period, dom_count)
        res = jnp.where(hit, moved, res)
    return res


def key_parts(keys, rows):
    owner = keys // SLOTS
    slot = keys % SLOTS
    row = owner % rows
    lane = slot + SLOTS * (owner // rows)
    return owner, slot, lane, row, (row + slot) % rows


def hot(index, count):
    which = lax.broadcasted_iota(jnp.int32, (count, index.shape[1]), 0)
    return jnp.where(which == index, 1.0, 0.0)


def dot_rows(left, right):
    return lax.dot_general(
        left.astype(jnp.bfloat16),
        right.astype(jnp.bfloat16),
        (((1,), (1,)), ((), ())),
        preferred_element_type=jnp.float32,
    )


def dot_plain(left, right):
    return jnp.dot(
        left.astype(jnp.bfloat16), right.astype(jnp.bfloat16), preferred_element_type=jnp.float32
    )


def mixed(handler, lane, row):
    x = (handler * 40503 + lane * 30011 + row * 52711) & 0xFFFF
    x = ((x ^ (x >> 7)) * 9973) & 0xFFFF
    x = ((x ^ (x >> 5)) * 12347) & 0xFFFF
    return (x >> 8).astype(jnp.float32) * (1.0 / 256.0)


def handlers_of(assigned, lane, row):
    return jnp.sum(
        hot(row, assigned.shape[0]) * dot_plain(assigned, hot(lane, LANES)), axis=0, keepdims=True
    )


def device_number():
    return lax.axis_index("grid") * lax.axis_size("dom") + lax.axis_index("dom")


def write_places(info, handler, extra, ok, me, devices, capacity):
    size = handler.shape[1]
    first = lax.broadcasted_iota(jnp.int32, (size, size), 0)
    second = lax.broadcasted_iota(jnp.int32, (size, size), 1)
    earlier = jnp.where(first < second, 1.0, 0.0)

    def placed(which, ahead):
        taken = hot(which.astype(jnp.int32), devices)
        rank = jnp.sum(taken * (dot_plain(taken, earlier) + ahead), axis=0, keepdims=True)
        place = which.astype(jnp.int32) * capacity + rank.astype(jnp.int32)
        stays = (which == me.astype(jnp.float32)) | (which < 0.0)
        return jnp.where(stays, me * capacity, place), stays, taken

    send, stays, taken = placed(handler, 0.0)
    send_extra, _, _ = placed(extra, jnp.sum(taken, axis=1, keepdims=True))
    kept = jnp.where(stays, 1, 0)
    flag = jnp.broadcast_to(ok, kept.shape).astype(jnp.int32)
    info[...] = jnp.concatenate([send, send, kept, flag, send_extra, flag, flag, flag], axis=0)


def owner_places_kernel(keys, info, *, devices, capacity):
    me = device_number()
    owner = (keys[pl.ds(me, 1), :] // SLOTS).astype(jnp.float32)
    none = jnp.full(owner.shape, -1.0, jnp.float32)
    write_places(info, owner, none, jnp.int32(0), me, devices, capacity)


def balance_kernel(keys, assigned, info, one, two, table, *, devices, capacity, full):
    rows = devices * SLOTS // LANES
    keys_all = keys[...]
    _, _, lane_all, row_one, row_two = key_parts(keys_all, rows)
    dom_count = lax.axis_size("dom")
    lane_more, one_more, two_more = [
        extra_entries(v, dom_count, -1) for v in (lane_all, row_one, row_two)
    ]

    def counted(one_row, two_row, lane_row):
        both = jnp.concatenate([hot(one_row, rows), hot(two_row, rows)], axis=0)
        return dot_rows(both, hot(lane_row, LANES))

    for d in range(devices):
        pick = slice(d, d + 1)
        counts = counted(row_one[pick], row_two[pick], lane_all[pick])
        place = d % dom_count
        if any(has_use(place, *use, dom_count) for use in row_zero_uses(dom_count)):
            counts = counts + counted(one_more[pick], two_more[pick], lane_more[pick])
        one[pl.ds(d, rows, stride=devices), :] = counts[:rows]
        two[pl.ds(d, rows, stride=devices), :] = counts[rows:]

    square = (devices, devices)
    own = lax.broadcasted_iota(jnp.int32, square, 0) == lax.broadcasted_iota(jnp.int32, square, 1)

    def price(load, steep):
        value = jnp.exp2(load * 0.3785) + steep * jnp.maximum(load - (capacity - 1), 0.0)
        return jnp.where(own, 0.0, value)

    def settle(counts_ref, group, first, load, number):
        base = number * group
        counts = jnp.concatenate(
            [
                counts_ref[pl.ds(pl.multiple_of((base + i) * devices, devices), devices), :]
                for i in range(group)
            ],
            axis=1,
        )
        shape = (devices, group * LANES)
        handler = lax.broadcasted_iota(jnp.int32, shape, 0)
        column = lax.broadcasted_iota(jnp.int32, shape, 1)
        handler_f = handler.astype(jnp.float32)
        cost = dot_plain(price(load, 4.0 if first else 8.0), counts)
        was = None
        if not first:
            old = jnp.concatenate([table[pl.ds(base + i, 1), :] for i in range(group)], axis=1)
            was = handler_f == old
            cost = jnp.where(was, dot_plain(price(load - 1.0, 8.0), counts) - 1.0, cost)
        noise = 0.5 * mixed(handler, column % LANES, base + column // LANES)
        ranked = jnp.floor((jnp.minimum(cost, 4000.0) + noise) * 64.0) * devices + handler_f
        least = jnp.min(ranked, axis=0, keepdims=True)
        chosen = least - jnp.floor(least * (1.0 / devices)) * devices
        for i in range(group):
            table[pl.ds(base + i, 1), :] = chosen[:, i * LANES : (i + 1) * LANES]
        change = jnp.where(handler_f == chosen, 1.0, 0.0)
        if not first:
            change = change - jnp.where(was, 1.0, 0.0)
        return load + dot_rows(change, counts)

    load = jnp.zeros(square, jnp.float32)
    load = lax.fori_loop(0, rows // 2, lambda i, x: settle(one, 2, True, x, i), load)
    spot = lax.broadcasted_iota(jnp.int32, (rows, LANES), 0)
    lane = lax.broadcasted_iota(jnp.int32, (rows, LANES), 1)
    from_row = (spot + rows - (lane % SLOTS) % rows) % rows
    moved = jnp.zeros((rows, LANES), jnp.float32)
    for r in range(rows):
        moved = jnp.where(from_row == r, table[r : r + 1, :], moved)
    table[...] = moved
    load = lax.fori_loop(0, rows // 2, lambda i, x: settle(two, 2, False, x, i), load)
    load = lax.fori_loop(0, rows // 4, lambda i, x: settle(two, 4, False, x, i), load)

    ok = jnp.max(jnp.where(own, 0.0, load)) <= capacity
    owner = (from_row + rows * (lane // SLOTS)).astype(jnp.float32)
    final = jnp.where(ok, table[...], owner)
    assigned[...] = final
    me = device_number()

    def found(device):
        _, _, lane_row, _, row = key_parts(keys[pl.ds(device, 1), :], rows)
        return handlers_of(final, lane_row, row)

    place = lax.axis_index("dom")
    column = lax.broadcasted_iota(jnp.int32, (1, keys.shape[1]), 1)
    extra = jnp.full((1, keys.shape[1]), -1.0, jnp.float32)
    for t, (offset, period) in enumerate(row_zero_uses(dom_count)):
        there = has_use(place, offset, period, dom_count)
        moved = found(jnp.where(there, me + offset, me))
        moved = pltpu.roll(moved, 8 * t, 1) if t else moved
        extra = jnp.where((column >= 8 * t) & (column < 8 * t + 8) & there, moved, extra)
    size = jnp.where(ok, capacity, full)
    write_places(info, found(me), extra, ok.astype(jnp.int32), me, devices, size)


def table_kernel(*refs, devices, capacity, pieces, balanced, more):
    if balanced:
        keys, assigned, out, handlers = refs
        rows = devices * SLOTS // LANES
        table = assigned[...]
        _, _, lane_all, _, row_all = key_parts(keys[...], rows)
        for d in range(devices):
            handlers[d : d + 1, :] = handlers_of(table, lane_all[d : d + 1], row_all[d : d + 1])
        piece = keys[...]
    else:
        keys, out, handlers = refs
        handlers[...] = (keys[...] // SLOTS).astype(jnp.float32)
        piece = keys[...] % SLOTS
    me = device_number()
    size = keys.shape[1]
    mine = handlers[...] == me.astype(jnp.float32)
    sender = lax.broadcasted_iota(jnp.int32, (devices, size), 0)
    first = lax.broadcasted_iota(jnp.int32, (size, size), 0)
    second = lax.broadcasted_iota(jnp.int32, (size, size), 1)
    earlier = jnp.where(first <= second, 1.0, 0.0)
    column = lax.broadcasted_iota(jnp.int32, (devices, size), 1)

    def ranked(hits, ahead):
        count = jnp.where(hits, 1.0, 0.0)
        return dot_plain(count, earlier) + ahead, jnp.sum(count, axis=1, keepdims=True)

    rank, total = ranked(mine, 0.0)
    groups = [(mine, rank, piece)]
    if more:
        dom_count = lax.axis_size("dom")
        mine_more = extra_entries(handlers[...], dom_count, -1.0) == me.astype(jnp.float32)
        rank_more, _ = ranked(mine_more, total)
        groups.append((mine_more, rank_more, extra_entries(piece, dom_count, 0)))
    found = jnp.full((devices, size), pieces, jnp.int32)
    for r in range(capacity):
        at = jnp.zeros((devices, 1), jnp.int32)
        for hits, ranks, piece_of in groups:
            hit = hits & (sender != me) & (ranks == r + 1.0)
            at = at + jnp.sum(jnp.where(hit, piece_of - pieces, 0), axis=1, keepdims=True)
        found = jnp.where(column == r, pieces + at, found)
    out[0:devices, :] = found
    rows_kept = [
        jnp.sum(
            jnp.where(hits & (sender == me), piece_of - pieces, 0), axis=0, keepdims=True
        )
        + pieces
        for hits, _, piece_of in groups
    ]
    rows_kept += [jnp.full((1, size), pieces, jnp.int32)] * (8 - len(rows_kept))
    out[devices : devices + 8, :] = jnp.concatenate(rows_kept, axis=0)


def sum_kernel(table, arrived, own, out, own_out, pieces, *, devices, capacity, extras):
    blocks = own.shape[0]
    zero = jnp.zeros((8, LANES), jnp.float32)

    def over_senders(act):
        def one(d, carry):
            for i in range(capacity):
                act(table[d, i], d * capacity + i)
            return carry

        lax.fori_loop(0, devices, one, 0, unroll=2)

    def over_kept(act):
        def one(k, carry):
            for i in range(8):
                act(table[devices, 8 * k + i], 8 * k + i)
            return carry

        lax.fori_loop(0, blocks // 8, one, 0)

    def clear(piece, at):
        pieces[piece] = zero

    def add(piece, at):
        pieces[piece] = pieces[piece] + arrived[at]

    def add_own(piece, at):
        pieces[piece] = pieces[piece] + own[at]

    def give(piece, at):
        out[at] = pieces[piece]

    def give_own(piece, at):
        own_out[at] = pieces[piece]

    over_senders(clear)
    over_kept(clear)
    for i in range(extras):
        clear(table[devices + 1, i], i)
    over_senders(add)
    over_kept(add_own)
    for i in range(extras):
        piece = table[devices + 1, i]
        pieces[piece] = pieces[piece] - 0.5 * own[i % 8]
    over_senders(give)
    over_kept(give_own)


def unpack_kernel(info, back, own, out, stage):
    for b in range(16 * TILES // 8):
        stage[pl.ds(8 * b, 8), :] = jnp.where(info[2, b] != 0, own[b], back[info[1, b]])
    for j in range(TILES):
        for i in range(2):
            out[8 * i : 8 * i + 8, j * LANES : (j + 1) * LANES] = stage[
                pl.ds(j + i * 8 * TILES, 8, stride=TILES), :
            ]


def f32(*shape):
    return jax.ShapeDtypeStruct(shape, jnp.float32)


def body(concentration, diffusion, velocity, levels, grid_signs, owner_list, slot_list):
    dom_count = lax.axis_size("dom")
    devices = lax.axis_size("grid") * dom_count
    rows = concentration.shape[1]
    conc = concentration[0]
    dif = diffusion[0]
    blocks = owner_list.shape[1]
    capacity = 2 * blocks // devices

    own_keys = owner_list * SLOTS + slot_list
    keys = lax.all_to_all(
        jnp.broadcast_to(own_keys[:, None], (devices, 4, blocks)),
        ("grid", "dom"),
        split_axis=0,
        concat_axis=0,
        tiled=True,
    )[:, 0]

    up = [(i, i + 1) for i in range(dom_count - 1)]
    down = [(i + 1, i) for i in range(dom_count - 1)]
    low_rows = jnp.concatenate([conc[rows - 2 :], dif[rows - 1 :]], axis=0)
    high_rows = jnp.concatenate([conc[:3], dif[:2]], axis=0)
    low = lax.ppermute(low_rows.reshape(3, TILES, LANES), "dom", up)
    high = lax.ppermute(high_rows.reshape(5, TILES, LANES), "dom", down)

    blocks_in, lead = pl.pallas_call(
        rows_kernel,
        out_shape=(f32(rows * TILES, LANES), f32(TILES, LANES)),
        in_specs=[SM, SM, SM, VM, VM, VM, VM],
        out_specs=(VM, VM),
        scratch_shapes=[
            pltpu.VMEM((TILES + 2 * PAD, 24, LANES), jnp.float32),
            pltpu.VMEM((TILES + 2 * PAD, 24, LANES), jnp.float32),
            pltpu.VMEM((TILES, 24, LANES), jnp.float32),
            pltpu.VMEM((TILES + 1, 16, LANES), jnp.float32),
            pltpu.VMEM((TILES + 64, 16, LANES), jnp.float32),
        ],
        compiler_params=params(),
        name="rows",
        cost_estimate=SMALL,
    )(levels, velocity, grid_signs, conc, dif, low, high)

    keys, blocks_in = lax.optimization_barrier((keys, blocks_in))
    balanced = capacity >= 8 and devices * SLOTS % LANES == 0 and devices <= 64
    info_shape = jax.ShapeDtypeStruct((8, blocks), jnp.int32)
    if balanced:
        key_rows = devices * SLOTS // LANES
        assigned, info = pl.pallas_call(
            functools.partial(
                balance_kernel, devices=devices, capacity=capacity // 2, full=capacity
            ),
            out_shape=(f32(key_rows, LANES), info_shape),
            in_specs=[VM],
            out_specs=(VM, VM),
            scratch_shapes=[
                pltpu.VMEM((key_rows * devices, LANES), jnp.float32),
                pltpu.VMEM((key_rows * devices, LANES), jnp.float32),
                pltpu.VMEM((key_rows, LANES), jnp.float32),
            ],
            compiler_params=params(),
            name="balance",
            cost_estimate=SMALL,
        )(keys)
    else:
        info = pl.pallas_call(
            functools.partial(owner_places_kernel, devices=devices, capacity=capacity),
            out_shape=info_shape,
            in_specs=[VM],
            out_specs=VM,
            compiler_params=params(),
            name="places",
            cost_estimate=SMALL,
        )(keys)

    def fixed():
        coarse = None
        for offset, period in row_zero_uses(dom_count):
            pairs = [
                (d, d + offset) for d in range(dom_count) if has_use(d, offset, period, dom_count)
            ]
            part = lax.ppermute(lead, "dom", pairs)
            coarse = part if coarse is None else coarse + part
        return pl.pallas_call(
            fix_kernel,
            out_shape=f32(rows * TILES, LANES),
            in_specs=[SM, SM, VM, VM],
            out_specs=VM,
            scratch_shapes=[
                pltpu.VMEM((TILES + 1, 8, LANES), jnp.float32),
                pltpu.VMEM((TILES + 64, 8, LANES), jnp.float32),
                pltpu.VMEM((8 * TILES, LANES), jnp.float32),
            ],
            compiler_params=params(),
            name="fix_row",
        )(levels, grid_signs, coarse, blocks_in)

    def route(own, slots, balanced, extras, tables):
        pieces = devices * SLOTS if balanced else SLOTS

        def exchange(x):
            return lax.all_to_all(
                x.reshape(devices, slots * 8, LANES),
                ("grid", "dom"),
                split_axis=0,
                concat_axis=0,
                tiled=True,
            ).reshape(devices * slots, 8, LANES)

        own = own.reshape(blocks, 8, LANES)
        outgoing = pl.pallas_call(
            functools.partial(scatter_kernel, extras=extras),
            out_shape=f32(devices * slots, 8, LANES),
            in_specs=[SM, VM],
            out_specs=VM,
            compiler_params=params(),
            name="scatter",
        )(info, own)
        arrived = exchange(outgoing)
        table = pl.pallas_call(
            functools.partial(
                table_kernel,
                devices=devices,
                capacity=slots,
                pieces=pieces,
                balanced=balanced,
                more=extras > 0,
            ),
            out_shape=jax.ShapeDtypeStruct((devices + 8, blocks), jnp.int32),
            in_specs=[VM] * len(tables),
            out_specs=VM,
            scratch_shapes=[pltpu.VMEM((devices, blocks), jnp.float32)],
            compiler_params=params(),
            name="piece_table",
        )(*tables)
        returned, own_back = pl.pallas_call(
            functools.partial(sum_kernel, devices=devices, capacity=slots, extras=extras),
            out_shape=(f32(devices * slots, 8, LANES), f32(blocks, 8, LANES)),
            in_specs=[SM, VM, VM],
            out_specs=(VM, VM),
            scratch_shapes=[pltpu.VMEM((pieces + 8, 8, LANES), jnp.float32)],
            compiler_params=params(),
            name="sum_pieces",
        )(table, arrived, own)
        back = exchange(returned)
        return pl.pallas_call(
            unpack_kernel,
            out_shape=f32(rows, TILES * LANES),
            in_specs=[SM, VM, VM],
            out_specs=VM,
            scratch_shapes=[pltpu.VMEM((16 * TILES, LANES), jnp.float32)],
            compiler_params=params(),
            name="unpack",
        )(info, back, own_back)

    if balanced:
        combined = lax.cond(
            info[3, 0] != 0,
            lambda: route(
                blocks_in, capacity // 2, True, 8 * len(row_zero_uses(dom_count)), (keys, assigned)
            ),
            lambda: route(fixed(), capacity, True, 0, (keys, assigned)),
        )
    else:
        combined = route(fixed(), capacity, False, 0, (keys,))
    return combined[None]


def solution(mesh):
    return jax.shard_map(
        body,
        mesh=mesh,
        in_specs=(
            P("grid", "dom", None),
            P("grid", "dom", None),
            P(),
            P("grid", None),
            P("grid"),
            P(("grid", "dom"), None),
            P(("grid", "dom"), None),
        ),
        out_specs=P("grid", "dom", None),
        check_vma=False,
    )
```

```python
import functools

import jax
import jax.numpy as jnp
from jax import lax
from jax.experimental import pallas as pl
from jax.experimental.pallas import tpu as pltpu
from jax.sharding import PartitionSpec as P

LR = 13
BLK = 1024
SLOTS = 64
LANES = 128
TILES = 2**LR // LANES
PAD = 9
VMEM_LIMIT = 48 * 1024 * 1024


def params():
    return pltpu.CompilerParams(vmem_limit_bytes=VMEM_LIMIT)


SMALL = pl.CostEstimate(flops=0, transcendentals=0, bytes_accessed=0)
VM = pl.BlockSpec(memory_space=pltpu.VMEM)
SM = pl.BlockSpec(memory_space=pltpu.SMEM)


def grid_step(first_bits, second_bits, weights, valid, src, dst, dif, lane_two, lane_three):
    lane = lax.broadcasted_iota(jnp.int32, (1, LANES), 1)
    first_mask = (1 << first_bits) - 1
    stride_two = 1 << first_bits
    stride_three = 1 << (first_bits + second_bits)
    two_mask = stride_three - 1
    up_one = (lane & first_mask) != first_mask
    down_one = (lane & first_mask) != 0

    def rolled(tile, stride):
        return pltpu.roll(tile, LANES - stride, 1), pltpu.roll(tile, stride, 1)

    def neighbours(j, x, nxt, stride, in_lanes, carry):
        if not in_lanes:
            step = stride // LANES
            return src[PAD + j + step], src[PAD + j - step], carry
        up_here, down_here, down_last = carry
        up_next, down_next = rolled(nxt, stride)
        ahead = jnp.where(lane < LANES - stride, up_here, up_next)
        before = jnp.where(lane >= stride, down_here, down_last)
        return ahead, before, (up_next, down_next, down_here)

    def one_tile(j, carry):
        x, carry_two, carry_three = carry
        nxt = src[PAD + j + 1]
        ahead = jnp.where(up_one, pltpu.roll(x, LANES - 1, 1), 0.0)
        before = jnp.where(down_one, pltpu.roll(x, 1, 1), 0.0)
        total = ahead + before
        drift = weights[0] * (ahead - before)
        ahead, before, carry_two = neighbours(j, x, nxt, stride_two, lane_two, carry_two)
        node = (j * LANES + lane) & two_mask
        ahead = jnp.where(node < stride_three - stride_two, ahead, 0.0)
        before = jnp.where(node >= stride_two, before, 0.0)
        total = total + (ahead + before)
        drift = drift + weights[1] * (ahead - before)
        ahead, before, carry_three = neighbours(j, x, nxt, stride_three, lane_three, carry_three)
        total = total + (ahead + before)
        drift = drift + weights[2] * (ahead - before)
        ahead = pltpu.roll(x, 23, 0)
        before = pltpu.roll(x, 1, 0)
        total = total + (ahead + before)
        drift = drift + weights[3] * (ahead - before)
        new = x + dif[j] * (total - 8.0 * x) - drift
        dst[PAD + j] = jnp.where(valid, new, 0.0)
        return nxt, carry_two, carry_three

    def start(stride, in_lanes):
        if not in_lanes:
            return ()
        up_here, down_here = rolled(src[PAD], stride)
        return up_here, down_here, jnp.zeros((24, LANES), jnp.float32)

    def several(k, carry):
        for i in range(4):
            carry = one_tile(4 * k + i, carry)
        return carry

    lax.fori_loop(
        0,
        TILES // 4,
        several,
        (src[PAD], start(stride_two, lane_two), start(stride_three, lane_three)),
    )


def bit_ends(levels, q):
    one = levels[0, 0]
    two = one + levels[0, 1]
    begin = jnp.where(q < one, 0, jnp.where(q < two, one, two))
    end = jnp.where(q < one, one, jnp.where(q < two, two, LR))
    return begin, end


def lane_matrix(levels):
    rows = lax.broadcasted_iota(jnp.int32, (LANES, LANES), 0)
    lane = lax.broadcasted_iota(jnp.int32, (LANES, LANES), 1)
    own = (rows == lane).astype(jnp.float32)
    nxt = jnp.zeros((LANES, LANES), jnp.float32)
    for q in range(7):
        begin, end = bit_ends(levels, q)
        below = (1 << q) - (1 << begin)
        above = (1 << jnp.minimum(end, 7)) - (2 << q)
        here = ((lane & below) == 0) & ((lane & (1 << q)) != 0)
        full = (lane & above) == above
        ahead = pltpu.roll(own, LANES - (1 << q), 1)
        before = pltpu.roll(own, 1 << q, 1)
        half = jnp.where(here, -0.5, 0.0)
        nxt = nxt + jnp.where(full & (end > 7), half * ahead, 0.0)
        own = own + half * (before + jnp.where(full, 0.0, ahead))
    return jnp.concatenate([own, nxt], axis=0)


def surplus_rows(levels, sign, x, y, matrix, stage):
    rows = x.shape[1]
    x[TILES] = jnp.zeros((rows, LANES), jnp.float32)
    y[pl.ds(0, 32)] = jnp.zeros((32, rows, LANES), jnp.float32)
    y[pl.ds(32 + TILES, 32)] = jnp.zeros((32, rows, LANES), jnp.float32)

    _, end_six = bit_ends(levels, 6)
    mask_six = (1 << (jnp.maximum(end_six, 7) - 7)) - 1
    chunk = 16
    for j0 in range(0, TILES, chunk):
        own = x[pl.ds(j0, chunk)].reshape(chunk * rows, LANES)
        nxt = jnp.concatenate(
            [
                jnp.where(((j0 + i) & mask_six) == mask_six, 0.0, x[j0 + i + 1])
                for i in range(chunk)
            ],
            axis=0,
        )
        res = jnp.dot(
            jnp.concatenate([own, nxt], axis=1),
            matrix,
            precision=lax.Precision.HIGHEST,
            preferred_element_type=jnp.float32,
        )
        y[pl.ds(32 + j0, chunk)] = res.reshape(chunk, rows, LANES)

    lane = lax.broadcasted_iota(jnp.int32, (1, LANES), 1)
    for q in range(7, LR):
        t = 1 << (q - 7)
        begin, end = bit_ends(levels, q)
        low_lane = 128 - (1 << jnp.minimum(begin, 7))
        half = jnp.where((lane & low_lane) == 0, -0.5, 0.0)
        below = t - (1 << (jnp.maximum(begin, 7) - 7))
        above = (1 << (end - 7)) - 2 * t
        for j in range(TILES):
            if j & t:
                mine = jnp.where((j & below) == 0, half, 0.0)
                ahead_on = jnp.where((j & above) == above, 0.0, 1.0)
                y[32 + j] = y[32 + j] + mine * (y[32 + j - t] + ahead_on * y[32 + j + t])

    factor = sign[0].astype(jnp.float32)
    for j in range(TILES):
        tile = factor * y[32 + j]
        for i in range(0, rows, 8):
            stage[pl.ds(j + i * TILES, 8, stride=TILES), :] = tile[i : i + 8]


def rows_kernel(
    levels,
    velocity,
    sign,
    info_in,
    conc,
    dif_in,
    low,
    high,
    out,
    lead,
    outgoing,
    u_a,
    u_b,
    dif,
    x,
    y,
    info,
    info_sem,
    *,
    extras,
):
    places = pltpu.make_async_copy(info_in, info, info_sem)
    places.start()
    place = lax.axis_index("dom")
    count = lax.axis_size("dom")
    zeros = jnp.zeros((PAD, 24, LANES), jnp.float32)
    for ref in (u_a, u_b):
        ref[pl.ds(0, PAD)] = zeros
        ref[pl.ds(PAD + TILES, PAD)] = zeros
    tail = jnp.zeros((8, LANES), jnp.float32)
    for j in range(TILES):
        cols = pl.ds(j * LANES, LANES)
        u_a[PAD + j, 0:16] = conc[:, cols]
        u_a[PAD + j, 16:24] = tail
        dif[j, 0:16] = 0.1 * dif_in[:, cols]
        dif[j, 16:24] = tail
    for i in range(3):
        u_a[PAD : PAD + TILES, 16 + i] = high[i]
    for i in range(2):
        u_a[PAD : PAD + TILES, 22 + i] = low[i]
        dif[:, 16 + i] = 0.1 * high[3 + i]
    dif[:, 23] = 0.1 * low[2]
    row = lax.broadcasted_iota(jnp.int32, (24, LANES), 0)
    valid = (row < 16) | ((row < 20) & (place < count - 1)) | ((row >= 20) & (place > 0))
    weights = [0.1 * velocity[d] for d in range(4)]
    first_bits = levels[0, 0]
    second_bits = levels[0, 1]

    def both(lane_two, lane_three):
        def run():
            for src, dst in ((u_a, u_b), (u_b, u_a)):
                grid_step(
                    first_bits, second_bits, weights, valid, src, dst, dif, lane_two, lane_three
                )

        return run

    small_two = first_bits < 7
    small_three = first_bits + second_bits < 7
    pl.when(small_three)(both(True, True))
    pl.when(small_two & jnp.logical_not(small_three))(both(True, False))
    pl.when(jnp.logical_not(small_two))(both(False, False))
    lead[...] = u_a[PAD : PAD + TILES, 0]
    for j in range(TILES):
        tile = u_a[PAD + j]
        for p in range(4):
            s = 1 << p
            around = pltpu.roll(tile, 24 - s, 0) + pltpu.roll(tile, s, 0)
            hit = ((row & (2 * s - 1)) == s) & (row < 16)
            tile = tile - 0.5 * jnp.where(hit, around, 0.0)
        x[j] = tile[0:16]
    next_lead = u_a[PAD : PAD + TILES, 16]
    x[0:TILES, 0] = x[0:TILES, 0] - jnp.where((place & 1) == 1, 0.5, 0.0) * next_lead
    surplus_rows(levels, sign, x, y, lane_matrix(levels), out)
    places.wait()
    send_blocks(info, lambda b: out[8 * b : 8 * b + 8, :], outgoing, extras)


def send_blocks(info, block, outgoing, extras):
    use = info[3, 0]
    for b in range(info.shape[1]):
        outgoing[info[0, b] * use] = block(b)
    for i in range(extras):
        outgoing[info[4, i] * use] = -0.5 * block(i % 8)


def fix_kernel(levels, sign, coarse, blocks, out, x, y, stage):
    x[...] = jnp.zeros_like(x)
    x[0:TILES, 0] = coarse[...]
    surplus_rows(levels, sign, x, y, lane_matrix(levels), stage)
    out[...] = blocks[...]
    out[0:TILES, :] = blocks[0:TILES, :] - 0.5 * stage[0:TILES, :]


def scatter_kernel(info, blocks, out):
    for b in range(blocks.shape[0]):
        out[info[0, b]] = blocks[b]


def row_zero_uses(dom_count):
    uses = []
    distance = 1
    while distance < dom_count:
        uses.append((distance, 2 * distance))
        if distance > 1 and dom_count > 2 * distance:
            uses.append((-distance, 2 * distance))
        distance *= 2
    return uses


def has_use(place, offset, period, dom_count):
    return (place % period == 0) & (place + offset >= 0) & (place + offset < dom_count)


def extra_entries(values, dom_count, fill):
    devices, size = values.shape
    place = lax.broadcasted_iota(jnp.int32, (devices, size), 0) % dom_count
    lane = lax.broadcasted_iota(jnp.int32, (devices, size), 1)
    res = jnp.full((devices, size), fill, values.dtype)
    for t, (offset, period) in enumerate(row_zero_uses(dom_count)):
        cut = offset % devices
        moved = jnp.concatenate([values[cut:], values[:cut]], axis=0)
        moved = pltpu.roll(moved, 8 * t, 1) if t else moved
        hit = (lane >= 8 * t) & (lane < 8 * t + 8) & has_use(place, offset, period, dom_count)
        res = jnp.where(hit, moved, res)
    return res


def key_parts(keys, rows):
    owner = keys // SLOTS
    slot = keys % SLOTS
    row = owner % rows
    lane = slot + SLOTS * (owner // rows)
    return owner, slot, lane, row, (row + slot) % rows


def hot(index, count):
    which = lax.broadcasted_iota(jnp.int32, (count, index.shape[1]), 0)
    return jnp.where(which == index, 1.0, 0.0)


def dot_rows(left, right):
    return lax.dot_general(
        left.astype(jnp.bfloat16),
        right.astype(jnp.bfloat16),
        (((1,), (1,)), ((), ())),
        preferred_element_type=jnp.float32,
    )


def dot_plain(left, right):
    return jnp.dot(
        left.astype(jnp.bfloat16), right.astype(jnp.bfloat16), preferred_element_type=jnp.float32
    )


def mixed(handler, lane, row):
    x = (handler * 40503 + lane * 30011 + row * 52711) & 0xFFFF
    x = ((x ^ (x >> 7)) * 9973) & 0xFFFF
    x = ((x ^ (x >> 5)) * 12347) & 0xFFFF
    return (x >> 8).astype(jnp.float32) * (1.0 / 256.0)


def handlers_of(assigned, lane, row):
    return jnp.sum(
        hot(row, assigned.shape[0]) * dot_plain(assigned, hot(lane, LANES)), axis=0, keepdims=True
    )


def device_number():
    return lax.axis_index("grid") * lax.axis_size("dom") + lax.axis_index("dom")


def write_places(info, handler, extra, ok, me, devices, capacity):
    size = handler.shape[1]
    first = lax.broadcasted_iota(jnp.int32, (size, size), 0)
    second = lax.broadcasted_iota(jnp.int32, (size, size), 1)
    earlier = jnp.where(first < second, 1.0, 0.0)

    def placed(which, ahead):
        taken = hot(which.astype(jnp.int32), devices)
        rank = jnp.sum(taken * (dot_plain(taken, earlier) + ahead), axis=0, keepdims=True)
        place = which.astype(jnp.int32) * capacity + rank.astype(jnp.int32)
        stays = (which == me.astype(jnp.float32)) | (which < 0.0)
        return jnp.where(stays, me * capacity, place), stays, taken

    send, stays, taken = placed(handler, 0.0)
    send_extra, _, _ = placed(extra, jnp.sum(taken, axis=1, keepdims=True))
    kept = jnp.where(stays, 1, 0)
    flag = jnp.broadcast_to(ok, kept.shape).astype(jnp.int32)
    info[...] = jnp.concatenate([send, send, kept, flag, send_extra, flag, flag, flag], axis=0)


def owner_places_kernel(keys, info, *, devices, capacity):
    me = device_number()
    owner = (keys[pl.ds(me, 1), :] // SLOTS).astype(jnp.float32)
    none = jnp.full(owner.shape, -1.0, jnp.float32)
    write_places(info, owner, none, jnp.int32(0), me, devices, capacity)


def balance_kernel(keys, assigned, info, good, one, two, table, *, devices, capacity, full):
    rows = devices * SLOTS // LANES
    keys_all = keys[...]
    _, _, lane_all, row_one, row_two = key_parts(keys_all, rows)
    dom_count = lax.axis_size("dom")
    lane_more, one_more, two_more = [
        extra_entries(v, dom_count, -1) for v in (lane_all, row_one, row_two)
    ]

    def counted(one_row, two_row, lane_row):
        both = jnp.concatenate([hot(one_row, rows), hot(two_row, rows)], axis=0)
        return dot_rows(both, hot(lane_row, LANES))

    for d in range(devices):
        pick = slice(d, d + 1)
        counts = counted(row_one[pick], row_two[pick], lane_all[pick])
        place = d % dom_count
        if any(has_use(place, *use, dom_count) for use in row_zero_uses(dom_count)):
            counts = counts + counted(one_more[pick], two_more[pick], lane_more[pick])
        one[pl.ds(d, rows, stride=devices), :] = counts[:rows]
        two[pl.ds(d, rows, stride=devices), :] = counts[rows:]

    square = (devices, devices)
    own = lax.broadcasted_iota(jnp.int32, square, 0) == lax.broadcasted_iota(jnp.int32, square, 1)

    def price(load, steep):
        value = jnp.exp2(load * 0.3785) + steep * jnp.maximum(load - (capacity - 1), 0.0)
        return jnp.where(own, 0.0, value)

    def settle(counts_ref, group, first, load, number):
        base = number * group
        counts = jnp.concatenate(
            [
                counts_ref[pl.ds(pl.multiple_of((base + i) * devices, devices), devices), :]
                for i in range(group)
            ],
            axis=1,
        )
        shape = (devices, group * LANES)
        handler = lax.broadcasted_iota(jnp.int32, shape, 0)
        column = lax.broadcasted_iota(jnp.int32, shape, 1)
        handler_f = handler.astype(jnp.float32)
        cost = dot_plain(price(load, 4.0 if first else 16.0), counts)
        was = None
        if not first:
            old = jnp.concatenate([table[pl.ds(base + i, 1), :] for i in range(group)], axis=1)
            was = handler_f == old
            cost = jnp.where(was, dot_plain(price(load - 1.0, 16.0), counts) - 5.0, cost)
        noise = 0.5 * mixed(handler, column % LANES, base + column // LANES)
        ranked = jnp.floor((jnp.minimum(cost, 4000.0) + noise) * 64.0) * devices + handler_f
        least = jnp.min(ranked, axis=0, keepdims=True)
        chosen = least - jnp.floor(least * (1.0 / devices)) * devices
        for i in range(group):
            table[pl.ds(base + i, 1), :] = chosen[:, i * LANES : (i + 1) * LANES]
        change = jnp.where(handler_f == chosen, 1.0, 0.0)
        if not first:
            change = change - jnp.where(was, 1.0, 0.0)
        return load + dot_rows(change, counts)

    def sweep(counts_ref, group, first, load):
        return lax.fori_loop(
            0, rows // group, lambda i, x: settle(counts_ref, group, first, x, i), load
        )

    def worst(load):
        return jnp.max(jnp.where(own, 0.0, load))

    load = sweep(one, 4, True, jnp.zeros(square, jnp.float32))
    spot = lax.broadcasted_iota(jnp.int32, (rows, LANES), 0)
    lane = lax.broadcasted_iota(jnp.int32, (rows, LANES), 1)
    from_row = (spot + rows - (lane % SLOTS) % rows) % rows
    moved = jnp.zeros((rows, LANES), jnp.float32)
    for r in range(rows):
        moved = jnp.where(from_row == r, table[r : r + 1, :], moved)
    table[...] = moved
    load = sweep(two, 4, False, load)

    def again(state):
        count, _, load = state
        load = lax.cond(
            count == 0,
            lambda x: sweep(two, 4, False, x),
            lambda x: sweep(two, 2, False, x),
            load,
        )
        return count + 1, worst(load), load

    _, most, _ = lax.while_loop(
        lambda state: (state[0] < 6) & (state[1] > capacity), again, (0, worst(load), load)
    )
    ok = most <= capacity
    good[0] = ok.astype(jnp.int32)
    owner = (from_row + rows * (lane // SLOTS)).astype(jnp.float32)
    final = jnp.where(ok, table[...], owner)
    assigned[...] = final
    me = device_number()

    def found(device):
        _, _, lane_row, _, row = key_parts(keys[pl.ds(device, 1), :], rows)
        return handlers_of(final, lane_row, row)

    place = lax.axis_index("dom")
    column = lax.broadcasted_iota(jnp.int32, (1, keys.shape[1]), 1)
    extra = jnp.full((1, keys.shape[1]), -1.0, jnp.float32)
    for t, (offset, period) in enumerate(row_zero_uses(dom_count)):
        there = has_use(place, offset, period, dom_count)
        moved = found(jnp.where(there, me + offset, me))
        moved = pltpu.roll(moved, 8 * t, 1) if t else moved
        extra = jnp.where((column >= 8 * t) & (column < 8 * t + 8) & there, moved, extra)
    size = jnp.where(ok, capacity, full)
    write_places(info, found(me), extra, ok.astype(jnp.int32), me, devices, size)


def table_kernel(*refs, devices, capacity, pieces, balanced, more):
    if balanced:
        keys, assigned, out, handlers = refs
        rows = devices * SLOTS // LANES
        table = assigned[...]
        _, _, lane_all, _, row_all = key_parts(keys[...], rows)
        for d in range(devices):
            handlers[d : d + 1, :] = handlers_of(table, lane_all[d : d + 1], row_all[d : d + 1])
        piece = keys[...]
    else:
        keys, out, handlers = refs
        handlers[...] = (keys[...] // SLOTS).astype(jnp.float32)
        piece = keys[...] % SLOTS
    me = device_number()
    size = keys.shape[1]
    mine = handlers[...] == me.astype(jnp.float32)
    sender = lax.broadcasted_iota(jnp.int32, (devices, size), 0)
    first = lax.broadcasted_iota(jnp.int32, (size, size), 0)
    second = lax.broadcasted_iota(jnp.int32, (size, size), 1)
    earlier = jnp.where(first <= second, 1.0, 0.0)
    column = lax.broadcasted_iota(jnp.int32, (devices, size), 1)

    def ranked(hits, ahead):
        count = jnp.where(hits, 1.0, 0.0)
        return dot_plain(count, earlier) + ahead, jnp.sum(count, axis=1, keepdims=True)

    rank, total = ranked(mine, 0.0)
    groups = [(mine, rank, piece)]
    if more:
        dom_count = lax.axis_size("dom")
        mine_more = extra_entries(handlers[...], dom_count, -1.0) == me.astype(jnp.float32)
        rank_more, _ = ranked(mine_more, total)
        groups.append((mine_more, rank_more, extra_entries(piece, dom_count, 0)))
    found = jnp.full((devices, size), pieces, jnp.int32)
    for r in range(capacity):
        at = jnp.zeros((devices, 1), jnp.int32)
        for hits, ranks, piece_of in groups:
            hit = hits & (sender != me) & (ranks == r + 1.0)
            at = at + jnp.sum(jnp.where(hit, piece_of - pieces, 0), axis=1, keepdims=True)
        found = jnp.where(column == r, pieces + at, found)
    out[0:devices, :] = found
    rows_kept = [
        jnp.sum(
            jnp.where(hits & (sender == me), piece_of - pieces, 0), axis=0, keepdims=True
        )
        + pieces
        for hits, _, piece_of in groups
    ]
    rows_kept += [jnp.full((1, size), pieces, jnp.int32)] * (8 - len(rows_kept))
    out[devices : devices + 8, :] = jnp.concatenate(rows_kept, axis=0)


def sum_kernel(table, arrived, own, out, own_out, pieces, *, devices, capacity, extras):
    blocks = own.shape[0]
    zero = jnp.zeros((8, LANES), jnp.float32)

    def over_senders(act):
        def one(d, carry):
            for i in range(capacity):
                act(table[d, i], d * capacity + i)
            return carry

        lax.fori_loop(0, devices, one, 0, unroll=2)

    def over_kept(act):
        def one(k, carry):
            for i in range(8):
                act(table[devices, 8 * k + i], 8 * k + i)
            return carry

        lax.fori_loop(0, blocks // 8, one, 0)

    def clear(piece, at):
        pieces[piece] = zero

    def add(piece, at):
        pieces[piece] = pieces[piece] + arrived[at]

    def add_own(piece, at):
        pieces[piece] = pieces[piece] + own[at]

    def give(piece, at):
        out[at] = pieces[piece]

    def give_own(piece, at):
        own_out[at] = pieces[piece]

    over_senders(clear)
    over_kept(clear)
    for i in range(extras):
        clear(table[devices + 1, i], i)
    over_senders(add)
    over_kept(add_own)
    for i in range(extras):
        piece = table[devices + 1, i]
        pieces[piece] = pieces[piece] - 0.5 * own[i % 8]
    over_senders(give)
    over_kept(give_own)


def unpack_kernel(info, back, own, out, stage):
    for b in range(16 * TILES // 8):
        stage[pl.ds(8 * b, 8), :] = jnp.where(info[2, b] != 0, own[b], back[info[1, b]])
    for j in range(TILES):
        for i in range(2):
            out[8 * i : 8 * i + 8, j * LANES : (j + 1) * LANES] = stage[
                pl.ds(j + i * 8 * TILES, 8, stride=TILES), :
            ]


def f32(*shape):
    return jax.ShapeDtypeStruct(shape, jnp.float32)


def body(concentration, diffusion, velocity, levels, grid_signs, owner_list, slot_list):
    dom_count = lax.axis_size("dom")
    devices = lax.axis_size("grid") * dom_count
    rows = concentration.shape[1]
    conc = concentration[0]
    dif = diffusion[0]
    blocks = owner_list.shape[1]
    capacity = 2 * blocks // devices

    own_keys = owner_list * SLOTS + slot_list
    keys = lax.all_to_all(
        jnp.broadcast_to(own_keys[:, None], (devices, 4, blocks)),
        ("grid", "dom"),
        split_axis=0,
        concat_axis=0,
        tiled=True,
    )[:, 0]

    up = [(i, i + 1) for i in range(dom_count - 1)]
    down = [(i + 1, i) for i in range(dom_count - 1)]
    low_rows = jnp.concatenate([conc[rows - 2 :], dif[rows - 1 :]], axis=0)
    high_rows = jnp.concatenate([conc[:3], dif[:2]], axis=0)
    low = lax.ppermute(low_rows.reshape(3, TILES, LANES), "dom", up)
    high = lax.ppermute(high_rows.reshape(5, TILES, LANES), "dom", down)

    balanced = capacity >= 8 and devices * SLOTS % LANES == 0 and devices <= 64
    info_shape = jax.ShapeDtypeStruct((8, blocks), jnp.int32)
    if balanced:
        key_rows = devices * SLOTS // LANES
        assigned, info, good = pl.pallas_call(
            functools.partial(
                balance_kernel, devices=devices, capacity=capacity // 2, full=capacity
            ),
            out_shape=(f32(key_rows, LANES), info_shape, jax.ShapeDtypeStruct((1,), jnp.int32)),
            in_specs=[VM],
            out_specs=(VM, VM, SM),
            scratch_shapes=[
                pltpu.VMEM((key_rows * devices, LANES), jnp.float32),
                pltpu.VMEM((key_rows * devices, LANES), jnp.float32),
                pltpu.VMEM((key_rows, LANES), jnp.float32),
            ],
            compiler_params=params(),
            name="balance",
            cost_estimate=SMALL,
        )(keys)
    else:
        info = pl.pallas_call(
            functools.partial(owner_places_kernel, devices=devices, capacity=capacity),
            out_shape=info_shape,
            in_specs=[VM],
            out_specs=VM,
            compiler_params=params(),
            name="places",
            cost_estimate=SMALL,
        )(keys)

    low, high, info = lax.optimization_barrier((low, high, info))
    slots = capacity // 2 if balanced else capacity
    extras = 8 * len(row_zero_uses(dom_count)) if balanced else 0
    blocks_in, lead, outgoing = pl.pallas_call(
        functools.partial(rows_kernel, extras=extras),
        out_shape=(
            f32(rows * TILES, LANES),
            f32(TILES, LANES),
            f32(devices * slots, 8, LANES),
        ),
        in_specs=[SM, SM, SM, VM, VM, VM, VM, VM],
        out_specs=(VM, VM, VM),
        scratch_shapes=[
            pltpu.VMEM((TILES + 2 * PAD, 24, LANES), jnp.float32),
            pltpu.VMEM((TILES + 2 * PAD, 24, LANES), jnp.float32),
            pltpu.VMEM((TILES, 24, LANES), jnp.float32),
            pltpu.VMEM((TILES + 1, 16, LANES), jnp.float32),
            pltpu.VMEM((TILES + 64, 16, LANES), jnp.float32),
            pltpu.SMEM((8, blocks), jnp.int32),
            pltpu.SemaphoreType.DMA,
        ],
        compiler_params=params(),
        name="rows",
        cost_estimate=SMALL,
    )(levels, velocity, grid_signs, info, conc, dif, low, high)

    def fixed():
        coarse = None
        for offset, period in row_zero_uses(dom_count):
            pairs = [
                (d, d + offset) for d in range(dom_count) if has_use(d, offset, period, dom_count)
            ]
            part = lax.ppermute(lead, "dom", pairs)
            coarse = part if coarse is None else coarse + part
        return pl.pallas_call(
            fix_kernel,
            out_shape=f32(rows * TILES, LANES),
            in_specs=[SM, SM, VM, VM],
            out_specs=VM,
            scratch_shapes=[
                pltpu.VMEM((TILES + 1, 8, LANES), jnp.float32),
                pltpu.VMEM((TILES + 64, 8, LANES), jnp.float32),
                pltpu.VMEM((8 * TILES, LANES), jnp.float32),
            ],
            compiler_params=params(),
            name="fix_row",
        )(levels, grid_signs, coarse, blocks_in)

    def route(own, outgoing, slots, extras, tables):
        pieces = devices * SLOTS if balanced else SLOTS

        def exchange(x):
            return lax.all_to_all(
                x.reshape(devices, slots * 8, LANES),
                ("grid", "dom"),
                split_axis=0,
                concat_axis=0,
                tiled=True,
            ).reshape(devices * slots, 8, LANES)

        own = own.reshape(blocks, 8, LANES)
        if outgoing is None:
            outgoing = pl.pallas_call(
                scatter_kernel,
                out_shape=f32(devices * slots, 8, LANES),
                in_specs=[SM, VM],
                out_specs=VM,
                compiler_params=params(),
                name="scatter",
            )(info, own)
        arrived = exchange(outgoing)
        table = pl.pallas_call(
            functools.partial(
                table_kernel,
                devices=devices,
                capacity=slots,
                pieces=pieces,
                balanced=balanced,
                more=extras > 0,
            ),
            out_shape=jax.ShapeDtypeStruct((devices + 8, blocks), jnp.int32),
            in_specs=[VM] * len(tables),
            out_specs=VM,
            scratch_shapes=[pltpu.VMEM((devices, blocks), jnp.float32)],
            compiler_params=params(),
            name="piece_table",
        )(*tables)
        returned, own_back = pl.pallas_call(
            functools.partial(sum_kernel, devices=devices, capacity=slots, extras=extras),
            out_shape=(f32(devices * slots, 8, LANES), f32(blocks, 8, LANES)),
            in_specs=[SM, VM, VM],
            out_specs=(VM, VM),
            scratch_shapes=[pltpu.VMEM((pieces + 8, 8, LANES), jnp.float32)],
            compiler_params=params(),
            name="sum_pieces",
        )(table, arrived, own)
        back = exchange(returned)
        return pl.pallas_call(
            unpack_kernel,
            out_shape=f32(rows, TILES * LANES),
            in_specs=[SM, VM, VM],
            out_specs=VM,
            scratch_shapes=[pltpu.VMEM((16 * TILES, LANES), jnp.float32)],
            compiler_params=params(),
            name="unpack",
        )(info, back, own_back)

    if balanced:
        combined = lax.cond(
            good[0] != 0,
            lambda: route(blocks_in, outgoing, slots, extras, (keys, assigned)),
            lambda: route(fixed(), None, capacity, 0, (keys, assigned)),
        )
    else:
        combined = route(fixed(), None, capacity, 0, (keys,))
    return combined[None]


def solution(mesh):
    return jax.shard_map(
        body,
        mesh=mesh,
        in_specs=(
            P("grid", "dom", None),
            P("grid", "dom", None),
            P(),
            P("grid", None),
            P("grid"),
            P(("grid", "dom"), None),
            P(("grid", "dom"), None),
        ),
        out_specs=P("grid", "dom", None),
        check_vma=False,
    )
```

```python
import functools

import jax
import jax.numpy as jnp
from jax import lax
from jax.experimental import pallas as pl
from jax.experimental.pallas import tpu as pltpu
from jax.sharding import PartitionSpec as P

LR = 13
BLK = 1024
SLOTS = 64
LANES = 128
TILES = 2**LR // LANES
PAD = 9
COPIES = 4
MOST_KEYS = 256
VMEM_LIMIT = 48 * 1024 * 1024


def params():
    return pltpu.CompilerParams(vmem_limit_bytes=VMEM_LIMIT)


SMALL = pl.CostEstimate(flops=0, transcendentals=0, bytes_accessed=0)
VM = pl.BlockSpec(memory_space=pltpu.VMEM)
HBM = pl.BlockSpec(memory_space=pltpu.HBM)
SM = pl.BlockSpec(memory_space=pltpu.SMEM)


def grid_step(first_bits, second_bits, weights, valid, src, dst, dif, lane_two, lane_three):
    lane = lax.broadcasted_iota(jnp.int32, (1, LANES), 1)
    first_mask = (1 << first_bits) - 1
    stride_two = 1 << first_bits
    stride_three = 1 << (first_bits + second_bits)
    two_mask = stride_three - 1
    up_one = (lane & first_mask) != first_mask
    down_one = (lane & first_mask) != 0

    def rolled(tile, stride):
        return pltpu.roll(tile, LANES - stride, 1), pltpu.roll(tile, stride, 1)

    def neighbours(j, x, nxt, stride, in_lanes, carry):
        if not in_lanes:
            step = stride // LANES
            return src[PAD + j + step], src[PAD + j - step], carry
        up_here, down_here, down_last = carry
        up_next, down_next = rolled(nxt, stride)
        ahead = jnp.where(lane < LANES - stride, up_here, up_next)
        before = jnp.where(lane >= stride, down_here, down_last)
        return ahead, before, (up_next, down_next, down_here)

    def one_tile(j, carry):
        x, carry_two, carry_three = carry
        nxt = src[PAD + j + 1]
        ahead = jnp.where(up_one, pltpu.roll(x, LANES - 1, 1), 0.0)
        before = jnp.where(down_one, pltpu.roll(x, 1, 1), 0.0)
        total = ahead + before
        drift = weights[0] * (ahead - before)
        ahead, before, carry_two = neighbours(j, x, nxt, stride_two, lane_two, carry_two)
        node = (j * LANES + lane) & two_mask
        ahead = jnp.where(node < stride_three - stride_two, ahead, 0.0)
        before = jnp.where(node >= stride_two, before, 0.0)
        total = total + (ahead + before)
        drift = drift + weights[1] * (ahead - before)
        ahead, before, carry_three = neighbours(j, x, nxt, stride_three, lane_three, carry_three)
        total = total + (ahead + before)
        drift = drift + weights[2] * (ahead - before)
        ahead = pltpu.roll(x, 23, 0)
        before = pltpu.roll(x, 1, 0)
        total = total + (ahead + before)
        drift = drift + weights[3] * (ahead - before)
        new = x + dif[j] * (total - 8.0 * x) - drift
        dst[PAD + j] = jnp.where(valid, new, 0.0)
        return nxt, carry_two, carry_three

    def start(stride, in_lanes):
        if not in_lanes:
            return ()
        up_here, down_here = rolled(src[PAD], stride)
        return up_here, down_here, jnp.zeros((24, LANES), jnp.float32)

    def several(k, carry):
        for i in range(4):
            carry = one_tile(4 * k + i, carry)
        return carry

    lax.fori_loop(
        0,
        TILES // 4,
        several,
        (src[PAD], start(stride_two, lane_two), start(stride_three, lane_three)),
    )


def bit_ends(levels, q):
    one = levels[0, 0]
    two = one + levels[0, 1]
    begin = jnp.where(q < one, 0, jnp.where(q < two, one, two))
    end = jnp.where(q < one, one, jnp.where(q < two, two, LR))
    return begin, end


def lane_matrix(levels):
    rows = lax.broadcasted_iota(jnp.int32, (LANES, LANES), 0)
    lane = lax.broadcasted_iota(jnp.int32, (LANES, LANES), 1)
    own = (rows == lane).astype(jnp.float32)
    nxt = jnp.zeros((LANES, LANES), jnp.float32)
    for q in range(7):
        begin, end = bit_ends(levels, q)
        below = (1 << q) - (1 << begin)
        above = (1 << jnp.minimum(end, 7)) - (2 << q)
        here = ((lane & below) == 0) & ((lane & (1 << q)) != 0)
        full = (lane & above) == above
        ahead = pltpu.roll(own, LANES - (1 << q), 1)
        before = pltpu.roll(own, 1 << q, 1)
        half = jnp.where(here, -0.5, 0.0)
        nxt = nxt + jnp.where(full & (end > 7), half * ahead, 0.0)
        own = own + half * (before + jnp.where(full, 0.0, ahead))
    return jnp.concatenate([own, nxt], axis=0)


def surplus_rows(levels, sign, x, y, matrix, stage):
    rows = x.shape[1]
    x[TILES] = jnp.zeros((rows, LANES), jnp.float32)
    y[pl.ds(0, 32)] = jnp.zeros((32, rows, LANES), jnp.float32)
    y[pl.ds(32 + TILES, 32)] = jnp.zeros((32, rows, LANES), jnp.float32)

    _, end_six = bit_ends(levels, 6)
    mask_six = (1 << (jnp.maximum(end_six, 7) - 7)) - 1
    chunk = 16
    for j0 in range(0, TILES, chunk):
        own = x[pl.ds(j0, chunk)].reshape(chunk * rows, LANES)
        nxt = jnp.concatenate(
            [
                jnp.where(((j0 + i) & mask_six) == mask_six, 0.0, x[j0 + i + 1])
                for i in range(chunk)
            ],
            axis=0,
        )
        res = jnp.dot(
            jnp.concatenate([own, nxt], axis=1),
            matrix,
            precision=lax.Precision.HIGHEST,
            preferred_element_type=jnp.float32,
        )
        y[pl.ds(32 + j0, chunk)] = res.reshape(chunk, rows, LANES)

    lane = lax.broadcasted_iota(jnp.int32, (1, LANES), 1)
    for q in range(7, LR):
        t = 1 << (q - 7)
        begin, end = bit_ends(levels, q)
        low_lane = 128 - (1 << jnp.minimum(begin, 7))
        half = jnp.where((lane & low_lane) == 0, -0.5, 0.0)
        below = t - (1 << (jnp.maximum(begin, 7) - 7))
        above = (1 << (end - 7)) - 2 * t
        for j in range(TILES):
            if j & t:
                mine = jnp.where((j & below) == 0, half, 0.0)
                ahead_on = jnp.where((j & above) == above, 0.0, 1.0)
                y[32 + j] = y[32 + j] + mine * (y[32 + j - t] + ahead_on * y[32 + j + t])

    factor = sign[0].astype(jnp.float32)
    for j in range(TILES):
        tile = factor * y[32 + j]
        for i in range(0, rows, 8):
            stage[pl.ds(j + i * TILES, 8, stride=TILES), :] = tile[i : i + 8]


def rows_kernel(
    levels,
    velocity,
    sign,
    info_in,
    conc,
    dif_in,
    low,
    high,
    out,
    lead,
    outgoing,
    u_a,
    u_b,
    dif,
    x,
    y,
    info,
    info_sem,
    *,
    extras,
):
    places = pltpu.make_async_copy(info_in, info, info_sem)
    places.start()
    place = lax.axis_index("dom")
    count = lax.axis_size("dom")
    zeros = jnp.zeros((PAD, 24, LANES), jnp.float32)
    for ref in (u_a, u_b):
        ref[pl.ds(0, PAD)] = zeros
        ref[pl.ds(PAD + TILES, PAD)] = zeros
    tail = jnp.zeros((8, LANES), jnp.float32)
    for j in range(TILES):
        cols = pl.ds(j * LANES, LANES)
        u_a[PAD + j, 0:16] = conc[:, cols]
        u_a[PAD + j, 16:24] = tail
        dif[j, 0:16] = 0.1 * dif_in[:, cols]
        dif[j, 16:24] = tail
    for i in range(3):
        u_a[PAD : PAD + TILES, 16 + i] = high[i]
    for i in range(2):
        u_a[PAD : PAD + TILES, 22 + i] = low[i]
        dif[:, 16 + i] = 0.1 * high[3 + i]
    dif[:, 23] = 0.1 * low[2]
    row = lax.broadcasted_iota(jnp.int32, (24, LANES), 0)
    valid = (row < 16) | ((row < 20) & (place < count - 1)) | ((row >= 20) & (place > 0))
    weights = [0.1 * velocity[d] for d in range(4)]
    first_bits = levels[0, 0]
    second_bits = levels[0, 1]

    def both(lane_two, lane_three):
        def run():
            for src, dst in ((u_a, u_b), (u_b, u_a)):
                grid_step(
                    first_bits, second_bits, weights, valid, src, dst, dif, lane_two, lane_three
                )

        return run

    small_two = first_bits < 7
    small_three = first_bits + second_bits < 7
    pl.when(small_three)(both(True, True))
    pl.when(small_two & jnp.logical_not(small_three))(both(True, False))
    pl.when(jnp.logical_not(small_two))(both(False, False))
    lead[...] = u_a[PAD : PAD + TILES, 0]
    for j in range(TILES):
        tile = u_a[PAD + j]
        for p in range(4):
            s = 1 << p
            around = pltpu.roll(tile, 24 - s, 0) + pltpu.roll(tile, s, 0)
            hit = ((row & (2 * s - 1)) == s) & (row < 16)
            tile = tile - 0.5 * jnp.where(hit, around, 0.0)
        x[j] = tile[0:16]
    next_lead = u_a[PAD : PAD + TILES, 16]
    x[0:TILES, 0] = x[0:TILES, 0] - jnp.where((place & 1) == 1, 0.5, 0.0) * next_lead
    surplus_rows(levels, sign, x, y, lane_matrix(levels), out)
    places.wait()
    send_blocks(info, lambda b: out[8 * b : 8 * b + 8, :], outgoing, extras)


def send_blocks(info, block, outgoing, extras):
    use = info[3, 0]
    for b in range(info.shape[1]):
        outgoing[info[0, b] * use] = block(b)
    for i in range(extras):
        outgoing[info[4, i] * use] = -0.5 * block(i % 8)


def fix_kernel(levels, sign, coarse, blocks, out, x, y, stage):
    x[...] = jnp.zeros_like(x)
    x[0:TILES, 0] = coarse[...]
    surplus_rows(levels, sign, x, y, lane_matrix(levels), stage)
    out[...] = blocks[...]
    out[0:TILES, :] = blocks[0:TILES, :] - 0.5 * stage[0:TILES, :]


def scatter_kernel(info, blocks, out):
    for b in range(blocks.shape[0]):
        out[info[0, b]] = blocks[b]


def row_zero_uses(dom_count):
    uses = []
    distance = 1
    while distance < dom_count:
        uses.append((distance, 2 * distance))
        if distance > 1 and dom_count > 2 * distance:
            uses.append((-distance, 2 * distance))
        distance *= 2
    return uses


def has_use(place, offset, period, dom_count):
    return (place % period == 0) & (place + offset >= 0) & (place + offset < dom_count)


def extra_entries(values, dom_count, fill):
    devices, size = values.shape
    place = lax.broadcasted_iota(jnp.int32, (devices, size), 0) % dom_count
    lane = lax.broadcasted_iota(jnp.int32, (devices, size), 1)
    res = jnp.full((devices, size), fill, values.dtype)
    for t, (offset, period) in enumerate(row_zero_uses(dom_count)):
        cut = offset % devices
        moved = jnp.concatenate([values[cut:], values[:cut]], axis=0)
        moved = pltpu.roll(moved, 8 * t, 1) if t else moved
        hit = (lane >= 8 * t) & (lane < 8 * t + 8) & has_use(place, offset, period, dom_count)
        res = jnp.where(hit, moved, res)
    return res


def key_parts(keys, rows):
    owner = keys // SLOTS
    slot = keys % SLOTS
    row = owner % rows
    lane = slot + SLOTS * (owner // rows)
    return owner, slot, lane, row, (row + slot) % rows


def hot(index, count):
    which = lax.broadcasted_iota(jnp.int32, (count, index.shape[1]), 0)
    return jnp.where(which == index, 1.0, 0.0)


def dot_rows(left, right):
    return lax.dot_general(
        left.astype(jnp.bfloat16),
        right.astype(jnp.bfloat16),
        (((1,), (1,)), ((), ())),
        preferred_element_type=jnp.float32,
    )


def dot_plain(left, right):
    return jnp.dot(
        left.astype(jnp.bfloat16), right.astype(jnp.bfloat16), preferred_element_type=jnp.float32
    )


def mixed(handler, lane, row):
    x = (handler * 40503 + lane * 30011 + row * 52711) & 0xFFFF
    x = ((x ^ (x >> 7)) * 9973) & 0xFFFF
    x = ((x ^ (x >> 5)) * 12347) & 0xFFFF
    return (x >> 8).astype(jnp.float32) * (1.0 / 256.0)


def handlers_of(assigned, lane, row):
    return jnp.sum(
        hot(row, assigned.shape[0]) * dot_plain(assigned, hot(lane, LANES)), axis=0, keepdims=True
    )


def all_keys(keys):
    return keys[pl.ds(0, keys.shape[0] // COPIES, stride=COPIES), :]


def keys_of(keys, device):
    return keys[pl.ds(device * COPIES, 1), :]


def device_number():
    return lax.axis_index("grid") * lax.axis_size("dom") + lax.axis_index("dom")


def write_places(info, handler, extra, ok, me, devices, capacity):
    size = handler.shape[1]
    first = lax.broadcasted_iota(jnp.int32, (size, size), 0)
    second = lax.broadcasted_iota(jnp.int32, (size, size), 1)
    earlier = jnp.where(first < second, 1.0, 0.0)

    def placed(which, ahead):
        taken = hot(which.astype(jnp.int32), devices)
        rank = jnp.sum(taken * (dot_plain(taken, earlier) + ahead), axis=0, keepdims=True)
        place = which.astype(jnp.int32) * capacity + rank.astype(jnp.int32)
        stays = (which == me.astype(jnp.float32)) | (which < 0.0)
        return jnp.where(stays, me * capacity, place), stays, taken

    send, stays, taken = placed(handler, 0.0)
    send_extra, _, _ = placed(extra, jnp.sum(taken, axis=1, keepdims=True))
    kept = jnp.where(stays, 1, 0)
    flag = jnp.broadcast_to(ok, kept.shape).astype(jnp.int32)
    info[...] = jnp.concatenate([send, send, kept, flag, send_extra, flag, flag, flag], axis=0)


def owner_places_kernel(keys, info, *, devices, capacity):
    me = device_number()
    owner = (keys_of(keys, me) // SLOTS).astype(jnp.float32)
    none = jnp.full(owner.shape, -1.0, jnp.float32)
    write_places(info, owner, none, jnp.int32(0), me, devices, capacity)


def balance_kernel(keys, assigned, info, good, one, two, table, *, devices, capacity, full):
    rows = devices * SLOTS // LANES
    deep = devices + 8
    keys_all = all_keys(keys)
    _, _, lane_all, row_one, row_two = key_parts(keys_all, rows)
    dom_count = lax.axis_size("dom")
    lane_more, one_more, two_more = [
        extra_entries(v, dom_count, -1) for v in (lane_all, row_one, row_two)
    ]

    def counted(one_row, two_row, lane_row):
        both = jnp.concatenate([hot(one_row, rows), hot(two_row, rows)], axis=0)
        return dot_rows(both, hot(lane_row, LANES))

    for d in range(devices):
        pick = slice(d, d + 1)
        counts = counted(row_one[pick], row_two[pick], lane_all[pick])
        place = d % dom_count
        if any(has_use(place, *use, dom_count) for use in row_zero_uses(dom_count)):
            counts = counts + counted(one_more[pick], two_more[pick], lane_more[pick])
        one[pl.ds(d, rows, stride=deep), :] = counts[:rows]
        two[pl.ds(d, rows, stride=deep), :] = counts[rows:]
    for r in range(rows):
        spare = pl.ds(r * deep + devices, deep - devices)
        one[spare, :] = jnp.ones((deep - devices, LANES), jnp.float32)
        two[spare, :] = jnp.ones((deep - devices, LANES), jnp.float32)

    square = (devices, deep)
    sender = lax.broadcasted_iota(jnp.int32, square, 1)
    own = (lax.broadcasted_iota(jnp.int32, square, 0) == sender) | (sender >= devices)

    def price(load, steep):
        value = jnp.exp2(load * 0.3785) + steep * jnp.maximum(load - (capacity - 1), 0.0)
        return jnp.where(own, 0.0, value)

    def settle(counts_ref, group, first, load, number):
        base = number * group
        counts = jnp.concatenate(
            [
                counts_ref[pl.ds(pl.multiple_of((base + i) * deep, 8), deep), :]
                for i in range(group)
            ],
            axis=1,
        )
        shape = (devices, group * LANES)
        handler = lax.broadcasted_iota(jnp.int32, shape, 0)
        column = lax.broadcasted_iota(jnp.int32, shape, 1)
        handler_f = handler.astype(jnp.float32)
        cost = dot_plain(price(load, 4.0 if first else 16.0), counts)
        was = None
        if not first:
            old = jnp.concatenate([table[pl.ds(base + i, 1), :] for i in range(group)], axis=1)
            was = handler_f == old
            cost = jnp.where(was, dot_plain(price(load - 1.0, 16.0), counts) - 5.0, cost)
        noise = 0.5 * mixed(handler, column % LANES, base + column // LANES)
        ranked = jnp.floor((jnp.minimum(cost, 4000.0) + noise) * 64.0) * devices + handler_f
        least = jnp.min(ranked, axis=0, keepdims=True)
        chosen = least - jnp.floor(least * (1.0 / devices)) * devices
        for i in range(group):
            table[pl.ds(base + i, 1), :] = chosen[:, i * LANES : (i + 1) * LANES]
        change = jnp.where(handler_f == chosen, 1.0, 0.0)
        if not first:
            change = change - jnp.where(was, 1.0, 0.0)
        return load + dot_rows(change, counts)

    def sweep(counts_ref, group, first, load):
        return lax.fori_loop(
            0, rows // group, lambda i, x: settle(counts_ref, group, first, x, i), load
        )

    def worst(load):
        return jnp.max(jnp.where(own, 0.0, load))

    load = sweep(one, 4, True, jnp.zeros(square, jnp.float32))
    spot = lax.broadcasted_iota(jnp.int32, (rows, LANES), 0)
    lane = lax.broadcasted_iota(jnp.int32, (rows, LANES), 1)
    from_row = (spot + rows - (lane % SLOTS) % rows) % rows
    moved = jnp.zeros((rows, LANES), jnp.float32)
    for r in range(rows):
        moved = jnp.where(from_row == r, table[r : r + 1, :], moved)
    table[...] = moved
    load = sweep(two, 4, False, load)

    def again(state):
        count, _, load = state
        load = lax.cond(
            count == 0,
            lambda x: sweep(two, 4, False, x),
            lambda x: sweep(two, 2, False, x),
            load,
        )
        return count + 1, worst(load), load

    _, most, load = lax.while_loop(
        lambda state: (state[0] < 6) & (state[1] > capacity), again, (0, worst(load), load)
    )
    ok = (most <= capacity) & (jnp.max(jnp.where(sender < devices, 0.0, load)) <= MOST_KEYS)
    good[0] = ok.astype(jnp.int32)
    owner = (from_row + rows * (lane // SLOTS)).astype(jnp.float32)
    final = jnp.where(ok, table[...], owner)
    assigned[...] = final
    me = device_number()

    def found(device):
        _, _, lane_row, _, row = key_parts(keys_of(keys, device), rows)
        return handlers_of(final, lane_row, row)

    place = lax.axis_index("dom")
    column = lax.broadcasted_iota(jnp.int32, (1, keys.shape[1]), 1)
    extra = jnp.full((1, keys.shape[1]), -1.0, jnp.float32)
    for t, (offset, period) in enumerate(row_zero_uses(dom_count)):
        there = has_use(place, offset, period, dom_count)
        moved = found(jnp.where(there, me + offset, me))
        moved = pltpu.roll(moved, 8 * t, 1) if t else moved
        extra = jnp.where((column >= 8 * t) & (column < 8 * t + 8) & there, moved, extra)
    size = jnp.where(ok, capacity, full)
    write_places(info, found(me), extra, ok.astype(jnp.int32), me, devices, size)


def flat_rows(devices, capacity):
    return -(-devices * capacity // LANES)


def table_kernel(*refs, devices, capacity, pieces, balanced, more):
    if balanced:
        keys, assigned, out, handlers, numbers = refs
        me = device_number()
        rows = devices * SLOTS // LANES
        table = assigned[...]
        mine = jnp.where(table == me.astype(jnp.float32), 1.0, 0.0)
        first = lax.broadcasted_iota(jnp.int32, (LANES, LANES), 0)
        second = lax.broadcasted_iota(jnp.int32, (LANES, LANES), 1)
        in_row = dot_plain(mine, jnp.where(first < second, 1.0, 0.0))
        upper = lax.broadcasted_iota(jnp.int32, (rows, rows), 0)
        lower = lax.broadcasted_iota(jnp.int32, (rows, rows), 1)
        above = dot_plain(jnp.where(lower < upper, 1.0, 0.0), mine)
        number = in_row + jnp.sum(above, axis=1, keepdims=True)
        both = jnp.concatenate([table, jnp.where(mine > 0.0, number, 0.0)], axis=0)
        _, _, lane_all, _, row_all = key_parts(all_keys(keys), rows)
        for d in range(devices):
            at = slice(d, d + 1)
            found = dot_plain(both, hot(lane_all[at], LANES))
            pick = hot(row_all[at], rows)
            handlers[at, :] = jnp.sum(pick * found[:rows], axis=0, keepdims=True)
            numbers[at, :] = jnp.sum(pick * found[rows:], axis=0, keepdims=True)
        piece = numbers[...].astype(jnp.int32)
    else:
        keys, out, handlers, numbers = refs
        me = device_number()
        handlers[...] = (all_keys(keys) // SLOTS).astype(jnp.float32)
        piece = all_keys(keys) % SLOTS
    size = piece.shape[1]
    mine = handlers[...] == me.astype(jnp.float32)
    sender = lax.broadcasted_iota(jnp.int32, (devices, size), 0)
    first = lax.broadcasted_iota(jnp.int32, (size, size), 0)
    second = lax.broadcasted_iota(jnp.int32, (size, size), 1)
    earlier = jnp.where(first <= second, 1.0, 0.0)
    column = lax.broadcasted_iota(jnp.int32, (devices, LANES), 1)

    def ranked(hits, ahead):
        count = jnp.where(hits, 1.0, 0.0)
        return dot_plain(count, earlier) + ahead, jnp.sum(count, axis=1, keepdims=True)

    rank, total = ranked(mine, 0.0)
    groups = [(mine, rank, piece)]
    if more:
        dom_count = lax.axis_size("dom")
        mine_more = extra_entries(handlers[...], dom_count, -1.0) == me.astype(jnp.float32)
        rank_more, _ = ranked(mine_more, total)
        groups.append((mine_more, rank_more, extra_entries(piece, dom_count, 0)))
    lines = [jnp.zeros((devices, LANES), jnp.int32) for _ in range(flat_rows(devices, capacity))]
    spot = lax.broadcasted_iota(jnp.int32, (devices, LANES), 0) * capacity
    for r in range(capacity):
        at = jnp.zeros((devices, 1), jnp.int32)
        for hits, ranks, piece_of in groups:
            hit = hits & (sender != me) & (ranks == r + 1.0)
            at = at + jnp.sum(jnp.where(hit, piece_of - pieces, 0), axis=1, keepdims=True)
        for i in range(len(lines)):
            lines[i] = jnp.where(column + LANES * i == spot + r, at, lines[i])
    lines = [jnp.sum(line, axis=0, keepdims=True) for line in lines]
    for hits, _, piece_of in groups:
        stays = hits & (sender == me)
        lines.append(jnp.sum(jnp.where(stays, piece_of - pieces, 0), axis=0, keepdims=True))
    lines += [jnp.zeros((1, LANES), jnp.int32)] * (8 - len(lines))
    out[...] = jnp.concatenate(lines, axis=0) + pieces


def own_sum_kernel(table, own, pieces, *, arrive_rows, extras):
    zero = jnp.zeros((8, LANES), jnp.float32)

    def clear(k, carry):
        for i in range(8):
            pieces[8 * k + i] = zero
        return carry

    lax.fori_loop(0, pieces.shape[0] // 8, clear, 0)

    def add(k, carry):
        for i in range(8):
            piece = table[arrive_rows, 8 * k + i]
            pieces[piece] = pieces[piece] + own[8 * k + i]
        return carry

    lax.fori_loop(0, own.shape[0] // 8, add, 0)
    for i in range(extras):
        piece = table[arrive_rows + 1, i]
        pieces[piece] = pieces[piece] - 0.5 * own[i % 8]


def sum_kernel(table, arrived, pieces_in, out, pieces):
    places = arrived.shape[0]
    for i in range(places):
        piece = table[i // LANES, i % LANES]
        pieces[piece] = pieces[piece] + arrived[i]
    for i in range(places):
        out[i] = pieces[table[i // LANES, i % LANES]]


def own_back_kernel(table, pieces, out, *, arrive_rows):
    for b in range(out.shape[0]):
        out[b] = pieces[table[arrive_rows, b]]


def unpack_kernel(info, back, own, out, stage, rows, sems):
    halves = []
    for i in range(2):
        for b in range(TILES * i, TILES * (i + 1)):
            stage[pl.ds(8 * b, 8), :] = jnp.where(info[2, b] != 0, own[b], back[info[1, b]])
        for j in range(TILES):
            rows[8 * i : 8 * i + 8, j * LANES : (j + 1) * LANES] = stage[
                pl.ds(j + i * 8 * TILES, 8, stride=TILES), :
            ]
        half = pl.ds(8 * i, 8)
        halves.append(pltpu.make_async_copy(rows.at[half], out.at[half], sems.at[i]))
        halves[i].start()
    for half in halves:
        half.wait()


def f32(*shape):
    return jax.ShapeDtypeStruct(shape, jnp.float32)


def body(concentration, diffusion, velocity, levels, grid_signs, owner_list, slot_list):
    dom_count = lax.axis_size("dom")
    devices = lax.axis_size("grid") * dom_count
    rows = concentration.shape[1]
    conc = concentration[0]
    dif = diffusion[0]
    blocks = owner_list.shape[1]
    capacity = 2 * blocks // devices

    own_keys = owner_list * SLOTS + slot_list
    keys = lax.all_to_all(
        jnp.broadcast_to(own_keys[:, None], (devices, COPIES, blocks)),
        ("grid", "dom"),
        split_axis=0,
        concat_axis=0,
        tiled=True,
    ).reshape(devices * COPIES, blocks)

    up = [(i, i + 1) for i in range(dom_count - 1)]
    down = [(i + 1, i) for i in range(dom_count - 1)]
    low_rows = jnp.concatenate([conc[rows - 2 :], dif[rows - 1 :]], axis=0)
    high_rows = jnp.concatenate([conc[:3], dif[:2]], axis=0)
    low = lax.ppermute(low_rows.reshape(3, TILES, LANES), "dom", up)
    high = lax.ppermute(high_rows.reshape(5, TILES, LANES), "dom", down)

    balanced = capacity >= 8 and devices * SLOTS % LANES == 0 and devices <= 64
    info_shape = jax.ShapeDtypeStruct((8, blocks), jnp.int32)
    if balanced:
        key_rows = devices * SLOTS // LANES
        assigned, info, good = pl.pallas_call(
            functools.partial(
                balance_kernel, devices=devices, capacity=capacity // 2, full=capacity
            ),
            out_shape=(f32(key_rows, LANES), info_shape, jax.ShapeDtypeStruct((1,), jnp.int32)),
            in_specs=[VM],
            out_specs=(VM, VM, SM),
            scratch_shapes=[
                pltpu.VMEM((key_rows * (devices + 8), LANES), jnp.float32),
                pltpu.VMEM((key_rows * (devices + 8), LANES), jnp.float32),
                pltpu.VMEM((key_rows, LANES), jnp.float32),
            ],
            compiler_params=params(),
            name="balance",
            cost_estimate=SMALL,
        )(keys)
    else:
        info = pl.pallas_call(
            functools.partial(owner_places_kernel, devices=devices, capacity=capacity),
            out_shape=info_shape,
            in_specs=[VM],
            out_specs=VM,
            compiler_params=params(),
            name="places",
            cost_estimate=SMALL,
        )(keys)

    low, high, info = lax.optimization_barrier((low, high, info))
    slots = capacity // 2 if balanced else capacity
    extras = 8 * len(row_zero_uses(dom_count)) if balanced else 0
    blocks_in, lead, outgoing = pl.pallas_call(
        functools.partial(rows_kernel, extras=extras),
        out_shape=(
            f32(rows * TILES, LANES),
            f32(TILES, LANES),
            f32(devices * slots, 8, LANES),
        ),
        in_specs=[SM, SM, SM, VM, VM, VM, VM, VM],
        out_specs=(VM, VM, VM),
        scratch_shapes=[
            pltpu.VMEM((TILES + 2 * PAD, 24, LANES), jnp.float32),
            pltpu.VMEM((TILES + 2 * PAD, 24, LANES), jnp.float32),
            pltpu.VMEM((TILES, 24, LANES), jnp.float32),
            pltpu.VMEM((TILES + 1, 16, LANES), jnp.float32),
            pltpu.VMEM((TILES + 64, 16, LANES), jnp.float32),
            pltpu.SMEM((8, blocks), jnp.int32),
            pltpu.SemaphoreType.DMA,
        ],
        compiler_params=params(),
        name="rows",
        cost_estimate=SMALL,
    )(levels, velocity, grid_signs, info, conc, dif, low, high)

    def fixed():
        coarse = None
        for offset, period in row_zero_uses(dom_count):
            pairs = [
                (d, d + offset) for d in range(dom_count) if has_use(d, offset, period, dom_count)
            ]
            part = lax.ppermute(lead, "dom", pairs)
            coarse = part if coarse is None else coarse + part
        return pl.pallas_call(
            fix_kernel,
            out_shape=f32(rows * TILES, LANES),
            in_specs=[SM, SM, VM, VM],
            out_specs=VM,
            scratch_shapes=[
                pltpu.VMEM((TILES + 1, 8, LANES), jnp.float32),
                pltpu.VMEM((TILES + 64, 8, LANES), jnp.float32),
                pltpu.VMEM((8 * TILES, LANES), jnp.float32),
            ],
            compiler_params=params(),
            name="fix_row",
        )(levels, grid_signs, coarse, blocks_in)

    def route(own, outgoing, slots, extras, tables):
        pieces = MOST_KEYS if balanced else SLOTS
        arrive_rows = flat_rows(devices, slots)

        def exchange(x):
            return lax.all_to_all(
                x.reshape(devices, slots * 8, LANES),
                ("grid", "dom"),
                split_axis=0,
                concat_axis=0,
                tiled=True,
            ).reshape(devices * slots, 8, LANES)

        own = own.reshape(blocks, 8, LANES)
        if outgoing is None:
            outgoing = pl.pallas_call(
                scatter_kernel,
                out_shape=f32(devices * slots, 8, LANES),
                in_specs=[SM, VM],
                out_specs=VM,
                compiler_params=params(),
                name="scatter",
            )(info, own)
        arrived = exchange(outgoing)
        table = pl.pallas_call(
            functools.partial(
                table_kernel,
                devices=devices,
                capacity=slots,
                pieces=pieces,
                balanced=balanced,
                more=extras > 0,
            ),
            out_shape=jax.ShapeDtypeStruct((8, LANES), jnp.int32),
            in_specs=[VM] * len(tables),
            out_specs=VM,
            scratch_shapes=[pltpu.VMEM((devices, blocks), jnp.float32)] * 2,
            compiler_params=params(),
            name="piece_table",
        )(*tables)
        all_pieces = f32(pieces + 8, 8, LANES)
        started = pl.pallas_call(
            functools.partial(own_sum_kernel, arrive_rows=arrive_rows, extras=extras),
            out_shape=all_pieces,
            in_specs=[SM, VM],
            out_specs=VM,
            compiler_params=params(),
            name="sum_own",
        )(table, own)
        returned, summed = pl.pallas_call(
            sum_kernel,
            out_shape=(f32(devices * slots, 8, LANES), all_pieces),
            in_specs=[SM, VM, VM],
            out_specs=(VM, VM),
            input_output_aliases={2: 1},
            compiler_params=params(),
            name="sum_arrived",
        )(table, arrived, started)
        own_back = pl.pallas_call(
            functools.partial(own_back_kernel, arrive_rows=arrive_rows),
            out_shape=f32(blocks, 8, LANES),
            in_specs=[SM, VM],
            out_specs=VM,
            compiler_params=params(),
            name="own_back",
        )(table, summed)
        back = exchange(returned)
        return pl.pallas_call(
            unpack_kernel,
            out_shape=f32(rows, TILES * LANES),
            in_specs=[SM, VM, VM],
            out_specs=HBM,
            scratch_shapes=[
                pltpu.VMEM((16 * TILES, LANES), jnp.float32),
                pltpu.VMEM((16, TILES * LANES), jnp.float32),
                pltpu.SemaphoreType.DMA((2,)),
            ],
            compiler_params=params(),
            name="unpack",
        )(info, back, own_back)

    if balanced:
        combined = lax.cond(
            good[0] != 0,
            lambda: route(blocks_in, outgoing, slots, extras, (keys, assigned)),
            lambda: route(fixed(), None, capacity, 0, (keys, assigned)),
        )
    else:
        combined = route(fixed(), None, capacity, 0, (keys,))
    return combined[None]


def solution(mesh):
    return jax.shard_map(
        body,
        mesh=mesh,
        in_specs=(
            P("grid", "dom", None),
            P("grid", "dom", None),
            P(),
            P("grid", None),
            P("grid"),
            P(("grid", "dom"), None),
            P(("grid", "dom"), None),
        ),
        out_specs=P("grid", "dom", None),
        check_vma=False,
    )
```

```python
import functools

import jax
import jax.numpy as jnp
from jax import lax
from jax.experimental import pallas as pl
from jax.experimental.pallas import tpu as pltpu
from jax.sharding import PartitionSpec as P

LR = 13
BLK = 1024
SLOTS = 64
LANES = 128
TILES = 2**LR // LANES
PAD = 9
COPIES = 8
MOST_KEYS = 256
VMEM_LIMIT = 48 * 1024 * 1024


def params():
    return pltpu.CompilerParams(vmem_limit_bytes=VMEM_LIMIT)


SMALL = pl.CostEstimate(flops=0, transcendentals=0, bytes_accessed=0)
VM = pl.BlockSpec(memory_space=pltpu.VMEM)
HBM = pl.BlockSpec(memory_space=pltpu.HBM)
SM = pl.BlockSpec(memory_space=pltpu.SMEM)


def grid_step(first_bits, second_bits, weights, valid, src, dst, dif, lane_two, lane_three):
    lane = lax.broadcasted_iota(jnp.int32, (1, LANES), 1)
    first_mask = (1 << first_bits) - 1
    stride_two = 1 << first_bits
    stride_three = 1 << (first_bits + second_bits)
    two_mask = stride_three - 1
    up_one = (lane & first_mask) != first_mask
    down_one = (lane & first_mask) != 0

    def rolled(tile, stride):
        return pltpu.roll(tile, LANES - stride, 1), pltpu.roll(tile, stride, 1)

    def neighbours(j, x, nxt, stride, in_lanes, carry):
        if not in_lanes:
            step = stride // LANES
            return src[PAD + j + step], src[PAD + j - step], carry
        up_here, down_here, down_last = carry
        up_next, down_next = rolled(nxt, stride)
        ahead = jnp.where(lane < LANES - stride, up_here, up_next)
        before = jnp.where(lane >= stride, down_here, down_last)
        return ahead, before, (up_next, down_next, down_here)

    def one_tile(j, carry):
        x, carry_two, carry_three = carry
        nxt = src[PAD + j + 1]
        ahead = jnp.where(up_one, pltpu.roll(x, LANES - 1, 1), 0.0)
        before = jnp.where(down_one, pltpu.roll(x, 1, 1), 0.0)
        total = ahead + before
        drift = weights[0] * (ahead - before)
        ahead, before, carry_two = neighbours(j, x, nxt, stride_two, lane_two, carry_two)
        node = (j * LANES + lane) & two_mask
        ahead = jnp.where(node < stride_three - stride_two, ahead, 0.0)
        before = jnp.where(node >= stride_two, before, 0.0)
        total = total + (ahead + before)
        drift = drift + weights[1] * (ahead - before)
        ahead, before, carry_three = neighbours(j, x, nxt, stride_three, lane_three, carry_three)
        total = total + (ahead + before)
        drift = drift + weights[2] * (ahead - before)
        ahead = pltpu.roll(x, 23, 0)
        before = pltpu.roll(x, 1, 0)
        total = total + (ahead + before)
        drift = drift + weights[3] * (ahead - before)
        new = x + dif[j] * (total - 8.0 * x) - drift
        dst[PAD + j] = jnp.where(valid, new, 0.0)
        return nxt, carry_two, carry_three

    def start(stride, in_lanes):
        if not in_lanes:
            return ()
        up_here, down_here = rolled(src[PAD], stride)
        return up_here, down_here, jnp.zeros((24, LANES), jnp.float32)

    def several(k, carry):
        for i in range(4):
            carry = one_tile(4 * k + i, carry)
        return carry

    lax.fori_loop(
        0,
        TILES // 4,
        several,
        (src[PAD], start(stride_two, lane_two), start(stride_three, lane_three)),
    )


def bit_ends(levels, q):
    one = levels[0, 0]
    two = one + levels[0, 1]
    begin = jnp.where(q < one, 0, jnp.where(q < two, one, two))
    end = jnp.where(q < one, one, jnp.where(q < two, two, LR))
    return begin, end


def lane_matrix(levels):
    rows = lax.broadcasted_iota(jnp.int32, (LANES, LANES), 0)
    lane = lax.broadcasted_iota(jnp.int32, (LANES, LANES), 1)
    own = (rows == lane).astype(jnp.float32)
    nxt = jnp.zeros((LANES, LANES), jnp.float32)
    for q in range(7):
        begin, end = bit_ends(levels, q)
        below = (1 << q) - (1 << begin)
        above = (1 << jnp.minimum(end, 7)) - (2 << q)
        here = ((lane & below) == 0) & ((lane & (1 << q)) != 0)
        full = (lane & above) == above
        ahead = pltpu.roll(own, LANES - (1 << q), 1)
        before = pltpu.roll(own, 1 << q, 1)
        half = jnp.where(here, -0.5, 0.0)
        nxt = nxt + jnp.where(full & (end > 7), half * ahead, 0.0)
        own = own + half * (before + jnp.where(full, 0.0, ahead))
    return jnp.concatenate([own, nxt], axis=0)


def surplus_rows(levels, factor, x, y, matrix, stage):
    rows = x.shape[1]
    x[TILES] = jnp.zeros((rows, LANES), jnp.float32)
    y[pl.ds(0, 32)] = jnp.zeros((32, rows, LANES), jnp.float32)
    y[pl.ds(32 + TILES, 32)] = jnp.zeros((32, rows, LANES), jnp.float32)

    _, end_six = bit_ends(levels, 6)
    mask_six = (1 << (jnp.maximum(end_six, 7) - 7)) - 1
    chunk = 16
    for j0 in range(0, TILES, chunk):
        own = x[pl.ds(j0, chunk)].reshape(chunk * rows, LANES)
        nxt = jnp.concatenate(
            [
                jnp.where(((j0 + i) & mask_six) == mask_six, 0.0, x[j0 + i + 1])
                for i in range(chunk)
            ],
            axis=0,
        )
        res = jnp.dot(
            jnp.concatenate([own, nxt], axis=1),
            matrix,
            precision=lax.Precision.HIGHEST,
            preferred_element_type=jnp.float32,
        )
        y[pl.ds(32 + j0, chunk)] = res.reshape(chunk, rows, LANES)

    lane = lax.broadcasted_iota(jnp.int32, (1, LANES), 1)
    for q in range(7, LR):
        t = 1 << (q - 7)
        begin, end = bit_ends(levels, q)
        low_lane = 128 - (1 << jnp.minimum(begin, 7))
        half = jnp.where((lane & low_lane) == 0, -0.5, 0.0)
        below = t - (1 << (jnp.maximum(begin, 7) - 7))
        above = (1 << (end - 7)) - 2 * t
        for j in range(TILES):
            if j & t:
                mine = jnp.where((j & below) == 0, half, 0.0)
                ahead_on = jnp.where((j & above) == above, 0.0, 1.0)
                y[32 + j] = y[32 + j] + mine * (y[32 + j - t] + ahead_on * y[32 + j + t])

    for j in range(TILES):
        tile = factor * y[32 + j]
        for i in range(0, rows, 8):
            stage[pl.ds(j + i * TILES, 8, stride=TILES), :] = tile[i : i + 8]


def rows_kernel(
    levels,
    velocity,
    sign_in,
    info_in,
    conc,
    dif_in,
    low,
    high,
    out,
    lead,
    outgoing,
    u_a,
    u_b,
    dif,
    x,
    y,
    info,
    sign,
    sems,
    *,
    extras,
):
    places = pltpu.make_async_copy(info_in, info, sems.at[0])
    places.start()
    signs = pltpu.make_async_copy(sign_in, sign, sems.at[1])
    signs.start()
    place = lax.axis_index("dom")
    count = lax.axis_size("dom")
    zeros = jnp.zeros((PAD, 24, LANES), jnp.float32)
    for ref in (u_a, u_b):
        ref[pl.ds(0, PAD)] = zeros
        ref[pl.ds(PAD + TILES, PAD)] = zeros
    tail = jnp.zeros((8, LANES), jnp.float32)
    for j in range(TILES):
        cols = pl.ds(j * LANES, LANES)
        u_a[PAD + j, 0:16] = conc[:, cols]
        u_a[PAD + j, 16:24] = tail
        dif[j, 0:16] = 0.1 * dif_in[:, cols]
        dif[j, 16:24] = tail
    for i in range(3):
        u_a[PAD : PAD + TILES, 16 + i] = high[i]
    for i in range(2):
        u_a[PAD : PAD + TILES, 22 + i] = low[i]
        dif[:, 16 + i] = 0.1 * high[3 + i]
    dif[:, 23] = 0.1 * low[2]
    row = lax.broadcasted_iota(jnp.int32, (24, LANES), 0)
    valid = (row < 16) | ((row < 20) & (place < count - 1)) | ((row >= 20) & (place > 0))
    weights = [0.1 * velocity[d] for d in range(4)]
    first_bits = levels[0, 0]
    second_bits = levels[0, 1]

    def both(lane_two, lane_three):
        def run():
            for src, dst in ((u_a, u_b), (u_b, u_a)):
                grid_step(
                    first_bits, second_bits, weights, valid, src, dst, dif, lane_two, lane_three
                )

        return run

    small_two = first_bits < 7
    small_three = first_bits + second_bits < 7
    pl.when(small_three)(both(True, True))
    pl.when(small_two & jnp.logical_not(small_three))(both(True, False))
    pl.when(jnp.logical_not(small_two))(both(False, False))
    signs.wait()
    factor = sign[0].astype(jnp.float32)
    lead[...] = factor * u_a[PAD : PAD + TILES, 0]
    for j in range(TILES):
        tile = u_a[PAD + j]
        for p in range(4):
            s = 1 << p
            around = pltpu.roll(tile, 24 - s, 0) + pltpu.roll(tile, s, 0)
            hit = ((row & (2 * s - 1)) == s) & (row < 16)
            tile = tile - 0.5 * jnp.where(hit, around, 0.0)
        x[j] = tile[0:16]
    next_lead = u_a[PAD : PAD + TILES, 16]
    x[0:TILES, 0] = x[0:TILES, 0] - jnp.where((place & 1) == 1, 0.5, 0.0) * next_lead
    surplus_rows(levels, factor, x, y, lane_matrix(levels), out)
    places.wait()
    send_blocks(info, lambda b: out[8 * b : 8 * b + 8, :], outgoing, extras)


def send_blocks(info, block, outgoing, extras):
    use = info[3, 0]
    for b in range(info.shape[1]):
        outgoing[info[0, b] * use] = block(b)
    for i in range(extras):
        outgoing[info[4, i] * use] = -0.5 * block(i % 8)


def fix_kernel(levels, coarse, blocks, out, x, y, stage):
    x[...] = jnp.zeros_like(x)
    x[0:TILES, 0] = coarse[...]
    surplus_rows(levels, 1.0, x, y, lane_matrix(levels), stage)
    out[...] = blocks[...]
    out[0:TILES, :] = blocks[0:TILES, :] - 0.5 * stage[0:TILES, :]


def scatter_kernel(info, blocks, out):
    for b in range(blocks.shape[0]):
        out[info[0, b]] = blocks[b]


def row_zero_uses(dom_count):
    uses = []
    distance = 1
    while distance < dom_count:
        uses.append((distance, 2 * distance))
        if distance > 1 and dom_count > 2 * distance:
            uses.append((-distance, 2 * distance))
        distance *= 2
    return uses


def has_use(place, offset, period, dom_count):
    return (place % period == 0) & (place + offset >= 0) & (place + offset < dom_count)


def extra_entries(values, dom_count, fill):
    devices, size = values.shape
    place = lax.broadcasted_iota(jnp.int32, (devices, size), 0) % dom_count
    lane = lax.broadcasted_iota(jnp.int32, (devices, size), 1)
    res = jnp.full((devices, size), fill, values.dtype)
    for t, (offset, period) in enumerate(row_zero_uses(dom_count)):
        cut = offset % devices
        moved = jnp.concatenate([values[cut:], values[:cut]], axis=0)
        moved = pltpu.roll(moved, 8 * t, 1) if t else moved
        hit = (lane >= 8 * t) & (lane < 8 * t + 8) & has_use(place, offset, period, dom_count)
        res = jnp.where(hit, moved, res)
    return res


def key_parts(keys, rows):
    owner = keys // SLOTS
    slot = keys % SLOTS
    row = owner % rows
    lane = slot + SLOTS * (owner // rows)
    return owner, slot, lane, row, (row + slot) % rows


def hot(index, count):
    which = lax.broadcasted_iota(jnp.int32, (count, index.shape[1]), 0)
    return jnp.where(which == index, 1.0, 0.0)


def dot_rows(left, right):
    return lax.dot_general(
        left.astype(jnp.bfloat16),
        right.astype(jnp.bfloat16),
        (((1,), (1,)), ((), ())),
        preferred_element_type=jnp.float32,
    )


def dot_plain(left, right):
    return jnp.dot(
        left.astype(jnp.bfloat16), right.astype(jnp.bfloat16), preferred_element_type=jnp.float32
    )


def mixed(handler, lane, row):
    x = (handler * 40503 + lane * 30011 + row * 52711) & 0xFFFF
    x = ((x ^ (x >> 7)) * 9973) & 0xFFFF
    x = ((x ^ (x >> 5)) * 12347) & 0xFFFF
    return (x >> 8).astype(jnp.float32) * (1.0 / 256.0)


def handlers_of(assigned, lane, row):
    return jnp.sum(
        hot(row, assigned.shape[0]) * dot_plain(assigned, hot(lane, LANES)), axis=0, keepdims=True
    )


def all_keys(keys):
    return keys[pl.ds(0, keys.shape[0] // COPIES, stride=COPIES), :]


def keys_of(keys, device):
    return keys[pl.ds(device * COPIES, 1), :]


def device_number():
    return lax.axis_index("grid") * lax.axis_size("dom") + lax.axis_index("dom")


def write_places(info, handler, extra, ok, me, devices, capacity):
    size = handler.shape[1]
    first = lax.broadcasted_iota(jnp.int32, (size, size), 0)
    second = lax.broadcasted_iota(jnp.int32, (size, size), 1)
    earlier = jnp.where(first < second, 1.0, 0.0)

    def placed(which, ahead):
        taken = hot(which.astype(jnp.int32), devices)
        rank = jnp.sum(taken * (dot_plain(taken, earlier) + ahead), axis=0, keepdims=True)
        place = which.astype(jnp.int32) * capacity + rank.astype(jnp.int32)
        stays = (which == me.astype(jnp.float32)) | (which < 0.0)
        return jnp.where(stays, me * capacity, place), stays, taken

    send, stays, taken = placed(handler, 0.0)
    send_extra, _, _ = placed(extra, jnp.sum(taken, axis=1, keepdims=True))
    kept = jnp.where(stays, 1, 0)
    flag = jnp.broadcast_to(ok, kept.shape).astype(jnp.int32)
    info[...] = jnp.concatenate([send, send, kept, flag, send_extra, flag, flag, flag], axis=0)


def spread_kernel(keys, out):
    out[...] = jnp.broadcast_to(keys[...], out.shape)


def halo_kernel(conc, dif, low, high):
    last = conc.shape[0] - 1
    for j in range(TILES):
        cols = slice(j * LANES, (j + 1) * LANES)
        for i, (ref, row) in enumerate(((conc, last - 1), (conc, last), (dif, last))):
            low[i, j : j + 1, :] = ref[row : row + 1, cols]
        for i, (ref, row) in enumerate(((conc, 0), (conc, 1), (conc, 2), (dif, 0), (dif, 1))):
            high[i, j : j + 1, :] = ref[row : row + 1, cols]


def owner_places_kernel(keys, info, *, devices, capacity):
    me = device_number()
    owner = (keys_of(keys, me) // SLOTS).astype(jnp.float32)
    none = jnp.full(owner.shape, -1.0, jnp.float32)
    write_places(info, owner, none, jnp.int32(0), me, devices, capacity)


def balance_kernel(
    keys, assigned, info, good_out, one, two, table, good, good_sem, *, devices, capacity, full
):
    rows = devices * SLOTS // LANES
    deep = devices + 8
    keys_all = all_keys(keys)
    _, _, lane_all, row_one, row_two = key_parts(keys_all, rows)
    dom_count = lax.axis_size("dom")
    lane_more, one_more, two_more = [
        extra_entries(v, dom_count, -1) for v in (lane_all, row_one, row_two)
    ]

    def counted(one_row, two_row, lane_row):
        both = jnp.concatenate([hot(one_row, rows), hot(two_row, rows)], axis=0)
        return dot_rows(both, hot(lane_row, LANES))

    for d in range(devices):
        pick = slice(d, d + 1)
        counts = counted(row_one[pick], row_two[pick], lane_all[pick])
        place = d % dom_count
        if any(has_use(place, *use, dom_count) for use in row_zero_uses(dom_count)):
            counts = counts + counted(one_more[pick], two_more[pick], lane_more[pick])
        one[pl.ds(d, rows, stride=deep), :] = counts[:rows]
        two[pl.ds(d, rows, stride=deep), :] = counts[rows:]
    for r in range(rows):
        spare = pl.ds(r * deep + devices, deep - devices)
        one[spare, :] = jnp.ones((deep - devices, LANES), jnp.float32)
        two[spare, :] = jnp.ones((deep - devices, LANES), jnp.float32)

    square = (devices, deep)
    sender = lax.broadcasted_iota(jnp.int32, square, 1)
    own = (lax.broadcasted_iota(jnp.int32, square, 0) == sender) | (sender >= devices)

    def price(load, steep):
        value = jnp.exp2(load * 0.3785) + steep * jnp.maximum(load - (capacity - 1), 0.0)
        return jnp.where(own, 0.0, value)

    def settle(counts_ref, group, first, load, number):
        base = number * group
        counts = jnp.concatenate(
            [
                counts_ref[pl.ds(pl.multiple_of((base + i) * deep, 8), deep), :]
                for i in range(group)
            ],
            axis=1,
        )
        shape = (devices, group * LANES)
        handler = lax.broadcasted_iota(jnp.int32, shape, 0)
        column = lax.broadcasted_iota(jnp.int32, shape, 1)
        handler_f = handler.astype(jnp.float32)
        cost = dot_plain(price(load, 4.0 if first else 16.0), counts)
        was = None
        if not first:
            old = jnp.concatenate([table[pl.ds(base + i, 1), :] for i in range(group)], axis=1)
            was = handler_f == old
            cost = jnp.where(was, dot_plain(price(load - 1.0, 16.0), counts) - 5.0, cost)
        noise = 0.5 * mixed(handler, column % LANES, base + column // LANES)
        ranked = jnp.floor((jnp.minimum(cost, 4000.0) + noise) * 64.0) * devices + handler_f
        least = jnp.min(ranked, axis=0, keepdims=True)
        chosen = least - jnp.floor(least * (1.0 / devices)) * devices
        for i in range(group):
            table[pl.ds(base + i, 1), :] = chosen[:, i * LANES : (i + 1) * LANES]
        change = jnp.where(handler_f == chosen, 1.0, 0.0)
        if not first:
            change = change - jnp.where(was, 1.0, 0.0)
        return load + dot_rows(change, counts)

    def sweep(counts_ref, group, first, load):
        return lax.fori_loop(
            0, rows // group, lambda i, x: settle(counts_ref, group, first, x, i), load
        )

    def worst(load):
        return jnp.max(jnp.where(own, 0.0, load))

    load = sweep(one, 4, True, jnp.zeros(square, jnp.float32))
    spot = lax.broadcasted_iota(jnp.int32, (rows, LANES), 0)
    lane = lax.broadcasted_iota(jnp.int32, (rows, LANES), 1)
    from_row = (spot + rows - (lane % SLOTS) % rows) % rows
    moved = jnp.zeros((rows, LANES), jnp.float32)
    for r in range(rows):
        moved = jnp.where(from_row == r, table[r : r + 1, :], moved)
    table[...] = moved
    load = sweep(two, 4, False, load)

    def again(state):
        count, _, load = state
        load = lax.cond(
            count == 0,
            lambda x: sweep(two, 4, False, x),
            lambda x: sweep(two, 2, False, x),
            load,
        )
        return count + 1, worst(load), load

    _, most, load = lax.while_loop(
        lambda state: (state[0] < 6) & (state[1] > capacity), again, (0, worst(load), load)
    )
    ok = (most <= capacity) & (jnp.max(jnp.where(sender < devices, 0.0, load)) <= MOST_KEYS)
    good[0] = ok.astype(jnp.int32)
    tell = pltpu.make_async_copy(good, good_out, good_sem)
    tell.start()
    owner = (from_row + rows * (lane // SLOTS)).astype(jnp.float32)
    final = jnp.where(ok, table[...], owner)
    assigned[...] = final
    me = device_number()

    def found(device):
        _, _, lane_row, _, row = key_parts(keys_of(keys, device), rows)
        return handlers_of(final, lane_row, row)

    place = lax.axis_index("dom")
    column = lax.broadcasted_iota(jnp.int32, (1, keys.shape[1]), 1)
    extra = jnp.full((1, keys.shape[1]), -1.0, jnp.float32)
    for t, (offset, period) in enumerate(row_zero_uses(dom_count)):
        there = has_use(place, offset, period, dom_count)
        moved = found(jnp.where(there, me + offset, me))
        moved = pltpu.roll(moved, 8 * t, 1) if t else moved
        extra = jnp.where((column >= 8 * t) & (column < 8 * t + 8) & there, moved, extra)
    size = jnp.where(ok, capacity, full)
    write_places(info, found(me), extra, ok.astype(jnp.int32), me, devices, size)
    tell.wait()


def flat_rows(devices, capacity):
    return -(-devices * capacity // LANES)


def table_kernel(*refs, devices, capacity, pieces, balanced, more):
    if balanced:
        keys, assigned, out, handlers, numbers = refs
        me = device_number()
        rows = devices * SLOTS // LANES
        table = assigned[...]
        mine = jnp.where(table == me.astype(jnp.float32), 1.0, 0.0)
        first = lax.broadcasted_iota(jnp.int32, (LANES, LANES), 0)
        second = lax.broadcasted_iota(jnp.int32, (LANES, LANES), 1)
        in_row = dot_plain(mine, jnp.where(first < second, 1.0, 0.0))
        upper = lax.broadcasted_iota(jnp.int32, (rows, rows), 0)
        lower = lax.broadcasted_iota(jnp.int32, (rows, rows), 1)
        above = dot_plain(jnp.where(lower < upper, 1.0, 0.0), mine)
        number = in_row + jnp.sum(above, axis=1, keepdims=True)
        both = jnp.concatenate([table, jnp.where(mine > 0.0, number, 0.0)], axis=0)
        _, _, lane_all, _, row_all = key_parts(all_keys(keys), rows)
        for d in range(devices):
            at = slice(d, d + 1)
            found = dot_plain(both, hot(lane_all[at], LANES))
            pick = hot(row_all[at], rows)
            handlers[at, :] = jnp.sum(pick * found[:rows], axis=0, keepdims=True)
            numbers[at, :] = jnp.sum(pick * found[rows:], axis=0, keepdims=True)
        piece = numbers[...].astype(jnp.int32)
    else:
        keys, out, handlers, numbers = refs
        me = device_number()
        handlers[...] = (all_keys(keys) // SLOTS).astype(jnp.float32)
        piece = all_keys(keys) % SLOTS
    size = piece.shape[1]
    mine = handlers[...] == me.astype(jnp.float32)
    sender = lax.broadcasted_iota(jnp.int32, (devices, size), 0)
    first = lax.broadcasted_iota(jnp.int32, (size, size), 0)
    second = lax.broadcasted_iota(jnp.int32, (size, size), 1)
    earlier = jnp.where(first <= second, 1.0, 0.0)
    column = lax.broadcasted_iota(jnp.int32, (devices, LANES), 1)

    def ranked(hits, ahead):
        count = jnp.where(hits, 1.0, 0.0)
        return dot_plain(count, earlier) + ahead, jnp.sum(count, axis=1, keepdims=True)

    rank, total = ranked(mine, 0.0)
    groups = [(mine, rank, piece)]
    if more:
        dom_count = lax.axis_size("dom")
        mine_more = extra_entries(handlers[...], dom_count, -1.0) == me.astype(jnp.float32)
        rank_more, _ = ranked(mine_more, total)
        groups.append((mine_more, rank_more, extra_entries(piece, dom_count, 0)))
    lines = [jnp.zeros((devices, LANES), jnp.int32) for _ in range(flat_rows(devices, capacity))]
    spot = lax.broadcasted_iota(jnp.int32, (devices, LANES), 0) * capacity
    for r in range(capacity):
        at = jnp.zeros((devices, 1), jnp.int32)
        for hits, ranks, piece_of in groups:
            hit = hits & (sender != me) & (ranks == r + 1.0)
            at = at + jnp.sum(jnp.where(hit, piece_of - pieces, 0), axis=1, keepdims=True)
        for i in range(len(lines)):
            lines[i] = jnp.where(column + LANES * i == spot + r, at, lines[i])
    lines = [jnp.sum(line, axis=0, keepdims=True) for line in lines]
    for hits, _, piece_of in groups:
        stays = hits & (sender == me)
        lines.append(jnp.sum(jnp.where(stays, piece_of - pieces, 0), axis=0, keepdims=True))
    lines += [jnp.zeros((1, LANES), jnp.int32)] * (8 - len(lines))
    out[...] = jnp.concatenate(lines, axis=0) + pieces


def own_sum_kernel(table, own, pieces, *, arrive_rows, extras):
    zero = jnp.zeros((8, LANES), jnp.float32)

    def clear(k, carry):
        for i in range(8):
            pieces[8 * k + i] = zero
        return carry

    lax.fori_loop(0, pieces.shape[0] // 8, clear, 0)

    def add(k, carry):
        for i in range(8):
            piece = table[arrive_rows, 8 * k + i]
            pieces[piece] = pieces[piece] + own[8 * k + i]
        return carry

    lax.fori_loop(0, own.shape[0] // 8, add, 0)
    for i in range(extras):
        piece = table[arrive_rows + 1, i]
        pieces[piece] = pieces[piece] - 0.5 * own[i % 8]


def sum_kernel(table, arrived, pieces_in, out, pieces):
    places = arrived.shape[0]
    for i in range(places):
        piece = table[i // LANES, i % LANES]
        pieces[piece] = pieces[piece] + arrived[i]
    for i in range(places):
        out[i] = pieces[table[i // LANES, i % LANES]]


def own_back_kernel(table, pieces, out, *, arrive_rows):
    for b in range(out.shape[0]):
        out[b] = pieces[table[arrive_rows, b]]


def unpack_kernel(info, back, own, out, stage, rows, sems):
    halves = []
    for i in range(2):
        for b in range(TILES * i, TILES * (i + 1)):
            stage[pl.ds(8 * b, 8), :] = jnp.where(info[2, b] != 0, own[b], back[info[1, b]])
        for j in range(TILES):
            rows[8 * i : 8 * i + 8, j * LANES : (j + 1) * LANES] = stage[
                pl.ds(j + i * 8 * TILES, 8, stride=TILES), :
            ]
        half = pl.ds(8 * i, 8)
        halves.append(pltpu.make_async_copy(rows.at[half], out.at[half], sems.at[i]))
        halves[i].start()
    for half in halves:
        half.wait()


def f32(*shape):
    return jax.ShapeDtypeStruct(shape, jnp.float32)


def body(concentration, diffusion, velocity, levels, grid_signs, owner_list, slot_list):
    dom_count = lax.axis_size("dom")
    devices = lax.axis_size("grid") * dom_count
    rows = concentration.shape[1]
    conc = concentration[0]
    dif = diffusion[0]
    blocks = owner_list.shape[1]
    capacity = 2 * blocks // devices

    spread = pl.pallas_call(
        spread_kernel,
        out_shape=jax.ShapeDtypeStruct((devices * COPIES, blocks), jnp.int32),
        in_specs=[VM],
        out_specs=VM,
        compiler_params=params(),
        name="spread_keys",
        cost_estimate=pl.CostEstimate(flops=10**10, transcendentals=0, bytes_accessed=0),
    )(owner_list * SLOTS + slot_list)
    spread, conc, dif = lax.optimization_barrier((spread, conc, dif))
    keys = lax.all_to_all(
        spread.reshape(devices, COPIES, blocks),
        ("grid", "dom"),
        split_axis=0,
        concat_axis=0,
        tiled=True,
    ).reshape(devices * COPIES, blocks)

    up = [(i, i + 1) for i in range(dom_count - 1)]
    down = [(i + 1, i) for i in range(dom_count - 1)]
    low_rows, high_rows = pl.pallas_call(
        halo_kernel,
        out_shape=(f32(3, TILES, LANES), f32(5, TILES, LANES)),
        in_specs=[VM, VM],
        out_specs=(VM, VM),
        compiler_params=params(),
        name="halo_rows",
    )(conc, dif)
    low = lax.ppermute(low_rows, "dom", up)
    high = lax.ppermute(high_rows, "dom", down)

    balanced = capacity >= 8 and devices * SLOTS % LANES == 0 and devices <= 64
    info_shape = jax.ShapeDtypeStruct((8, blocks), jnp.int32)
    if balanced:
        key_rows = devices * SLOTS // LANES
        assigned, info, good = pl.pallas_call(
            functools.partial(
                balance_kernel, devices=devices, capacity=capacity // 2, full=capacity
            ),
            out_shape=(f32(key_rows, LANES), info_shape, jax.ShapeDtypeStruct((1,), jnp.int32)),
            in_specs=[VM],
            out_specs=(VM, VM, HBM),
            scratch_shapes=[
                pltpu.VMEM((key_rows * (devices + 8), LANES), jnp.float32),
                pltpu.VMEM((key_rows * (devices + 8), LANES), jnp.float32),
                pltpu.VMEM((key_rows, LANES), jnp.float32),
                pltpu.SMEM((1,), jnp.int32),
                pltpu.SemaphoreType.DMA,
            ],
            compiler_params=params(),
            name="balance",
            cost_estimate=SMALL,
        )(keys)
    else:
        info = pl.pallas_call(
            functools.partial(owner_places_kernel, devices=devices, capacity=capacity),
            out_shape=info_shape,
            in_specs=[VM],
            out_specs=VM,
            compiler_params=params(),
            name="places",
            cost_estimate=SMALL,
        )(keys)

    low, high, info = lax.optimization_barrier((low, high, info))
    slots = capacity // 2 if balanced else capacity
    extras = 8 * len(row_zero_uses(dom_count)) if balanced else 0
    blocks_in, lead, outgoing = pl.pallas_call(
        functools.partial(rows_kernel, extras=extras),
        out_shape=(
            f32(rows * TILES, LANES),
            f32(TILES, LANES),
            f32(devices * slots, 8, LANES),
        ),
        in_specs=[SM, SM, HBM, VM, VM, VM, VM, VM],
        out_specs=(VM, VM, VM),
        scratch_shapes=[
            pltpu.VMEM((TILES + 2 * PAD, 24, LANES), jnp.float32),
            pltpu.VMEM((TILES + 2 * PAD, 24, LANES), jnp.float32),
            pltpu.VMEM((TILES, 24, LANES), jnp.float32),
            pltpu.VMEM((TILES + 1, 16, LANES), jnp.float32),
            pltpu.VMEM((TILES + 64, 16, LANES), jnp.float32),
            pltpu.SMEM((8, blocks), jnp.int32),
            pltpu.SMEM((1,), jnp.int32),
            pltpu.SemaphoreType.DMA((2,)),
        ],
        compiler_params=params(),
        name="rows",
        cost_estimate=SMALL,
    )(levels, velocity, grid_signs, info, conc, dif, low, high)

    def fixed():
        coarse = None
        for offset, period in row_zero_uses(dom_count):
            pairs = [
                (d, d + offset) for d in range(dom_count) if has_use(d, offset, period, dom_count)
            ]
            part = lax.ppermute(lead, "dom", pairs)
            coarse = part if coarse is None else coarse + part
        return pl.pallas_call(
            fix_kernel,
            out_shape=f32(rows * TILES, LANES),
            in_specs=[SM, VM, VM],
            out_specs=VM,
            scratch_shapes=[
                pltpu.VMEM((TILES + 1, 8, LANES), jnp.float32),
                pltpu.VMEM((TILES + 64, 8, LANES), jnp.float32),
                pltpu.VMEM((8 * TILES, LANES), jnp.float32),
            ],
            compiler_params=params(),
            name="fix_row",
        )(levels, coarse, blocks_in)

    def route(own, outgoing, slots, extras, tables):
        pieces = MOST_KEYS if balanced else SLOTS
        arrive_rows = flat_rows(devices, slots)

        def exchange(x):
            return lax.all_to_all(
                x.reshape(devices, slots * 8, LANES),
                ("grid", "dom"),
                split_axis=0,
                concat_axis=0,
                tiled=True,
            ).reshape(devices * slots, 8, LANES)

        own = own.reshape(blocks, 8, LANES)
        if outgoing is None:
            outgoing = pl.pallas_call(
                scatter_kernel,
                out_shape=f32(devices * slots, 8, LANES),
                in_specs=[SM, VM],
                out_specs=VM,
                compiler_params=params(),
                name="scatter",
            )(info, own)
        arrived = exchange(outgoing)
        table = pl.pallas_call(
            functools.partial(
                table_kernel,
                devices=devices,
                capacity=slots,
                pieces=pieces,
                balanced=balanced,
                more=extras > 0,
            ),
            out_shape=jax.ShapeDtypeStruct((8, LANES), jnp.int32),
            in_specs=[VM] * len(tables),
            out_specs=VM,
            scratch_shapes=[pltpu.VMEM((devices, blocks), jnp.float32)] * 2,
            compiler_params=params(),
            name="piece_table",
        )(*tables)
        all_pieces = f32(pieces + 8, 8, LANES)
        started = pl.pallas_call(
            functools.partial(own_sum_kernel, arrive_rows=arrive_rows, extras=extras),
            out_shape=all_pieces,
            in_specs=[SM, VM],
            out_specs=VM,
            compiler_params=params(),
            name="sum_own",
        )(table, own)
        returned, summed = pl.pallas_call(
            sum_kernel,
            out_shape=(f32(devices * slots, 8, LANES), all_pieces),
            in_specs=[SM, VM, VM],
            out_specs=(VM, VM),
            input_output_aliases={2: 1},
            compiler_params=params(),
            name="sum_arrived",
        )(table, arrived, started)
        own_back = pl.pallas_call(
            functools.partial(own_back_kernel, arrive_rows=arrive_rows),
            out_shape=f32(blocks, 8, LANES),
            in_specs=[SM, VM],
            out_specs=VM,
            compiler_params=params(),
            name="own_back",
        )(table, summed)
        return exchange(returned), own_back

    def unpacked(back, own_back):
        return pl.pallas_call(
            unpack_kernel,
            out_shape=f32(rows, TILES * LANES),
            in_specs=[SM, VM, VM],
            out_specs=HBM,
            scratch_shapes=[
                pltpu.VMEM((16 * TILES, LANES), jnp.float32),
                pltpu.VMEM((16, TILES * LANES), jnp.float32),
                pltpu.SemaphoreType.DMA((2,)),
            ],
            compiler_params=params(),
            name="unpack",
        )(info, back, own_back)

    if balanced:
        brought = route(blocks_in, outgoing, slots, extras, (keys, assigned))
        combined = lax.cond(
            good[0] != 0,
            lambda: unpacked(*brought),
            lambda: unpacked(*route(fixed(), None, capacity, 0, (keys, assigned))),
        )
    else:
        combined = unpacked(*route(fixed(), None, capacity, 0, (keys,)))
    return combined[None]


def solution(mesh):
    return jax.shard_map(
        body,
        mesh=mesh,
        in_specs=(
            P("grid", "dom", None),
            P("grid", "dom", None),
            P(),
            P("grid", None),
            P("grid"),
            P(("grid", "dom"), None),
            P(("grid", "dom"), None),
        ),
        out_specs=P("grid", "dom", None),
        check_vma=False,
    )
```

```python
import functools

import jax
import jax.numpy as jnp
from jax import lax
from jax.experimental import pallas as pl
from jax.experimental.pallas import tpu as pltpu
from jax.sharding import PartitionSpec as P

LR = 13
BLK = 1024
SLOTS = 64
LANES = 128
TILES = 2**LR // LANES
PAD = 9
COPIES = 8
MOST_KEYS = 256
VMEM_LIMIT = 48 * 1024 * 1024


def params():
    return pltpu.CompilerParams(vmem_limit_bytes=VMEM_LIMIT)


SMALL = pl.CostEstimate(flops=0, transcendentals=0, bytes_accessed=0)
VM = pl.BlockSpec(memory_space=pltpu.VMEM)
HBM = pl.BlockSpec(memory_space=pltpu.HBM)
SM = pl.BlockSpec(memory_space=pltpu.SMEM)


def grid_step(first_bits, second_bits, weights, valid, src, dst, dif, lane_two, lane_three):
    lane = lax.broadcasted_iota(jnp.int32, (1, LANES), 1)
    first_mask = (1 << first_bits) - 1
    stride_two = 1 << first_bits
    stride_three = 1 << (first_bits + second_bits)
    two_mask = stride_three - 1
    up_one = (lane & first_mask) != first_mask
    down_one = (lane & first_mask) != 0

    def rolled(tile, stride):
        return pltpu.roll(tile, LANES - stride, 1), pltpu.roll(tile, stride, 1)

    def neighbours(j, x, nxt, stride, in_lanes, carry):
        if not in_lanes:
            step = stride // LANES
            return src[PAD + j + step], src[PAD + j - step], carry
        up_here, down_here, down_last = carry
        up_next, down_next = rolled(nxt, stride)
        ahead = jnp.where(lane < LANES - stride, up_here, up_next)
        before = jnp.where(lane >= stride, down_here, down_last)
        return ahead, before, (up_next, down_next, down_here)

    def one_tile(j, carry):
        x, carry_two, carry_three = carry
        nxt = src[PAD + j + 1]
        ahead = jnp.where(up_one, pltpu.roll(x, LANES - 1, 1), 0.0)
        before = jnp.where(down_one, pltpu.roll(x, 1, 1), 0.0)
        total = ahead + before
        drift = weights[0] * (ahead - before)
        ahead, before, carry_two = neighbours(j, x, nxt, stride_two, lane_two, carry_two)
        node = (j * LANES + lane) & two_mask
        ahead = jnp.where(node < stride_three - stride_two, ahead, 0.0)
        before = jnp.where(node >= stride_two, before, 0.0)
        total = total + (ahead + before)
        drift = drift + weights[1] * (ahead - before)
        ahead, before, carry_three = neighbours(j, x, nxt, stride_three, lane_three, carry_three)
        total = total + (ahead + before)
        drift = drift + weights[2] * (ahead - before)
        ahead = pltpu.roll(x, 23, 0)
        before = pltpu.roll(x, 1, 0)
        total = total + (ahead + before)
        drift = drift + weights[3] * (ahead - before)
        new = x + dif[j] * (total - 8.0 * x) - drift
        dst[PAD + j] = jnp.where(valid, new, 0.0)
        return nxt, carry_two, carry_three

    def start(stride, in_lanes):
        if not in_lanes:
            return ()
        up_here, down_here = rolled(src[PAD], stride)
        return up_here, down_here, jnp.zeros((24, LANES), jnp.float32)

    def several(k, carry):
        for i in range(8):
            carry = one_tile(8 * k + i, carry)
        return carry

    lax.fori_loop(
        0,
        TILES // 8,
        several,
        (src[PAD], start(stride_two, lane_two), start(stride_three, lane_three)),
    )


def bit_ends(levels, q):
    one = levels[0, 0]
    two = one + levels[0, 1]
    begin = jnp.where(q < one, 0, jnp.where(q < two, one, two))
    end = jnp.where(q < one, one, jnp.where(q < two, two, LR))
    return begin, end


def lane_matrix(levels):
    rows = lax.broadcasted_iota(jnp.int32, (LANES, LANES), 0)
    lane = lax.broadcasted_iota(jnp.int32, (LANES, LANES), 1)
    own = (rows == lane).astype(jnp.float32)
    nxt = jnp.zeros((LANES, LANES), jnp.float32)
    for q in range(7):
        begin, end = bit_ends(levels, q)
        below = (1 << q) - (1 << begin)
        above = (1 << jnp.minimum(end, 7)) - (2 << q)
        here = ((lane & below) == 0) & ((lane & (1 << q)) != 0)
        full = (lane & above) == above
        ahead = pltpu.roll(own, LANES - (1 << q), 1)
        before = pltpu.roll(own, 1 << q, 1)
        half = jnp.where(here, -0.5, 0.0)
        nxt = nxt + jnp.where(full & (end > 7), half * ahead, 0.0)
        own = own + half * (before + jnp.where(full, 0.0, ahead))
    return jnp.concatenate([own, nxt], axis=0)


def exact_dot(left, right):
    total = None
    for _ in range(3):
        part = left.astype(jnp.bfloat16)
        term = jnp.dot(part, right, preferred_element_type=jnp.float32)
        total = term if total is None else total + term
        left = left - part.astype(jnp.float32)
    return total


def surplus_rows(levels, factor, x, y, matrix, stage):
    rows = x.shape[1]
    x[TILES] = jnp.zeros((rows, LANES), jnp.float32)
    y[pl.ds(0, 32)] = jnp.zeros((32, rows, LANES), jnp.float32)
    y[pl.ds(32 + TILES, 32)] = jnp.zeros((32, rows, LANES), jnp.float32)

    _, end_six = bit_ends(levels, 6)
    mask_six = (1 << (jnp.maximum(end_six, 7) - 7)) - 1
    chunk = 16
    matrix = matrix.astype(jnp.bfloat16)
    for j0 in range(0, TILES, chunk):
        own = x[pl.ds(j0, chunk)].reshape(chunk * rows, LANES)
        nxt = jnp.concatenate(
            [
                jnp.where(((j0 + i) & mask_six) == mask_six, 0.0, x[j0 + i + 1])
                for i in range(chunk)
            ],
            axis=0,
        )
        res = exact_dot(jnp.concatenate([own, nxt], axis=1), matrix)
        y[pl.ds(32 + j0, chunk)] = res.reshape(chunk, rows, LANES)

    lane = lax.broadcasted_iota(jnp.int32, (1, LANES), 1)
    for q in range(7, LR):
        t = 1 << (q - 7)
        begin, end = bit_ends(levels, q)
        low_lane = 128 - (1 << jnp.minimum(begin, 7))
        half = jnp.where((lane & low_lane) == 0, -0.5, 0.0)
        below = t - (1 << (jnp.maximum(begin, 7) - 7))
        above = (1 << (end - 7)) - 2 * t
        for j in range(TILES):
            if j & t:
                mine = jnp.where((j & below) == 0, half, 0.0)
                ahead_on = jnp.where((j & above) == above, 0.0, 1.0)
                y[32 + j] = y[32 + j] + mine * (y[32 + j - t] + ahead_on * y[32 + j + t])

    for j in range(TILES):
        tile = factor * y[32 + j]
        for i in range(0, rows, 8):
            stage[pl.ds(j + i * TILES, 8, stride=TILES), :] = tile[i : i + 8]


def rows_kernel(
    levels,
    velocity,
    sign_in,
    info_in,
    conc,
    dif_in,
    low,
    high,
    out,
    lead,
    outgoing,
    u_a,
    u_b,
    dif,
    x,
    y,
    info,
    sign,
    sems,
    *,
    extras,
):
    places = pltpu.make_async_copy(info_in, info, sems.at[0])
    places.start()
    signs = pltpu.make_async_copy(sign_in, sign, sems.at[1])
    signs.start()
    place = lax.axis_index("dom")
    count = lax.axis_size("dom")
    zeros = jnp.zeros((PAD, 24, LANES), jnp.float32)
    for ref in (u_a, u_b):
        ref[pl.ds(0, PAD)] = zeros
        ref[pl.ds(PAD + TILES, PAD)] = zeros
    tail = jnp.zeros((8, LANES), jnp.float32)
    for j in range(TILES):
        cols = pl.ds(j * LANES, LANES)
        u_a[PAD + j, 0:16] = conc[:, cols]
        u_a[PAD + j, 16:24] = tail
        dif[j, 0:16] = 0.1 * dif_in[:, cols]
        dif[j, 16:24] = tail
    for i in range(3):
        u_a[PAD : PAD + TILES, 16 + i] = high[i]
    for i in range(2):
        u_a[PAD : PAD + TILES, 22 + i] = low[i]
        dif[:, 16 + i] = 0.1 * high[3 + i]
    dif[:, 23] = 0.1 * low[2]
    row = lax.broadcasted_iota(jnp.int32, (24, LANES), 0)
    valid = (row < 16) | ((row < 20) & (place < count - 1)) | ((row >= 20) & (place > 0))
    weights = [0.1 * velocity[d] for d in range(4)]
    first_bits = levels[0, 0]
    second_bits = levels[0, 1]

    def both(lane_two, lane_three):
        def run():
            for src, dst in ((u_a, u_b), (u_b, u_a)):
                grid_step(
                    first_bits, second_bits, weights, valid, src, dst, dif, lane_two, lane_three
                )

        return run

    small_two = first_bits < 7
    small_three = first_bits + second_bits < 7
    pl.when(small_three)(both(True, True))
    pl.when(small_two & jnp.logical_not(small_three))(both(True, False))
    pl.when(jnp.logical_not(small_two))(both(False, False))
    signs.wait()
    factor = sign[0].astype(jnp.float32)
    lead[...] = factor * u_a[PAD : PAD + TILES, 0]
    for j in range(TILES):
        tile = u_a[PAD + j]
        for p in range(4):
            s = 1 << p
            around = pltpu.roll(tile, 24 - s, 0) + pltpu.roll(tile, s, 0)
            hit = ((row & (2 * s - 1)) == s) & (row < 16)
            tile = tile - 0.5 * jnp.where(hit, around, 0.0)
        x[j] = tile[0:16]
    next_lead = u_a[PAD : PAD + TILES, 16]
    x[0:TILES, 0] = x[0:TILES, 0] - jnp.where((place & 1) == 1, 0.5, 0.0) * next_lead
    surplus_rows(levels, factor, x, y, lane_matrix(levels), out)
    places.wait()
    send_blocks(info, lambda b: out[8 * b : 8 * b + 8, :], outgoing, extras)


def send_blocks(info, block, outgoing, extras):
    use = info[3, 0]
    for b in range(info.shape[1]):
        outgoing[info[0, b] * use] = block(b)
    for i in range(extras):
        outgoing[info[4, i] * use] = -0.5 * block(i % 8)


def fix_kernel(levels, coarse, blocks, out, x, y, stage):
    x[...] = jnp.zeros_like(x)
    x[0:TILES, 0] = coarse[...]
    surplus_rows(levels, 1.0, x, y, lane_matrix(levels), stage)
    out[...] = blocks[...]
    out[0:TILES, :] = blocks[0:TILES, :] - 0.5 * stage[0:TILES, :]


def scatter_kernel(info, blocks, out):
    for b in range(blocks.shape[0]):
        out[info[0, b]] = blocks[b]


def row_zero_uses(dom_count):
    uses = []
    distance = 1
    while distance < dom_count:
        uses.append((distance, 2 * distance))
        if distance > 1 and dom_count > 2 * distance:
            uses.append((-distance, 2 * distance))
        distance *= 2
    return uses


def has_use(place, offset, period, dom_count):
    return (place % period == 0) & (place + offset >= 0) & (place + offset < dom_count)


def extra_entries(values, dom_count, fill):
    devices, size = values.shape
    place = lax.broadcasted_iota(jnp.int32, (devices, size), 0) % dom_count
    lane = lax.broadcasted_iota(jnp.int32, (devices, size), 1)
    res = jnp.full((devices, size), fill, values.dtype)
    for t, (offset, period) in enumerate(row_zero_uses(dom_count)):
        cut = offset % devices
        moved = jnp.concatenate([values[cut:], values[:cut]], axis=0)
        moved = pltpu.roll(moved, 8 * t, 1) if t else moved
        hit = (lane >= 8 * t) & (lane < 8 * t + 8) & has_use(place, offset, period, dom_count)
        res = jnp.where(hit, moved, res)
    return res


def key_parts(keys, rows):
    owner = keys // SLOTS
    slot = keys % SLOTS
    row = owner % rows
    lane = slot + SLOTS * (owner // rows)
    return owner, slot, lane, row, (row + slot) % rows


def hot(index, count):
    which = lax.broadcasted_iota(jnp.int32, (count, index.shape[1]), 0)
    return jnp.where(which == index, 1.0, 0.0)


def dot_rows(left, right):
    return lax.dot_general(
        left.astype(jnp.bfloat16),
        right.astype(jnp.bfloat16),
        (((1,), (1,)), ((), ())),
        preferred_element_type=jnp.float32,
    )


def dot_plain(left, right):
    return jnp.dot(
        left.astype(jnp.bfloat16), right.astype(jnp.bfloat16), preferred_element_type=jnp.float32
    )


def mixed(handler, lane, row):
    x = (handler * 40503 + lane * 30011 + row * 52711) & 0xFFFF
    x = ((x ^ (x >> 7)) * 9973) & 0xFFFF
    x = ((x ^ (x >> 5)) * 12347) & 0xFFFF
    return (x >> 8).astype(jnp.float32) * (1.0 / 256.0)


def handlers_of(assigned, lane, row):
    return jnp.sum(
        hot(row, assigned.shape[0]) * dot_plain(assigned, hot(lane, LANES)), axis=0, keepdims=True
    )


def all_keys(keys):
    return keys[pl.ds(0, keys.shape[0] // COPIES, stride=COPIES), :]


def keys_of(keys, device):
    return keys[pl.ds(device * COPIES, 1), :]


def device_number():
    return lax.axis_index("grid") * lax.axis_size("dom") + lax.axis_index("dom")


def write_places(info, handler, extra, ok, me, devices, capacity):
    size = handler.shape[1]
    first = lax.broadcasted_iota(jnp.int32, (size, size), 0)
    second = lax.broadcasted_iota(jnp.int32, (size, size), 1)
    earlier = jnp.where(first < second, 1.0, 0.0)

    def placed(which, ahead):
        taken = hot(which.astype(jnp.int32), devices)
        rank = jnp.sum(taken * (dot_plain(taken, earlier) + ahead), axis=0, keepdims=True)
        place = which.astype(jnp.int32) * capacity + rank.astype(jnp.int32)
        stays = (which == me.astype(jnp.float32)) | (which < 0.0)
        return jnp.where(stays, me * capacity, place), stays, taken

    send, stays, taken = placed(handler, 0.0)
    send_extra, _, _ = placed(extra, jnp.sum(taken, axis=1, keepdims=True))
    kept = jnp.where(stays, 1, 0)
    flag = jnp.broadcast_to(ok, kept.shape).astype(jnp.int32)
    info[...] = jnp.concatenate([send, send, kept, flag, send_extra, flag, flag, flag], axis=0)


def spread_kernel(keys, out):
    out[...] = jnp.broadcast_to(keys[...], out.shape)


def halo_kernel(conc, dif, low, high):
    last = conc.shape[0] - 1
    for j in range(TILES):
        cols = slice(j * LANES, (j + 1) * LANES)
        for i, (ref, row) in enumerate(((conc, last - 1), (conc, last), (dif, last))):
            low[i, j : j + 1, :] = ref[row : row + 1, cols]
        for i, (ref, row) in enumerate(((conc, 0), (conc, 1), (conc, 2), (dif, 0), (dif, 1))):
            high[i, j : j + 1, :] = ref[row : row + 1, cols]


def owner_places_kernel(keys, info, *, devices, capacity):
    me = device_number()
    owner = (keys_of(keys, me) // SLOTS).astype(jnp.float32)
    none = jnp.full(owner.shape, -1.0, jnp.float32)
    write_places(info, owner, none, jnp.int32(0), me, devices, capacity)


def balance_kernel(
    keys, assigned, info, good_out, one, two, table, good, good_sem, *, devices, capacity, full
):
    rows = devices * SLOTS // LANES
    deep = devices + 8
    keys_all = all_keys(keys)
    _, _, lane_all, row_one, row_two = key_parts(keys_all, rows)
    dom_count = lax.axis_size("dom")
    lane_more, one_more, two_more = [
        extra_entries(v, dom_count, -1) for v in (lane_all, row_one, row_two)
    ]

    def counted(one_row, two_row, lane_row):
        both = jnp.concatenate([hot(one_row, rows), hot(two_row, rows)], axis=0)
        return dot_rows(both, hot(lane_row, LANES))

    for d in range(devices):
        pick = slice(d, d + 1)
        counts = counted(row_one[pick], row_two[pick], lane_all[pick])
        place = d % dom_count
        if any(has_use(place, *use, dom_count) for use in row_zero_uses(dom_count)):
            counts = counts + counted(one_more[pick], two_more[pick], lane_more[pick])
        one[pl.ds(d, rows, stride=deep), :] = counts[:rows]
        two[pl.ds(d, rows, stride=deep), :] = counts[rows:]
    for r in range(rows):
        spare = pl.ds(r * deep + devices, deep - devices)
        one[spare, :] = jnp.ones((deep - devices, LANES), jnp.float32)
        two[spare, :] = jnp.ones((deep - devices, LANES), jnp.float32)

    square = (devices, deep)
    sender = lax.broadcasted_iota(jnp.int32, square, 1)
    own = (lax.broadcasted_iota(jnp.int32, square, 0) == sender) | (sender >= devices)

    def price(load, steep):
        value = jnp.exp2(load * 0.3785) + steep * jnp.maximum(load - (capacity - 1), 0.0)
        return jnp.where(own, 0.0, value)

    def settle(counts_ref, group, first, load, number):
        base = number * group
        counts = jnp.concatenate(
            [
                counts_ref[pl.ds(pl.multiple_of((base + i) * deep, 8), deep), :]
                for i in range(group)
            ],
            axis=1,
        )
        shape = (devices, group * LANES)
        handler = lax.broadcasted_iota(jnp.int32, shape, 0)
        column = lax.broadcasted_iota(jnp.int32, shape, 1)
        handler_f = handler.astype(jnp.float32)
        cost = dot_plain(price(load, 4.0 if first else 16.0), counts)
        was = None
        if not first:
            old = jnp.concatenate([table[pl.ds(base + i, 1), :] for i in range(group)], axis=1)
            was = handler_f == old
            cost = jnp.where(was, dot_plain(price(load - 1.0, 16.0), counts) - 5.0, cost)
        noise = 0.5 * mixed(handler, column % LANES, base + column // LANES)
        ranked = jnp.floor((jnp.minimum(cost, 4000.0) + noise) * 64.0) * devices + handler_f
        least = jnp.min(ranked, axis=0, keepdims=True)
        chosen = least - jnp.floor(least * (1.0 / devices)) * devices
        for i in range(group):
            table[pl.ds(base + i, 1), :] = chosen[:, i * LANES : (i + 1) * LANES]
        change = jnp.where(handler_f == chosen, 1.0, 0.0)
        if not first:
            change = change - jnp.where(was, 1.0, 0.0)
        return load + dot_rows(change, counts)

    def sweep(counts_ref, group, first, load):
        return lax.fori_loop(
            0, rows // group, lambda i, x: settle(counts_ref, group, first, x, i), load
        )

    def worst(load):
        return jnp.max(jnp.where(own, 0.0, load))

    load = sweep(one, 4, True, jnp.zeros(square, jnp.float32))
    spot = lax.broadcasted_iota(jnp.int32, (rows, LANES), 0)
    lane = lax.broadcasted_iota(jnp.int32, (rows, LANES), 1)
    from_row = (spot + rows - (lane % SLOTS) % rows) % rows
    moved = jnp.zeros((rows, LANES), jnp.float32)
    for r in range(rows):
        moved = jnp.where(from_row == r, table[r : r + 1, :], moved)
    table[...] = moved
    load = sweep(two, 4, False, load)

    def again(state):
        count, _, load = state
        load = lax.cond(
            count == 0,
            lambda x: sweep(two, 4, False, x),
            lambda x: sweep(two, 2, False, x),
            load,
        )
        return count + 1, worst(load), load

    _, most, load = lax.while_loop(
        lambda state: (state[0] < 6) & (state[1] > capacity), again, (0, worst(load), load)
    )
    ok = (most <= capacity) & (jnp.max(jnp.where(sender < devices, 0.0, load)) <= MOST_KEYS)
    good[0] = ok.astype(jnp.int32)
    tell = pltpu.make_async_copy(good, good_out, good_sem)
    tell.start()
    owner = (from_row + rows * (lane // SLOTS)).astype(jnp.float32)
    final = jnp.where(ok, table[...], owner)
    assigned[...] = final
    me = device_number()

    def found(device):
        _, _, lane_row, _, row = key_parts(keys_of(keys, device), rows)
        return handlers_of(final, lane_row, row)

    place = lax.axis_index("dom")
    column = lax.broadcasted_iota(jnp.int32, (1, keys.shape[1]), 1)
    extra = jnp.full((1, keys.shape[1]), -1.0, jnp.float32)
    for t, (offset, period) in enumerate(row_zero_uses(dom_count)):
        there = has_use(place, offset, period, dom_count)
        moved = found(jnp.where(there, me + offset, me))
        moved = pltpu.roll(moved, 8 * t, 1) if t else moved
        extra = jnp.where((column >= 8 * t) & (column < 8 * t + 8) & there, moved, extra)
    size = jnp.where(ok, capacity, full)
    write_places(info, found(me), extra, ok.astype(jnp.int32), me, devices, size)
    tell.wait()


def flat_rows(devices, capacity):
    return -(-devices * capacity // LANES)


def table_kernel(*refs, devices, capacity, pieces, balanced, more):
    if balanced:
        keys, assigned, out, handlers, numbers = refs
        me = device_number()
        rows = devices * SLOTS // LANES
        table = assigned[...]
        mine = jnp.where(table == me.astype(jnp.float32), 1.0, 0.0)
        first = lax.broadcasted_iota(jnp.int32, (LANES, LANES), 0)
        second = lax.broadcasted_iota(jnp.int32, (LANES, LANES), 1)
        in_row = dot_plain(mine, jnp.where(first < second, 1.0, 0.0))
        upper = lax.broadcasted_iota(jnp.int32, (rows, rows), 0)
        lower = lax.broadcasted_iota(jnp.int32, (rows, rows), 1)
        above = dot_plain(jnp.where(lower < upper, 1.0, 0.0), mine)
        number = in_row + jnp.sum(above, axis=1, keepdims=True)
        both = jnp.concatenate([table, jnp.where(mine > 0.0, number, 0.0)], axis=0)
        _, _, lane_all, _, row_all = key_parts(all_keys(keys), rows)
        for d in range(devices):
            at = slice(d, d + 1)
            found = dot_plain(both, hot(lane_all[at], LANES))
            pick = hot(row_all[at], rows)
            handlers[at, :] = jnp.sum(pick * found[:rows], axis=0, keepdims=True)
            numbers[at, :] = jnp.sum(pick * found[rows:], axis=0, keepdims=True)
        piece = numbers[...].astype(jnp.int32)
    else:
        keys, out, handlers, numbers = refs
        me = device_number()
        handlers[...] = (all_keys(keys) // SLOTS).astype(jnp.float32)
        piece = all_keys(keys) % SLOTS
    size = piece.shape[1]
    mine = handlers[...] == me.astype(jnp.float32)
    sender = lax.broadcasted_iota(jnp.int32, (devices, size), 0)
    first = lax.broadcasted_iota(jnp.int32, (size, size), 0)
    second = lax.broadcasted_iota(jnp.int32, (size, size), 1)
    earlier = jnp.where(first <= second, 1.0, 0.0)
    column = lax.broadcasted_iota(jnp.int32, (devices, LANES), 1)

    def ranked(hits, ahead):
        count = jnp.where(hits, 1.0, 0.0)
        return dot_plain(count, earlier) + ahead, jnp.sum(count, axis=1, keepdims=True)

    rank, total = ranked(mine, 0.0)
    groups = [(mine, rank, piece)]
    if more:
        dom_count = lax.axis_size("dom")
        mine_more = extra_entries(handlers[...], dom_count, -1.0) == me.astype(jnp.float32)
        rank_more, _ = ranked(mine_more, total)
        groups.append((mine_more, rank_more, extra_entries(piece, dom_count, 0)))
    lines = [jnp.zeros((devices, LANES), jnp.int32) for _ in range(flat_rows(devices, capacity))]
    spot = lax.broadcasted_iota(jnp.int32, (devices, LANES), 0) * capacity
    for r in range(capacity):
        at = jnp.zeros((devices, 1), jnp.int32)
        for hits, ranks, piece_of in groups:
            hit = hits & (sender != me) & (ranks == r + 1.0)
            at = at + jnp.sum(jnp.where(hit, piece_of - pieces, 0), axis=1, keepdims=True)
        for i in range(len(lines)):
            lines[i] = jnp.where(column + LANES * i == spot + r, at, lines[i])
    lines = [jnp.sum(line, axis=0, keepdims=True) for line in lines]
    for hits, _, piece_of in groups:
        stays = hits & (sender == me)
        lines.append(jnp.sum(jnp.where(stays, piece_of - pieces, 0), axis=0, keepdims=True))
    lines += [jnp.zeros((1, LANES), jnp.int32)] * (8 - len(lines))
    out[...] = jnp.concatenate(lines, axis=0) + pieces


def own_sum_kernel(table, own, pieces, *, arrive_rows, extras):
    zero = jnp.zeros((8, LANES), jnp.float32)

    def clear(k, carry):
        for i in range(8):
            pieces[8 * k + i] = zero
        return carry

    lax.fori_loop(0, pieces.shape[0] // 8, clear, 0)

    def add(k, carry):
        for i in range(8):
            piece = table[arrive_rows, 8 * k + i]
            pieces[piece] = pieces[piece] + own[8 * k + i]
        return carry

    lax.fori_loop(0, own.shape[0] // 8, add, 0)
    for i in range(extras):
        piece = table[arrive_rows + 1, i]
        pieces[piece] = pieces[piece] - 0.5 * own[i % 8]


def sum_kernel(table, arrived, pieces_in, out, pieces):
    places = arrived.shape[0]
    for i in range(places):
        piece = table[i // LANES, i % LANES]
        pieces[piece] = pieces[piece] + arrived[i]
    for i in range(places):
        out[i] = pieces[table[i // LANES, i % LANES]]


def own_back_kernel(table, pieces, out, *, arrive_rows):
    for b in range(out.shape[0]):
        out[b] = pieces[table[arrive_rows, b]]


def unpack_kernel(info, back, own, out, stage, rows, sems):
    halves = []
    for i in range(2):
        for b in range(TILES * i, TILES * (i + 1)):
            stage[pl.ds(8 * b, 8), :] = jnp.where(info[2, b] != 0, own[b], back[info[1, b]])
        for j in range(TILES):
            rows[8 * i : 8 * i + 8, j * LANES : (j + 1) * LANES] = stage[
                pl.ds(j + i * 8 * TILES, 8, stride=TILES), :
            ]
        half = pl.ds(8 * i, 8)
        halves.append(pltpu.make_async_copy(rows.at[half], out.at[half], sems.at[i]))
        halves[i].start()
    for half in halves:
        half.wait()


def f32(*shape):
    return jax.ShapeDtypeStruct(shape, jnp.float32)


def body(concentration, diffusion, velocity, levels, grid_signs, owner_list, slot_list):
    dom_count = lax.axis_size("dom")
    devices = lax.axis_size("grid") * dom_count
    rows = concentration.shape[1]
    conc = concentration[0]
    dif = diffusion[0]
    blocks = owner_list.shape[1]
    capacity = 2 * blocks // devices

    spread = pl.pallas_call(
        spread_kernel,
        out_shape=jax.ShapeDtypeStruct((devices * COPIES, blocks), jnp.int32),
        in_specs=[VM],
        out_specs=VM,
        compiler_params=params(),
        name="spread_keys",
        cost_estimate=pl.CostEstimate(flops=10**10, transcendentals=0, bytes_accessed=0),
    )(owner_list * SLOTS + slot_list)
    spread, conc, dif = lax.optimization_barrier((spread, conc, dif))
    keys = lax.all_to_all(
        spread.reshape(devices, COPIES, blocks),
        ("grid", "dom"),
        split_axis=0,
        concat_axis=0,
        tiled=True,
    ).reshape(devices * COPIES, blocks)

    up = [(i, i + 1) for i in range(dom_count - 1)]
    down = [(i + 1, i) for i in range(dom_count - 1)]
    low_rows, high_rows = pl.pallas_call(
        halo_kernel,
        out_shape=(f32(3, TILES, LANES), f32(5, TILES, LANES)),
        in_specs=[VM, VM],
        out_specs=(VM, VM),
        compiler_params=params(),
        name="halo_rows",
    )(conc, dif)
    low = lax.ppermute(low_rows, "dom", up)
    high = lax.ppermute(high_rows, "dom", down)

    balanced = capacity >= 8 and devices * SLOTS % LANES == 0 and devices <= 64
    info_shape = jax.ShapeDtypeStruct((8, blocks), jnp.int32)
    if balanced:
        key_rows = devices * SLOTS // LANES
        assigned, info, good = pl.pallas_call(
            functools.partial(
                balance_kernel, devices=devices, capacity=capacity // 2, full=capacity
            ),
            out_shape=(f32(key_rows, LANES), info_shape, jax.ShapeDtypeStruct((1,), jnp.int32)),
            in_specs=[VM],
            out_specs=(VM, VM, HBM),
            scratch_shapes=[
                pltpu.VMEM((key_rows * (devices + 8), LANES), jnp.float32),
                pltpu.VMEM((key_rows * (devices + 8), LANES), jnp.float32),
                pltpu.VMEM((key_rows, LANES), jnp.float32),
                pltpu.SMEM((1,), jnp.int32),
                pltpu.SemaphoreType.DMA,
            ],
            compiler_params=params(),
            name="balance",
            cost_estimate=SMALL,
        )(keys)
    else:
        info = pl.pallas_call(
            functools.partial(owner_places_kernel, devices=devices, capacity=capacity),
            out_shape=info_shape,
            in_specs=[VM],
            out_specs=VM,
            compiler_params=params(),
            name="places",
            cost_estimate=SMALL,
        )(keys)

    low, high, info = lax.optimization_barrier((low, high, info))
    slots = capacity // 2 if balanced else capacity
    extras = 8 * len(row_zero_uses(dom_count)) if balanced else 0
    blocks_in, lead, outgoing = pl.pallas_call(
        functools.partial(rows_kernel, extras=extras),
        out_shape=(
            f32(rows * TILES, LANES),
            f32(TILES, LANES),
            f32(devices * slots, 8, LANES),
        ),
        in_specs=[SM, SM, HBM, VM, VM, VM, VM, VM],
        out_specs=(VM, VM, VM),
        scratch_shapes=[
            pltpu.VMEM((TILES + 2 * PAD, 24, LANES), jnp.float32),
            pltpu.VMEM((TILES + 2 * PAD, 24, LANES), jnp.float32),
            pltpu.VMEM((TILES, 24, LANES), jnp.float32),
            pltpu.VMEM((TILES + 1, 16, LANES), jnp.float32),
            pltpu.VMEM((TILES + 64, 16, LANES), jnp.float32),
            pltpu.SMEM((8, blocks), jnp.int32),
            pltpu.SMEM((1,), jnp.int32),
            pltpu.SemaphoreType.DMA((2,)),
        ],
        compiler_params=params(),
        name="rows",
        cost_estimate=SMALL,
    )(levels, velocity, grid_signs, info, conc, dif, low, high)

    def fixed():
        coarse = None
        for offset, period in row_zero_uses(dom_count):
            pairs = [
                (d, d + offset) for d in range(dom_count) if has_use(d, offset, period, dom_count)
            ]
            part = lax.ppermute(lead, "dom", pairs)
            coarse = part if coarse is None else coarse + part
        return pl.pallas_call(
            fix_kernel,
            out_shape=f32(rows * TILES, LANES),
            in_specs=[SM, VM, VM],
            out_specs=VM,
            scratch_shapes=[
                pltpu.VMEM((TILES + 1, 8, LANES), jnp.float32),
                pltpu.VMEM((TILES + 64, 8, LANES), jnp.float32),
                pltpu.VMEM((8 * TILES, LANES), jnp.float32),
            ],
            compiler_params=params(),
            name="fix_row",
        )(levels, coarse, blocks_in)

    def route(own, outgoing, slots, extras, tables):
        pieces = MOST_KEYS if balanced else SLOTS
        arrive_rows = flat_rows(devices, slots)

        def exchange(x):
            return lax.all_to_all(
                x.reshape(devices, slots * 8, LANES),
                ("grid", "dom"),
                split_axis=0,
                concat_axis=0,
                tiled=True,
            ).reshape(devices * slots, 8, LANES)

        own = own.reshape(blocks, 8, LANES)
        if outgoing is None:
            outgoing = pl.pallas_call(
                scatter_kernel,
                out_shape=f32(devices * slots, 8, LANES),
                in_specs=[SM, VM],
                out_specs=VM,
                compiler_params=params(),
                name="scatter",
            )(info, own)
        arrived = exchange(outgoing)
        table = pl.pallas_call(
            functools.partial(
                table_kernel,
                devices=devices,
                capacity=slots,
                pieces=pieces,
                balanced=balanced,
                more=extras > 0,
            ),
            out_shape=jax.ShapeDtypeStruct((8, LANES), jnp.int32),
            in_specs=[VM] * len(tables),
            out_specs=VM,
            scratch_shapes=[pltpu.VMEM((devices, blocks), jnp.float32)] * 2,
            compiler_params=params(),
            name="piece_table",
        )(*tables)
        all_pieces = f32(pieces + 8, 8, LANES)
        started = pl.pallas_call(
            functools.partial(own_sum_kernel, arrive_rows=arrive_rows, extras=extras),
            out_shape=all_pieces,
            in_specs=[SM, VM],
            out_specs=VM,
            compiler_params=params(),
            name="sum_own",
        )(table, own)
        returned, summed = pl.pallas_call(
            sum_kernel,
            out_shape=(f32(devices * slots, 8, LANES), all_pieces),
            in_specs=[SM, VM, VM],
            out_specs=(VM, VM),
            input_output_aliases={2: 1},
            compiler_params=params(),
            name="sum_arrived",
        )(table, arrived, started)
        own_back = pl.pallas_call(
            functools.partial(own_back_kernel, arrive_rows=arrive_rows),
            out_shape=f32(blocks, 8, LANES),
            in_specs=[SM, VM],
            out_specs=VM,
            compiler_params=params(),
            name="own_back",
        )(table, summed)
        return exchange(returned), own_back

    def unpacked(back, own_back):
        return pl.pallas_call(
            unpack_kernel,
            out_shape=f32(rows, TILES * LANES),
            in_specs=[SM, VM, VM],
            out_specs=HBM,
            scratch_shapes=[
                pltpu.VMEM((16 * TILES, LANES), jnp.float32),
                pltpu.VMEM((16, TILES * LANES), jnp.float32),
                pltpu.SemaphoreType.DMA((2,)),
            ],
            compiler_params=params(),
            name="unpack",
        )(info, back, own_back)

    if balanced:
        brought = route(blocks_in, outgoing, slots, extras, (keys, assigned))
        combined = lax.cond(
            good[0] != 0,
            lambda: unpacked(*brought),
            lambda: unpacked(*route(fixed(), None, capacity, 0, (keys, assigned))),
        )
    else:
        combined = unpacked(*route(fixed(), None, capacity, 0, (keys,)))
    return combined[None]


def solution(mesh):
    return jax.shard_map(
        body,
        mesh=mesh,
        in_specs=(
            P("grid", "dom", None),
            P("grid", "dom", None),
            P(),
            P("grid", None),
            P("grid"),
            P(("grid", "dom"), None),
            P(("grid", "dom"), None),
        ),
        out_specs=P("grid", "dom", None),
        check_vma=False,
    )
```

```python
import functools

import jax
import jax.numpy as jnp
from jax import lax
from jax.experimental import pallas as pl
from jax.experimental.pallas import tpu as pltpu
from jax.sharding import PartitionSpec as P

LR = 13
BLK = 1024
SLOTS = 64
LANES = 128
TILES = 2**LR // LANES
PAD = 9
BESIDE = 4
COPIES = 8
MOST_KEYS = 256
VMEM_LIMIT = 48 * 1024 * 1024


def params():
    return pltpu.CompilerParams(vmem_limit_bytes=VMEM_LIMIT)


SMALL = pl.CostEstimate(flops=0, transcendentals=0, bytes_accessed=0)
VM = pl.BlockSpec(memory_space=pltpu.VMEM)
HBM = pl.BlockSpec(memory_space=pltpu.HBM)
SM = pl.BlockSpec(memory_space=pltpu.SMEM)


def grid_step(
    first_bits, second_bits, weights, valid, src, dst, dif, lane_two, lane_three, beside, state
):
    lane = lax.broadcasted_iota(jnp.int32, (1, LANES), 1)
    first_mask = (1 << first_bits) - 1
    stride_two = 1 << first_bits
    stride_three = 1 << (first_bits + second_bits)
    two_mask = stride_three - 1
    up_one = (lane & first_mask) != first_mask
    down_one = (lane & first_mask) != 0

    def rolled(tile, stride):
        return pltpu.roll(tile, LANES - stride, 1), pltpu.roll(tile, stride, 1)

    def neighbours(j, x, nxt, stride, in_lanes, carry):
        if not in_lanes:
            step = stride // LANES
            return src[PAD + j + step], src[PAD + j - step], carry
        up_here, down_here, down_last = carry
        up_next, down_next = rolled(nxt, stride)
        ahead = jnp.where(lane < LANES - stride, up_here, up_next)
        before = jnp.where(lane >= stride, down_here, down_last)
        return ahead, before, (up_next, down_next, down_here)

    def one_tile(j, carry):
        x, carry_two, carry_three = carry
        nxt = src[PAD + j + 1]
        ahead = jnp.where(up_one, pltpu.roll(x, LANES - 1, 1), 0.0)
        before = jnp.where(down_one, pltpu.roll(x, 1, 1), 0.0)
        total = ahead + before
        drift = weights[0] * (ahead - before)
        ahead, before, carry_two = neighbours(j, x, nxt, stride_two, lane_two, carry_two)
        node = (j * LANES + lane) & two_mask
        ahead = jnp.where(node < stride_three - stride_two, ahead, 0.0)
        before = jnp.where(node >= stride_two, before, 0.0)
        total = total + (ahead + before)
        drift = drift + weights[1] * (ahead - before)
        ahead, before, carry_three = neighbours(j, x, nxt, stride_three, lane_three, carry_three)
        total = total + (ahead + before)
        drift = drift + weights[2] * (ahead - before)
        ahead = pltpu.roll(x, 23, 0)
        before = pltpu.roll(x, 1, 0)
        total = total + (ahead + before)
        drift = drift + weights[3] * (ahead - before)
        new = x + dif[j] * (total - 8.0 * x) - drift
        dst[PAD + j] = jnp.where(valid, new, 0.0)
        return nxt, carry_two, carry_three

    def start(stride, in_lanes):
        if not in_lanes:
            return ()
        up_here, down_here = rolled(src[PAD], stride)
        return up_here, down_here, jnp.zeros((24, LANES), jnp.float32)

    turns = BESIDE if beside is not None else 8
    tiles = TILES // turns

    def several(k, carry):
        tile_carry, state = carry
        if beside is not None:
            state = beside(k, state)
        for i in range(tiles):
            tile_carry = one_tile(tiles * k + i, tile_carry)
        return tile_carry, state

    first = (src[PAD], start(stride_two, lane_two), start(stride_three, lane_three))
    return lax.fori_loop(0, turns, several, (first, state))[1]


def bit_ends(levels, q):
    one = levels[0, 0]
    two = one + levels[0, 1]
    begin = jnp.where(q < one, 0, jnp.where(q < two, one, two))
    end = jnp.where(q < one, one, jnp.where(q < two, two, LR))
    return begin, end


def lane_matrix(levels):
    rows = lax.broadcasted_iota(jnp.int32, (LANES, LANES), 0)
    lane = lax.broadcasted_iota(jnp.int32, (LANES, LANES), 1)
    own = (rows == lane).astype(jnp.float32)
    nxt = jnp.zeros((LANES, LANES), jnp.float32)
    for q in range(7):
        begin, end = bit_ends(levels, q)
        below = (1 << q) - (1 << begin)
        above = (1 << jnp.minimum(end, 7)) - (2 << q)
        here = ((lane & below) == 0) & ((lane & (1 << q)) != 0)
        full = (lane & above) == above
        ahead = pltpu.roll(own, LANES - (1 << q), 1)
        before = pltpu.roll(own, 1 << q, 1)
        half = jnp.where(here, -0.5, 0.0)
        nxt = nxt + jnp.where(full & (end > 7), half * ahead, 0.0)
        own = own + half * (before + jnp.where(full, 0.0, ahead))
    return jnp.concatenate([own, nxt], axis=0)


def exact_dot(left, right):
    total = None
    for _ in range(3):
        part = left.astype(jnp.bfloat16)
        term = jnp.dot(part, right, preferred_element_type=jnp.float32)
        total = term if total is None else total + term
        left = left - part.astype(jnp.float32)
    return total


def surplus_rows(levels, factor, x, y, matrix, stage):
    rows = x.shape[1]
    x[TILES] = jnp.zeros((rows, LANES), jnp.float32)
    y[pl.ds(0, 32)] = jnp.zeros((32, rows, LANES), jnp.float32)
    y[pl.ds(32 + TILES, 32)] = jnp.zeros((32, rows, LANES), jnp.float32)

    _, end_six = bit_ends(levels, 6)
    mask_six = (1 << (jnp.maximum(end_six, 7) - 7)) - 1
    chunk = 16
    matrix = matrix.astype(jnp.bfloat16)
    for j0 in range(0, TILES, chunk):
        own = x[pl.ds(j0, chunk)].reshape(chunk * rows, LANES)
        nxt = jnp.concatenate(
            [
                jnp.where(((j0 + i) & mask_six) == mask_six, 0.0, x[j0 + i + 1])
                for i in range(chunk)
            ],
            axis=0,
        )
        res = exact_dot(jnp.concatenate([own, nxt], axis=1), matrix)
        y[pl.ds(32 + j0, chunk)] = res.reshape(chunk, rows, LANES)

    lane = lax.broadcasted_iota(jnp.int32, (1, LANES), 1)
    for q in range(7, LR):
        t = 1 << (q - 7)
        begin, end = bit_ends(levels, q)
        low_lane = 128 - (1 << jnp.minimum(begin, 7))
        half = jnp.where((lane & low_lane) == 0, -0.5, 0.0)
        below = t - (1 << (jnp.maximum(begin, 7) - 7))
        above = (1 << (end - 7)) - 2 * t
        for j in range(TILES):
            if j & t:
                mine = jnp.where((j & below) == 0, half, 0.0)
                ahead_on = jnp.where((j & above) == above, 0.0, 1.0)
                y[32 + j] = y[32 + j] + mine * (y[32 + j - t] + ahead_on * y[32 + j + t])

    for j in range(TILES):
        tile = factor * y[32 + j]
        for i in range(0, rows, 8):
            stage[pl.ds(j + i * TILES, 8, stride=TILES), :] = tile[i : i + 8]


def rows_kernel(*refs, extras, balance):
    levels, velocity, sign_in, keys, conc, dif_in, low, high, *refs = refs
    if balance is not None:
        two, table_in, loads_in, *refs = refs
    out, lead, outgoing, *refs = refs
    balancing = None
    if balance is None:
        info_in = keys
    else:
        assigned, info_in, good_out, *refs = refs
    u_a, u_b, dif, x, y, info, sign, sems, *refs = refs
    places = pltpu.make_async_copy(info_in, info, sems.at[0])
    if balance is None:
        places.start()
    else:
        table, loads, good = refs
        table[...] = table_in[...]
        balancing = Balancing(keys, None, two, table, **balance)
        tell = pltpu.make_async_copy(good, good_out, sems.at[2])
    signs = pltpu.make_async_copy(sign_in, sign, sems.at[1])
    signs.start()
    place = lax.axis_index("dom")
    count = lax.axis_size("dom")
    zeros = jnp.zeros((PAD, 24, LANES), jnp.float32)
    for ref in (u_a, u_b):
        ref[pl.ds(0, PAD)] = zeros
        ref[pl.ds(PAD + TILES, PAD)] = zeros
    tail = jnp.zeros((8, LANES), jnp.float32)
    for j in range(TILES):
        cols = pl.ds(j * LANES, LANES)
        u_a[PAD + j, 0:16] = conc[:, cols]
        u_a[PAD + j, 16:24] = tail
        dif[j, 0:16] = 0.1 * dif_in[:, cols]
        dif[j, 16:24] = tail
    for i in range(3):
        u_a[PAD : PAD + TILES, 16 + i] = high[i]
    for i in range(2):
        u_a[PAD : PAD + TILES, 22 + i] = low[i]
        dif[:, 16 + i] = 0.1 * high[3 + i]
    dif[:, 23] = 0.1 * low[2]
    row = lax.broadcasted_iota(jnp.int32, (24, LANES), 0)
    valid = (row < 16) | ((row < 20) & (place < count - 1)) | ((row >= 20) & (place > 0))
    weights = [0.1 * velocity[d] for d in range(4)]
    first_bits = levels[0, 0]
    second_bits = levels[0, 1]

    def both(lane_two, lane_three):
        def step(src, dst, beside, state):
            return grid_step(
                first_bits,
                second_bits,
                weights,
                valid,
                src,
                dst,
                dif,
                lane_two,
                lane_three,
                beside,
                state,
            )

        def run():
            if balancing is None:
                step(u_a, u_b, None, 0)
                step(u_b, u_a, None, 0)
            else:
                load = step(u_a, u_b, balancing.later_round, loads_in[...])
                loads[...] = step(u_b, u_a, balancing.later_round, load)

        return run

    small_two = first_bits < 7
    small_three = first_bits + second_bits < 7
    pl.when(small_three)(both(True, True))
    pl.when(small_two & jnp.logical_not(small_three))(both(True, False))
    pl.when(jnp.logical_not(small_two))(both(False, False))
    if balancing is not None:
        balancing.finish(loads[...], assigned, info_in, good, tell)
        places.start()
    signs.wait()
    factor = sign[0].astype(jnp.float32)
    lead[...] = factor * u_a[PAD : PAD + TILES, 0]
    for j in range(TILES):
        tile = u_a[PAD + j]
        for p in range(4):
            s = 1 << p
            around = pltpu.roll(tile, 24 - s, 0) + pltpu.roll(tile, s, 0)
            hit = ((row & (2 * s - 1)) == s) & (row < 16)
            tile = tile - 0.5 * jnp.where(hit, around, 0.0)
        x[j] = tile[0:16]
    next_lead = u_a[PAD : PAD + TILES, 16]
    x[0:TILES, 0] = x[0:TILES, 0] - jnp.where((place & 1) == 1, 0.5, 0.0) * next_lead
    surplus_rows(levels, factor, x, y, lane_matrix(levels), out)
    places.wait()
    send_blocks(info, lambda b: out[8 * b : 8 * b + 8, :], outgoing, extras)
    if balancing is not None:
        tell.wait()


def send_blocks(info, block, outgoing, extras):
    use = info[3, 0]
    for b in range(info.shape[1]):
        outgoing[info[0, b] * use] = block(b)
    for i in range(extras):
        outgoing[info[4, i] * use] = -0.5 * block(i % 8)


def fix_kernel(levels, coarse, blocks, out, x, y, stage):
    x[...] = jnp.zeros_like(x)
    x[0:TILES, 0] = coarse[...]
    surplus_rows(levels, 1.0, x, y, lane_matrix(levels), stage)
    out[...] = blocks[...]
    out[0:TILES, :] = blocks[0:TILES, :] - 0.5 * stage[0:TILES, :]


def scatter_kernel(info, blocks, out):
    for b in range(blocks.shape[0]):
        out[info[0, b]] = blocks[b]


def row_zero_uses(dom_count):
    uses = []
    distance = 1
    while distance < dom_count:
        uses.append((distance, 2 * distance))
        if distance > 1 and dom_count > 2 * distance:
            uses.append((-distance, 2 * distance))
        distance *= 2
    return uses


def has_use(place, offset, period, dom_count):
    return (place % period == 0) & (place + offset >= 0) & (place + offset < dom_count)


def extra_entries(values, dom_count, fill):
    devices, size = values.shape
    place = lax.broadcasted_iota(jnp.int32, (devices, size), 0) % dom_count
    lane = lax.broadcasted_iota(jnp.int32, (devices, size), 1)
    res = jnp.full((devices, size), fill, values.dtype)
    for t, (offset, period) in enumerate(row_zero_uses(dom_count)):
        cut = offset % devices
        moved = jnp.concatenate([values[cut:], values[:cut]], axis=0)
        moved = pltpu.roll(moved, 8 * t, 1) if t else moved
        hit = (lane >= 8 * t) & (lane < 8 * t + 8) & has_use(place, offset, period, dom_count)
        res = jnp.where(hit, moved, res)
    return res


def key_parts(keys, rows):
    owner = keys // SLOTS
    slot = keys % SLOTS
    row = owner % rows
    lane = slot + SLOTS * (owner // rows)
    return owner, slot, lane, row, (row + slot) % rows


def hot(index, count):
    which = lax.broadcasted_iota(jnp.int32, (count, index.shape[1]), 0)
    return jnp.where(which == index, 1.0, 0.0)


def dot_rows(left, right):
    return lax.dot_general(
        left.astype(jnp.bfloat16),
        right.astype(jnp.bfloat16),
        (((1,), (1,)), ((), ())),
        preferred_element_type=jnp.float32,
    )


def dot_plain(left, right):
    return jnp.dot(
        left.astype(jnp.bfloat16), right.astype(jnp.bfloat16), preferred_element_type=jnp.float32
    )


def mixed(handler, lane, row):
    x = (handler * 40503 + lane * 30011 + row * 52711) & 0xFFFF
    x = ((x ^ (x >> 7)) * 9973) & 0xFFFF
    x = ((x ^ (x >> 5)) * 12347) & 0xFFFF
    return (x >> 8).astype(jnp.float32) * (1.0 / 256.0)


def handlers_of(assigned, lane, row):
    return jnp.sum(
        hot(row, assigned.shape[0]) * dot_plain(assigned, hot(lane, LANES)), axis=0, keepdims=True
    )


def all_keys(keys):
    return keys[pl.ds(0, keys.shape[0] // COPIES, stride=COPIES), :]


def keys_of(keys, device):
    return keys[pl.ds(device * COPIES, 1), :]


def device_number():
    return lax.axis_index("grid") * lax.axis_size("dom") + lax.axis_index("dom")


def write_places(info, handler, extra, ok, me, devices, capacity):
    size = handler.shape[1]
    first = lax.broadcasted_iota(jnp.int32, (size, size), 0)
    second = lax.broadcasted_iota(jnp.int32, (size, size), 1)
    earlier = jnp.where(first < second, 1.0, 0.0)

    def placed(which, ahead):
        taken = hot(which.astype(jnp.int32), devices)
        rank = jnp.sum(taken * (dot_plain(taken, earlier) + ahead), axis=0, keepdims=True)
        place = which.astype(jnp.int32) * capacity + rank.astype(jnp.int32)
        stays = (which == me.astype(jnp.float32)) | (which < 0.0)
        return jnp.where(stays, me * capacity, place), stays, taken

    send, stays, taken = placed(handler, 0.0)
    send_extra, _, _ = placed(extra, jnp.sum(taken, axis=1, keepdims=True))
    kept = jnp.where(stays, 1, 0)
    flag = jnp.broadcast_to(ok, kept.shape).astype(jnp.int32)
    info[...] = jnp.concatenate([send, send, kept, flag, send_extra, flag, flag, flag], axis=0)


def spread_kernel(keys, out):
    out[...] = jnp.broadcast_to(keys[...], out.shape)


def halo_kernel(conc, dif, low, high):
    last = conc.shape[0] - 1
    for j in range(TILES):
        cols = slice(j * LANES, (j + 1) * LANES)
        for i, (ref, row) in enumerate(((conc, last - 1), (conc, last), (dif, last))):
            low[i, j : j + 1, :] = ref[row : row + 1, cols]
        for i, (ref, row) in enumerate(((conc, 0), (conc, 1), (conc, 2), (dif, 0), (dif, 1))):
            high[i, j : j + 1, :] = ref[row : row + 1, cols]


def owner_places_kernel(keys, info, *, devices, capacity):
    me = device_number()
    owner = (keys_of(keys, me) // SLOTS).astype(jnp.float32)
    none = jnp.full(owner.shape, -1.0, jnp.float32)
    write_places(info, owner, none, jnp.int32(0), me, devices, capacity)


def first_rounds_kernel(keys, two, table, loads, one, *, devices, capacity, full):
    rows = devices * SLOTS // LANES
    deep = devices + 8
    keys_all = all_keys(keys)
    _, _, lane_all, row_one, row_two = key_parts(keys_all, rows)
    dom_count = lax.axis_size("dom")
    lane_more, one_more, two_more = [
        extra_entries(v, dom_count, -1) for v in (lane_all, row_one, row_two)
    ]

    def counted(one_row, two_row, lane_row):
        both = jnp.concatenate([hot(one_row, rows), hot(two_row, rows)], axis=0)
        return dot_rows(both, hot(lane_row, LANES))

    for d in range(devices):
        pick = slice(d, d + 1)
        counts = counted(row_one[pick], row_two[pick], lane_all[pick])
        place = d % dom_count
        if any(has_use(place, *use, dom_count) for use in row_zero_uses(dom_count)):
            counts = counts + counted(one_more[pick], two_more[pick], lane_more[pick])
        one[pl.ds(d, rows, stride=deep), :] = counts[:rows]
        two[pl.ds(d, rows, stride=deep), :] = counts[rows:]
    for r in range(rows):
        spare = pl.ds(r * deep + devices, deep - devices)
        one[spare, :] = jnp.ones((deep - devices, LANES), jnp.float32)
        two[spare, :] = jnp.ones((deep - devices, LANES), jnp.float32)
    balancing = Balancing(
        keys, one, two, table, devices=devices, capacity=capacity, full=full
    )
    loads[...] = lax.fori_loop(0, BESIDE, balancing.first_round, balancing.no_load())
    balancing.rearrange()


class Balancing:
    def __init__(self, keys, one, two, table, *, devices, capacity, full):
        self.keys, self.one, self.two, self.table = keys, one, two, table
        self.devices, self.capacity, self.full = devices, capacity, full
        self.rows = devices * SLOTS // LANES
        self.deep = devices + 8

    def own(self):
        square = (self.devices, self.deep)
        sender = lax.broadcasted_iota(jnp.int32, square, 1)
        own = lax.broadcasted_iota(jnp.int32, square, 0) == sender
        return own | (sender >= self.devices), sender

    def no_load(self):
        return jnp.zeros((self.devices, self.deep), jnp.float32)

    def price(self, load, steep):
        value = jnp.exp2(load * 0.3785) + steep * jnp.maximum(load - (self.capacity - 1), 0.0)
        return jnp.where(self.own()[0], 0.0, value)

    def settle(self, counts_ref, group, first, load, number):
        devices, deep, table = self.devices, self.deep, self.table
        base = number * group
        counts = jnp.concatenate(
            [
                counts_ref[pl.ds(pl.multiple_of((base + i) * deep, 8), deep), :]
                for i in range(group)
            ],
            axis=1,
        )
        shape = (devices, group * LANES)
        handler = lax.broadcasted_iota(jnp.int32, shape, 0)
        column = lax.broadcasted_iota(jnp.int32, shape, 1)
        handler_f = handler.astype(jnp.float32)
        cost = dot_plain(self.price(load, 4.0 if first else 16.0), counts)
        was = None
        if not first:
            old = jnp.concatenate([table[pl.ds(base + i, 1), :] for i in range(group)], axis=1)
            was = handler_f == old
            cost = jnp.where(was, dot_plain(self.price(load - 1.0, 16.0), counts) - 5.0, cost)
        noise = 0.5 * mixed(handler, column % LANES, base + column // LANES)
        ranked = jnp.floor((jnp.minimum(cost, 4000.0) + noise) * 64.0) * devices + handler_f
        least = jnp.min(ranked, axis=0, keepdims=True)
        chosen = least - jnp.floor(least * (1.0 / devices)) * devices
        for i in range(group):
            table[pl.ds(base + i, 1), :] = chosen[:, i * LANES : (i + 1) * LANES]
        change = jnp.where(handler_f == chosen, 1.0, 0.0)
        if not first:
            change = change - jnp.where(was, 1.0, 0.0)
        return load + dot_rows(change, counts)

    def first_round(self, number, load):
        return self.settle(self.one, self.rows // BESIDE, True, load, number)

    def later_round(self, number, load):
        return self.settle(self.two, self.rows // BESIDE, False, load, number)

    def from_row(self):
        spot = lax.broadcasted_iota(jnp.int32, (self.rows, LANES), 0)
        lane = lax.broadcasted_iota(jnp.int32, (self.rows, LANES), 1)
        return (spot + self.rows - (lane % SLOTS) % self.rows) % self.rows, lane

    def rearrange(self):
        from_row, _ = self.from_row()
        moved = jnp.zeros((self.rows, LANES), jnp.float32)
        for r in range(self.rows):
            moved = jnp.where(from_row == r, self.table[r : r + 1, :], moved)
        self.table[...] = moved

    def finish(self, load, assigned, info, good, tell):
        devices, capacity, rows, keys = self.devices, self.capacity, self.rows, self.keys
        own, sender = self.own()

        def sweep(group, load):
            return lax.fori_loop(
                0, rows // group, lambda i, x: self.settle(self.two, group, False, x, i), load
            )

        def worst(load):
            return jnp.max(jnp.where(own, 0.0, load))

        def again(state):
            count, _, load = state
            load = lax.cond(count == 0, lambda x: sweep(4, x), lambda x: sweep(2, x), load)
            return count + 1, worst(load), load

        _, most, load = lax.while_loop(
            lambda state: (state[0] < 6) & (state[1] > capacity), again, (0, worst(load), load)
        )
        ok = (most <= capacity) & (jnp.max(jnp.where(sender < devices, 0.0, load)) <= MOST_KEYS)
        good[0] = ok.astype(jnp.int32)
        tell.start()
        from_row, lane = self.from_row()
        owner = (from_row + rows * (lane // SLOTS)).astype(jnp.float32)
        final = jnp.where(ok, self.table[...], owner)
        assigned[...] = final
        me = device_number()

        def found(device):
            _, _, lane_row, _, row = key_parts(keys_of(keys, device), rows)
            return handlers_of(final, lane_row, row)

        dom_count = lax.axis_size("dom")
        place = lax.axis_index("dom")
        column = lax.broadcasted_iota(jnp.int32, (1, keys.shape[1]), 1)
        extra = jnp.full((1, keys.shape[1]), -1.0, jnp.float32)
        for t, (offset, period) in enumerate(row_zero_uses(dom_count)):
            there = has_use(place, offset, period, dom_count)
            moved = found(jnp.where(there, me + offset, me))
            moved = pltpu.roll(moved, 8 * t, 1) if t else moved
            extra = jnp.where((column >= 8 * t) & (column < 8 * t + 8) & there, moved, extra)
        size = jnp.where(ok, capacity, self.full)
        write_places(info, found(me), extra, ok.astype(jnp.int32), me, devices, size)


def flat_rows(devices, capacity):
    return -(-devices * capacity // LANES)


def table_kernel(*refs, devices, capacity, pieces, balanced, more):
    if balanced:
        keys, assigned, out, handlers, numbers = refs
        me = device_number()
        rows = devices * SLOTS // LANES
        table = assigned[...]
        mine = jnp.where(table == me.astype(jnp.float32), 1.0, 0.0)
        first = lax.broadcasted_iota(jnp.int32, (LANES, LANES), 0)
        second = lax.broadcasted_iota(jnp.int32, (LANES, LANES), 1)
        in_row = dot_plain(mine, jnp.where(first < second, 1.0, 0.0))
        upper = lax.broadcasted_iota(jnp.int32, (rows, rows), 0)
        lower = lax.broadcasted_iota(jnp.int32, (rows, rows), 1)
        above = dot_plain(jnp.where(lower < upper, 1.0, 0.0), mine)
        number = in_row + jnp.sum(above, axis=1, keepdims=True)
        both = jnp.concatenate([table, jnp.where(mine > 0.0, number, 0.0)], axis=0)
        _, _, lane_all, _, row_all = key_parts(all_keys(keys), rows)
        for d in range(devices):
            at = slice(d, d + 1)
            found = dot_plain(both, hot(lane_all[at], LANES))
            pick = hot(row_all[at], rows)
            handlers[at, :] = jnp.sum(pick * found[:rows], axis=0, keepdims=True)
            numbers[at, :] = jnp.sum(pick * found[rows:], axis=0, keepdims=True)
        piece = numbers[...].astype(jnp.int32)
    else:
        keys, out, handlers, numbers = refs
        me = device_number()
        handlers[...] = (all_keys(keys) // SLOTS).astype(jnp.float32)
        piece = all_keys(keys) % SLOTS
    size = piece.shape[1]
    mine = handlers[...] == me.astype(jnp.float32)
    sender = lax.broadcasted_iota(jnp.int32, (devices, size), 0)
    first = lax.broadcasted_iota(jnp.int32, (size, size), 0)
    second = lax.broadcasted_iota(jnp.int32, (size, size), 1)
    earlier = jnp.where(first <= second, 1.0, 0.0)
    column = lax.broadcasted_iota(jnp.int32, (devices, LANES), 1)

    def ranked(hits, ahead):
        count = jnp.where(hits, 1.0, 0.0)
        return dot_plain(count, earlier) + ahead, jnp.sum(count, axis=1, keepdims=True)

    rank, total = ranked(mine, 0.0)
    groups = [(mine, rank, piece)]
    if more:
        dom_count = lax.axis_size("dom")
        mine_more = extra_entries(handlers[...], dom_count, -1.0) == me.astype(jnp.float32)
        rank_more, _ = ranked(mine_more, total)
        groups.append((mine_more, rank_more, extra_entries(piece, dom_count, 0)))
    lines = [jnp.zeros((devices, LANES), jnp.int32) for _ in range(flat_rows(devices, capacity))]
    spot = lax.broadcasted_iota(jnp.int32, (devices, LANES), 0) * capacity
    for r in range(capacity):
        at = jnp.zeros((devices, 1), jnp.int32)
        for hits, ranks, piece_of in groups:
            hit = hits & (sender != me) & (ranks == r + 1.0)
            at = at + jnp.sum(jnp.where(hit, piece_of - pieces, 0), axis=1, keepdims=True)
        for i in range(len(lines)):
            lines[i] = jnp.where(column + LANES * i == spot + r, at, lines[i])
    lines = [jnp.sum(line, axis=0, keepdims=True) for line in lines]
    for hits, _, piece_of in groups:
        stays = hits & (sender == me)
        lines.append(jnp.sum(jnp.where(stays, piece_of - pieces, 0), axis=0, keepdims=True))
    lines += [jnp.zeros((1, LANES), jnp.int32)] * (8 - len(lines))
    out[...] = jnp.concatenate(lines, axis=0) + pieces


def own_sum_kernel(table, own, pieces, *, arrive_rows, extras):
    zero = jnp.zeros((8, LANES), jnp.float32)

    def clear(k, carry):
        for i in range(8):
            pieces[8 * k + i] = zero
        return carry

    lax.fori_loop(0, pieces.shape[0] // 8, clear, 0)

    def add(k, carry):
        for i in range(8):
            piece = table[arrive_rows, 8 * k + i]
            pieces[piece] = pieces[piece] + own[8 * k + i]
        return carry

    lax.fori_loop(0, own.shape[0] // 8, add, 0)
    for i in range(extras):
        piece = table[arrive_rows + 1, i]
        pieces[piece] = pieces[piece] - 0.5 * own[i % 8]


def sum_kernel(table, arrived, pieces_in, out, pieces):
    places = arrived.shape[0]
    for i in range(places):
        piece = table[i // LANES, i % LANES]
        pieces[piece] = pieces[piece] + arrived[i]
    for i in range(places):
        out[i] = pieces[table[i // LANES, i % LANES]]


def own_back_kernel(table, pieces, out, *, arrive_rows):
    for b in range(out.shape[0]):
        out[b] = pieces[table[arrive_rows, b]]


def unpack_kernel(info, back, own, out, stage, rows, sems):
    halves = []
    for i in range(2):
        for b in range(TILES * i, TILES * (i + 1)):
            stage[pl.ds(8 * b, 8), :] = jnp.where(info[2, b] != 0, own[b], back[info[1, b]])
        for j in range(TILES):
            rows[8 * i : 8 * i + 8, j * LANES : (j + 1) * LANES] = stage[
                pl.ds(j + i * 8 * TILES, 8, stride=TILES), :
            ]
        half = pl.ds(8 * i, 8)
        halves.append(pltpu.make_async_copy(rows.at[half], out.at[half], sems.at[i]))
        halves[i].start()
    for half in halves:
        half.wait()


def f32(*shape):
    return jax.ShapeDtypeStruct(shape, jnp.float32)


def body(concentration, diffusion, velocity, levels, grid_signs, owner_list, slot_list):
    dom_count = lax.axis_size("dom")
    devices = lax.axis_size("grid") * dom_count
    rows = concentration.shape[1]
    conc = concentration[0]
    dif = diffusion[0]
    blocks = owner_list.shape[1]
    capacity = 2 * blocks // devices

    spread = pl.pallas_call(
        spread_kernel,
        out_shape=jax.ShapeDtypeStruct((devices * COPIES, blocks), jnp.int32),
        in_specs=[VM],
        out_specs=VM,
        compiler_params=params(),
        name="spread_keys",
        cost_estimate=pl.CostEstimate(flops=10**10, transcendentals=0, bytes_accessed=0),
    )(owner_list * SLOTS + slot_list)
    spread, conc, dif = lax.optimization_barrier((spread, conc, dif))
    keys = lax.all_to_all(
        spread.reshape(devices, COPIES, blocks),
        ("grid", "dom"),
        split_axis=0,
        concat_axis=0,
        tiled=True,
    ).reshape(devices * COPIES, blocks)

    up = [(i, i + 1) for i in range(dom_count - 1)]
    down = [(i + 1, i) for i in range(dom_count - 1)]
    low_rows, high_rows = pl.pallas_call(
        halo_kernel,
        out_shape=(f32(3, TILES, LANES), f32(5, TILES, LANES)),
        in_specs=[VM, VM],
        out_specs=(VM, VM),
        compiler_params=params(),
        name="halo_rows",
    )(conc, dif)
    low = lax.ppermute(low_rows, "dom", up)
    high = lax.ppermute(high_rows, "dom", down)

    balanced = capacity >= 8 and devices * SLOTS % LANES == 0 and devices <= 64
    info_shape = jax.ShapeDtypeStruct((8, blocks), jnp.int32)
    slots = capacity // 2 if balanced else capacity
    extras = 8 * len(row_zero_uses(dom_count)) if balanced else 0
    row_shapes = (f32(rows * TILES, LANES), f32(TILES, LANES), f32(devices * slots, 8, LANES))
    row_scratch = [
        pltpu.VMEM((TILES + 2 * PAD, 24, LANES), jnp.float32),
        pltpu.VMEM((TILES + 2 * PAD, 24, LANES), jnp.float32),
        pltpu.VMEM((TILES, 24, LANES), jnp.float32),
        pltpu.VMEM((TILES + 1, 16, LANES), jnp.float32),
        pltpu.VMEM((TILES + 64, 16, LANES), jnp.float32),
        pltpu.SMEM((8, blocks), jnp.int32),
        pltpu.SMEM((1,), jnp.int32),
        pltpu.SemaphoreType.DMA((3,)),
    ]
    row_call = functools.partial(
        pl.pallas_call,
        in_specs=[SM, SM, HBM, VM, VM, VM, VM, VM] + [VM] * 3 * balanced,
        compiler_params=params(),
        name="rows",
        cost_estimate=SMALL,
    )
    if balanced:
        key_rows = devices * SLOTS // LANES
        balance = dict(devices=devices, capacity=slots, full=capacity)
        begun = pl.pallas_call(
            functools.partial(first_rounds_kernel, **balance),
            out_shape=(
                f32(key_rows * (devices + 8), LANES),
                f32(key_rows, LANES),
                f32(devices, devices + 8),
            ),
            in_specs=[VM],
            out_specs=(VM, VM, VM),
            scratch_shapes=[pltpu.VMEM((key_rows * (devices + 8), LANES), jnp.float32)],
            compiler_params=params(),
            name="first_rounds",
            cost_estimate=SMALL,
        )(keys)
        low, high, *begun = lax.optimization_barrier((low, high, *begun))
        blocks_in, lead, outgoing, assigned, info, good = row_call(
            functools.partial(
                rows_kernel,
                extras=extras,
                balance=balance,
            ),
            out_shape=row_shapes
            + (f32(key_rows, LANES), info_shape, jax.ShapeDtypeStruct((1,), jnp.int32)),
            out_specs=(VM, VM, VM, VM, VM, HBM),
            scratch_shapes=row_scratch
            + [
                pltpu.VMEM((key_rows, LANES), jnp.float32),
                pltpu.VMEM((devices, devices + 8), jnp.float32),
                pltpu.SMEM((1,), jnp.int32),
            ],
        )(levels, velocity, grid_signs, keys, conc, dif, low, high, *begun)
    else:
        info = pl.pallas_call(
            functools.partial(owner_places_kernel, devices=devices, capacity=capacity),
            out_shape=info_shape,
            in_specs=[VM],
            out_specs=VM,
            compiler_params=params(),
            name="places",
        )(keys)
        blocks_in, lead, outgoing = row_call(
            functools.partial(rows_kernel, extras=extras, balance=None),
            out_shape=row_shapes,
            out_specs=(VM, VM, VM),
            scratch_shapes=row_scratch,
        )(levels, velocity, grid_signs, info, conc, dif, low, high)

    def fixed():
        coarse = None
        for offset, period in row_zero_uses(dom_count):
            pairs = [
                (d, d + offset) for d in range(dom_count) if has_use(d, offset, period, dom_count)
            ]
            part = lax.ppermute(lead, "dom", pairs)
            coarse = part if coarse is None else coarse + part
        return pl.pallas_call(
            fix_kernel,
            out_shape=f32(rows * TILES, LANES),
            in_specs=[SM, VM, VM],
            out_specs=VM,
            scratch_shapes=[
                pltpu.VMEM((TILES + 1, 8, LANES), jnp.float32),
                pltpu.VMEM((TILES + 64, 8, LANES), jnp.float32),
                pltpu.VMEM((8 * TILES, LANES), jnp.float32),
            ],
            compiler_params=params(),
            name="fix_row",
        )(levels, coarse, blocks_in)

    def route(own, outgoing, slots, extras, tables):
        pieces = MOST_KEYS if balanced else SLOTS
        arrive_rows = flat_rows(devices, slots)

        def exchange(x):
            return lax.all_to_all(
                x.reshape(devices, slots * 8, LANES),
                ("grid", "dom"),
                split_axis=0,
                concat_axis=0,
                tiled=True,
            ).reshape(devices * slots, 8, LANES)

        own = own.reshape(blocks, 8, LANES)
        if outgoing is None:
            outgoing = pl.pallas_call(
                scatter_kernel,
                out_shape=f32(devices * slots, 8, LANES),
                in_specs=[SM, VM],
                out_specs=VM,
                compiler_params=params(),
                name="scatter",
            )(info, own)
        arrived = exchange(outgoing)
        table = pl.pallas_call(
            functools.partial(
                table_kernel,
                devices=devices,
                capacity=slots,
                pieces=pieces,
                balanced=balanced,
                more=extras > 0,
            ),
            out_shape=jax.ShapeDtypeStruct((8, LANES), jnp.int32),
            in_specs=[VM] * len(tables),
            out_specs=VM,
            scratch_shapes=[pltpu.VMEM((devices, blocks), jnp.float32)] * 2,
            compiler_params=params(),
            name="piece_table",
        )(*tables)
        all_pieces = f32(pieces + 8, 8, LANES)
        started = pl.pallas_call(
            functools.partial(own_sum_kernel, arrive_rows=arrive_rows, extras=extras),
            out_shape=all_pieces,
            in_specs=[SM, VM],
            out_specs=VM,
            compiler_params=params(),
            name="sum_own",
        )(table, own)
        returned, summed = pl.pallas_call(
            sum_kernel,
            out_shape=(f32(devices * slots, 8, LANES), all_pieces),
            in_specs=[SM, VM, VM],
            out_specs=(VM, VM),
            input_output_aliases={2: 1},
            compiler_params=params(),
            name="sum_arrived",
        )(table, arrived, started)
        own_back = pl.pallas_call(
            functools.partial(own_back_kernel, arrive_rows=arrive_rows),
            out_shape=f32(blocks, 8, LANES),
            in_specs=[SM, VM],
            out_specs=VM,
            compiler_params=params(),
            name="own_back",
        )(table, summed)
        return exchange(returned), own_back

    def unpacked(back, own_back):
        return pl.pallas_call(
            unpack_kernel,
            out_shape=f32(rows, TILES * LANES),
            in_specs=[SM, VM, VM],
            out_specs=HBM,
            scratch_shapes=[
                pltpu.VMEM((16 * TILES, LANES), jnp.float32),
                pltpu.VMEM((16, TILES * LANES), jnp.float32),
                pltpu.SemaphoreType.DMA((2,)),
            ],
            compiler_params=params(),
            name="unpack",
        )(info, back, own_back)

    if balanced:
        brought = route(blocks_in, outgoing, slots, extras, (keys, assigned))
        combined = lax.cond(
            good[0] != 0,
            lambda: unpacked(*brought),
            lambda: unpacked(*route(fixed(), None, capacity, 0, (keys, assigned))),
        )
    else:
        combined = unpacked(*route(fixed(), None, capacity, 0, (keys,)))
    return combined[None]


def solution(mesh):
    return jax.shard_map(
        body,
        mesh=mesh,
        in_specs=(
            P("grid", "dom", None),
            P("grid", "dom", None),
            P(),
            P("grid", None),
            P("grid"),
            P(("grid", "dom"), None),
            P(("grid", "dom"), None),
        ),
        out_specs=P("grid", "dom", None),
        check_vma=False,
    )
```

```python
import functools

import jax
import jax.numpy as jnp
from jax import lax
from jax.experimental import pallas as pl
from jax.experimental.pallas import tpu as pltpu
from jax.sharding import PartitionSpec as P

LR = 13
BLK = 1024
SLOTS = 64
LANES = 128
TILES = 2**LR // LANES
PAD = 9
BESIDE = 4
COPIES = 8
MOST_KEYS = 256
VMEM_LIMIT = 48 * 1024 * 1024


def params():
    return pltpu.CompilerParams(vmem_limit_bytes=VMEM_LIMIT)


SMALL = pl.CostEstimate(flops=0, transcendentals=0, bytes_accessed=0)
VM = pl.BlockSpec(memory_space=pltpu.VMEM)
HBM = pl.BlockSpec(memory_space=pltpu.HBM)
SM = pl.BlockSpec(memory_space=pltpu.SMEM)


def grid_step(
    first_bits, second_bits, weights, valid, src, dst, dif, lane_two, lane_three, beside, state
):
    lane = lax.broadcasted_iota(jnp.int32, (1, LANES), 1)
    first_mask = (1 << first_bits) - 1
    stride_two = 1 << first_bits
    stride_three = 1 << (first_bits + second_bits)
    two_mask = stride_three - 1
    up_one = (lane & first_mask) != first_mask
    down_one = (lane & first_mask) != 0

    def rolled(tile, stride):
        return pltpu.roll(tile, LANES - stride, 1), pltpu.roll(tile, stride, 1)

    def neighbours(j, x, nxt, stride, in_lanes, carry):
        if not in_lanes:
            step = stride // LANES
            return src[PAD + j + step], src[PAD + j - step], carry
        up_here, down_here, down_last = carry
        up_next, down_next = rolled(nxt, stride)
        ahead = jnp.where(lane < LANES - stride, up_here, up_next)
        before = jnp.where(lane >= stride, down_here, down_last)
        return ahead, before, (up_next, down_next, down_here)

    def one_tile(j, carry):
        x, carry_two, carry_three = carry
        nxt = src[PAD + j + 1]
        ahead = jnp.where(up_one, pltpu.roll(x, LANES - 1, 1), 0.0)
        before = jnp.where(down_one, pltpu.roll(x, 1, 1), 0.0)
        total = ahead + before
        drift = weights[0] * (ahead - before)
        ahead, before, carry_two = neighbours(j, x, nxt, stride_two, lane_two, carry_two)
        node = (j * LANES + lane) & two_mask
        ahead = jnp.where(node < stride_three - stride_two, ahead, 0.0)
        before = jnp.where(node >= stride_two, before, 0.0)
        total = total + (ahead + before)
        drift = drift + weights[1] * (ahead - before)
        ahead, before, carry_three = neighbours(j, x, nxt, stride_three, lane_three, carry_three)
        total = total + (ahead + before)
        drift = drift + weights[2] * (ahead - before)
        ahead = pltpu.roll(x, 23, 0)
        before = pltpu.roll(x, 1, 0)
        total = total + (ahead + before)
        drift = drift + weights[3] * (ahead - before)
        new = x + dif[j] * (total - 8.0 * x) - drift
        dst[PAD + j, 0:16] = new[0:16]
        dst[PAD + j, 16:24] = jnp.where(valid, new[16:24], 0.0)
        return nxt, carry_two, carry_three

    def start(stride, in_lanes):
        if not in_lanes:
            return ()
        up_here, down_here = rolled(src[PAD], stride)
        return up_here, down_here, jnp.zeros((24, LANES), jnp.float32)

    turns = BESIDE if beside is not None else 8
    tiles = TILES // turns

    def several(k, carry):
        tile_carry, state = carry
        if beside is not None:
            state = beside(k, state)
        for i in range(tiles):
            tile_carry = one_tile(tiles * k + i, tile_carry)
        return tile_carry, state

    first = (src[PAD], start(stride_two, lane_two), start(stride_three, lane_three))
    return lax.fori_loop(0, turns, several, (first, state))[1]


def bit_ends(levels, q):
    one = levels[0, 0]
    two = one + levels[0, 1]
    begin = jnp.where(q < one, 0, jnp.where(q < two, one, two))
    end = jnp.where(q < one, one, jnp.where(q < two, two, LR))
    return begin, end


def lane_matrix(levels):
    rows = lax.broadcasted_iota(jnp.int32, (LANES, LANES), 0)
    lane = lax.broadcasted_iota(jnp.int32, (LANES, LANES), 1)
    own = (rows == lane).astype(jnp.float32)
    nxt = jnp.zeros((LANES, LANES), jnp.float32)
    for q in range(7):
        begin, end = bit_ends(levels, q)
        below = (1 << q) - (1 << begin)
        above = (1 << jnp.minimum(end, 7)) - (2 << q)
        here = ((lane & below) == 0) & ((lane & (1 << q)) != 0)
        full = (lane & above) == above
        ahead = pltpu.roll(own, LANES - (1 << q), 1)
        before = pltpu.roll(own, 1 << q, 1)
        half = jnp.where(here, -0.5, 0.0)
        nxt = nxt + jnp.where(full & (end > 7), half * ahead, 0.0)
        own = own + half * (before + jnp.where(full, 0.0, ahead))
    return jnp.concatenate([own, nxt], axis=0)


def exact_dot(left, right):
    total = None
    for _ in range(3):
        part = left.astype(jnp.bfloat16)
        term = jnp.dot(part, right, preferred_element_type=jnp.float32)
        total = term if total is None else total + term
        left = left - part.astype(jnp.float32)
    return total


def surplus_rows(levels, factor, x, y, matrix, stage):
    rows = x.shape[1]
    x[TILES] = jnp.zeros((rows, LANES), jnp.float32)
    y[pl.ds(0, 32)] = jnp.zeros((32, rows, LANES), jnp.float32)
    y[pl.ds(32 + TILES, 32)] = jnp.zeros((32, rows, LANES), jnp.float32)

    _, end_six = bit_ends(levels, 6)
    mask_six = (1 << (jnp.maximum(end_six, 7) - 7)) - 1
    chunk = 16
    matrix = matrix.astype(jnp.bfloat16)
    for j0 in range(0, TILES, chunk):
        own = x[pl.ds(j0, chunk)].reshape(chunk * rows, LANES)
        nxt = jnp.concatenate(
            [
                jnp.where(((j0 + i) & mask_six) == mask_six, 0.0, x[j0 + i + 1])
                for i in range(chunk)
            ],
            axis=0,
        )
        res = exact_dot(jnp.concatenate([own, nxt], axis=1), matrix)
        y[pl.ds(32 + j0, chunk)] = res.reshape(chunk, rows, LANES)

    lane = lax.broadcasted_iota(jnp.int32, (1, LANES), 1)
    for q in range(7, LR):
        t = 1 << (q - 7)
        begin, end = bit_ends(levels, q)
        low_lane = 128 - (1 << jnp.minimum(begin, 7))
        half = jnp.where((lane & low_lane) == 0, -0.5, 0.0)
        below = t - (1 << (jnp.maximum(begin, 7) - 7))
        above = (1 << (end - 7)) - 2 * t
        for j in range(TILES):
            if j & t:
                mine = jnp.where((j & below) == 0, half, 0.0)
                ahead_on = jnp.where((j & above) == above, 0.0, 1.0)
                y[32 + j] = y[32 + j] + mine * (y[32 + j - t] + ahead_on * y[32 + j + t])

    for j in range(TILES):
        tile = factor * y[32 + j]
        for i in range(0, rows, 8):
            stage[pl.ds(j + i * TILES, 8, stride=TILES), :] = tile[i : i + 8]


def rows_kernel(*refs, extras, balance):
    levels, velocity, sign_in, keys, conc, dif_in, low, high, *refs = refs
    if balance is not None:
        two, table_in, loads_in, *refs = refs
    out, lead, outgoing, *refs = refs
    balancing = None
    if balance is None:
        info_in = keys
    else:
        assigned, info_in, good_out, *refs = refs
    u_a, u_b, dif, x, y, info, sign, sems, *refs = refs
    places = pltpu.make_async_copy(info_in, info, sems.at[0])
    if balance is None:
        places.start()
    else:
        table, loads, good = refs
        table[...] = table_in[...]
        balancing = Balancing(keys, None, two, table, **balance)
        tell = pltpu.make_async_copy(good, good_out, sems.at[2])
    signs = pltpu.make_async_copy(sign_in, sign, sems.at[1])
    signs.start()
    place = lax.axis_index("dom")
    count = lax.axis_size("dom")
    zeros = jnp.zeros((PAD, 24, LANES), jnp.float32)
    for ref in (u_a, u_b):
        ref[pl.ds(0, PAD)] = zeros
        ref[pl.ds(PAD + TILES, PAD)] = zeros
    tail = jnp.zeros((8, LANES), jnp.float32)
    for j in range(TILES):
        cols = pl.ds(j * LANES, LANES)
        u_a[PAD + j, 0:16] = conc[:, cols]
        u_a[PAD + j, 16:24] = tail
        dif[j, 0:16] = 0.1 * dif_in[:, cols]
        dif[j, 16:24] = tail
    for i in range(3):
        u_a[PAD : PAD + TILES, 16 + i] = high[i]
    for i in range(2):
        u_a[PAD : PAD + TILES, 22 + i] = low[i]
        dif[:, 16 + i] = 0.1 * high[3 + i]
    dif[:, 23] = 0.1 * low[2]
    row = lax.broadcasted_iota(jnp.int32, (24, LANES), 0)
    halo_row = lax.broadcasted_iota(jnp.int32, (8, LANES), 0)
    valid = ((halo_row < 4) & (place < count - 1)) | ((halo_row >= 4) & (place > 0))
    weights = [0.1 * velocity[d] for d in range(4)]
    first_bits = levels[0, 0]
    second_bits = levels[0, 1]

    def both(lane_two, lane_three):
        def step(src, dst, beside, state):
            return grid_step(
                first_bits,
                second_bits,
                weights,
                valid,
                src,
                dst,
                dif,
                lane_two,
                lane_three,
                beside,
                state,
            )

        def run():
            if balancing is None:
                step(u_a, u_b, None, 0)
                step(u_b, u_a, None, 0)
            else:
                load = step(u_a, u_b, balancing.later_round, loads_in[...])
                loads[...] = step(u_b, u_a, balancing.later_round, load)

        return run

    small_two = first_bits < 7
    small_three = first_bits + second_bits < 7
    pl.when(small_three)(both(True, True))
    pl.when(small_two & jnp.logical_not(small_three))(both(True, False))
    pl.when(jnp.logical_not(small_two))(both(False, False))
    if balancing is not None:
        balancing.finish(loads[...], assigned, info_in, good, tell)
        places.start()
    signs.wait()
    factor = sign[0].astype(jnp.float32)
    lead[...] = factor * u_a[PAD : PAD + TILES, 0]
    for j in range(TILES):
        tile = u_a[PAD + j]
        for p in range(4):
            s = 1 << p
            around = pltpu.roll(tile, 24 - s, 0) + pltpu.roll(tile, s, 0)
            hit = ((row & (2 * s - 1)) == s) & (row < 16)
            tile = tile - 0.5 * jnp.where(hit, around, 0.0)
        x[j] = tile[0:16]
    next_lead = u_a[PAD : PAD + TILES, 16]
    x[0:TILES, 0] = x[0:TILES, 0] - jnp.where((place & 1) == 1, 0.5, 0.0) * next_lead
    surplus_rows(levels, factor, x, y, lane_matrix(levels), out)
    places.wait()
    send_blocks(info, lambda b: out[8 * b : 8 * b + 8, :], outgoing, extras)
    if balancing is not None:
        tell.wait()


def send_blocks(info, block, outgoing, extras):
    use = info[3, 0]
    for b in range(info.shape[1]):
        outgoing[info[0, b] * use] = block(b)
    for i in range(extras):
        outgoing[info[4, i] * use] = -0.5 * block(i % 8)


def fix_kernel(levels, coarse, blocks, out, x, y, stage):
    x[...] = jnp.zeros_like(x)
    x[0:TILES, 0] = coarse[...]
    surplus_rows(levels, 1.0, x, y, lane_matrix(levels), stage)
    out[...] = blocks[...]
    out[0:TILES, :] = blocks[0:TILES, :] - 0.5 * stage[0:TILES, :]


def scatter_kernel(info, blocks, out):
    for b in range(blocks.shape[0]):
        out[info[0, b]] = blocks[b]


def row_zero_uses(dom_count):
    uses = []
    distance = 1
    while distance < dom_count:
        uses.append((distance, 2 * distance))
        if distance > 1 and dom_count > 2 * distance:
            uses.append((-distance, 2 * distance))
        distance *= 2
    return uses


def has_use(place, offset, period, dom_count):
    return (place % period == 0) & (place + offset >= 0) & (place + offset < dom_count)


def extra_entries(values, dom_count, fill):
    devices, size = values.shape
    place = lax.broadcasted_iota(jnp.int32, (devices, size), 0) % dom_count
    lane = lax.broadcasted_iota(jnp.int32, (devices, size), 1)
    res = jnp.full((devices, size), fill, values.dtype)
    for t, (offset, period) in enumerate(row_zero_uses(dom_count)):
        cut = offset % devices
        moved = jnp.concatenate([values[cut:], values[:cut]], axis=0)
        moved = pltpu.roll(moved, 8 * t, 1) if t else moved
        hit = (lane >= 8 * t) & (lane < 8 * t + 8) & has_use(place, offset, period, dom_count)
        res = jnp.where(hit, moved, res)
    return res


def key_parts(keys, rows):
    owner = keys // SLOTS
    slot = keys % SLOTS
    row = owner % rows
    lane = slot + SLOTS * (owner // rows)
    return owner, slot, lane, row, (row + slot) % rows


def hot(index, count):
    which = lax.broadcasted_iota(jnp.int32, (count, index.shape[1]), 0)
    return jnp.where(which == index, 1.0, 0.0)


def dot_rows(left, right):
    return lax.dot_general(
        left.astype(jnp.bfloat16),
        right.astype(jnp.bfloat16),
        (((1,), (1,)), ((), ())),
        preferred_element_type=jnp.float32,
    )


def dot_plain(left, right):
    return jnp.dot(
        left.astype(jnp.bfloat16), right.astype(jnp.bfloat16), preferred_element_type=jnp.float32
    )


def tie_breakers(devices):
    handler = lax.broadcasted_iota(jnp.int32, (devices, LANES), 0)
    lane = lax.broadcasted_iota(jnp.int32, (devices, LANES), 1)
    x = (handler * 40503 + lane * 30011) & 0xFFFF
    x = ((x ^ (x >> 7)) * 9973) & 0xFFFF
    x = ((x ^ (x >> 5)) * 12347) & 0xFFFF
    return (x >> 8).astype(jnp.float32) * (1.0 / 256.0)


def handlers_of(assigned, lane, row):
    return jnp.sum(
        hot(row, assigned.shape[0]) * dot_plain(assigned, hot(lane, LANES)), axis=0, keepdims=True
    )


def all_keys(keys):
    return keys[pl.ds(0, keys.shape[0] // COPIES, stride=COPIES), :]


def keys_of(keys, device):
    return keys[pl.ds(device * COPIES, 1), :]


def device_number():
    return lax.axis_index("grid") * lax.axis_size("dom") + lax.axis_index("dom")


def write_places(info, handler, extra, ok, me, devices, capacity):
    size = handler.shape[1]
    first = lax.broadcasted_iota(jnp.int32, (size, size), 0)
    second = lax.broadcasted_iota(jnp.int32, (size, size), 1)
    earlier = jnp.where(first < second, 1.0, 0.0)

    def placed(which, ahead):
        taken = hot(which.astype(jnp.int32), devices)
        rank = jnp.sum(taken * (dot_plain(taken, earlier) + ahead), axis=0, keepdims=True)
        place = which.astype(jnp.int32) * capacity + rank.astype(jnp.int32)
        stays = (which == me.astype(jnp.float32)) | (which < 0.0)
        return jnp.where(stays, me * capacity, place), stays, taken

    send, stays, taken = placed(handler, 0.0)
    send_extra, _, _ = placed(extra, jnp.sum(taken, axis=1, keepdims=True))
    kept = jnp.where(stays, 1, 0)
    flag = jnp.broadcast_to(ok, kept.shape).astype(jnp.int32)
    info[...] = jnp.concatenate([send, send, kept, flag, send_extra, flag, flag, flag], axis=0)


def spread_kernel(keys, out):
    out[...] = jnp.broadcast_to(keys[...], out.shape)


def halo_kernel(conc, dif, low, high):
    last = conc.shape[0] - 1
    for j in range(TILES):
        cols = slice(j * LANES, (j + 1) * LANES)
        for i, (ref, row) in enumerate(((conc, last - 1), (conc, last), (dif, last))):
            low[i, j : j + 1, :] = ref[row : row + 1, cols]
        for i, (ref, row) in enumerate(((conc, 0), (conc, 1), (conc, 2), (dif, 0), (dif, 1))):
            high[i, j : j + 1, :] = ref[row : row + 1, cols]


def owner_places_kernel(keys, info, *, devices, capacity):
    me = device_number()
    owner = (keys_of(keys, me) // SLOTS).astype(jnp.float32)
    none = jnp.full(owner.shape, -1.0, jnp.float32)
    write_places(info, owner, none, jnp.int32(0), me, devices, capacity)


def first_rounds_kernel(keys, two, table, loads, one, *, devices, capacity, full):
    rows = devices * SLOTS // LANES
    deep = devices + 8
    keys_all = all_keys(keys)
    _, _, lane_all, row_one, row_two = key_parts(keys_all, rows)
    dom_count = lax.axis_size("dom")
    lane_more, one_more, two_more = [
        extra_entries(v, dom_count, -1) for v in (lane_all, row_one, row_two)
    ]

    def counted(one_row, two_row, lane_row):
        both = jnp.concatenate([hot(one_row, rows), hot(two_row, rows)], axis=0)
        return dot_rows(both, hot(lane_row, LANES))

    for d in range(devices):
        pick = slice(d, d + 1)
        counts = counted(row_one[pick], row_two[pick], lane_all[pick])
        place = d % dom_count
        if any(has_use(place, *use, dom_count) for use in row_zero_uses(dom_count)):
            counts = counts + counted(one_more[pick], two_more[pick], lane_more[pick])
        one[pl.ds(d, rows, stride=deep), :] = counts[:rows]
        two[pl.ds(d, rows, stride=deep), :] = counts[rows:]
    for r in range(rows):
        spare = pl.ds(r * deep + devices, deep - devices)
        one[spare, :] = jnp.ones((deep - devices, LANES), jnp.float32)
        two[spare, :] = jnp.ones((deep - devices, LANES), jnp.float32)
    balancing = Balancing(
        keys, one, two, table, devices=devices, capacity=capacity, full=full
    )
    loads[...] = lax.fori_loop(0, BESIDE, balancing.first_round, balancing.no_load())
    balancing.rearrange()


class Balancing:
    def __init__(self, keys, one, two, table, *, devices, capacity, full):
        self.keys, self.one, self.two, self.table = keys, one, two, table
        self.devices, self.capacity, self.full = devices, capacity, full
        self.rows = devices * SLOTS // LANES
        self.deep = devices + 8
        self.ties = 0.5 * tie_breakers(devices)

    def own(self):
        square = (self.devices, self.deep)
        sender = lax.broadcasted_iota(jnp.int32, square, 1)
        own = lax.broadcasted_iota(jnp.int32, square, 0) == sender
        return own | (sender >= self.devices), sender

    def no_load(self):
        return jnp.zeros((self.devices, self.deep), jnp.float32)

    def price(self, load, steep):
        value = jnp.exp2(load * 0.3785) + steep * jnp.maximum(load - (self.capacity - 1), 0.0)
        return jnp.where(self.own()[0], 0.0, value)

    def settle(self, counts_ref, group, first, load, number):
        devices, deep, table = self.devices, self.deep, self.table
        base = number * group
        counts = jnp.concatenate(
            [
                counts_ref[pl.ds(pl.multiple_of((base + i) * deep, 8), deep), :]
                for i in range(group)
            ],
            axis=1,
        )
        shape = (devices, group * LANES)
        handler = lax.broadcasted_iota(jnp.int32, shape, 0)
        handler_f = handler.astype(jnp.float32)
        was = None
        if first:
            cost = dot_plain(self.price(load, 4.0), counts)
        else:
            old = jnp.concatenate([table[pl.ds(base + i, 1), :] for i in range(group)], axis=1)
            was = handler_f == old
            prices = jnp.concatenate([self.price(load, 16.0), self.price(load - 1.0, 16.0)], axis=0)
            costs = dot_plain(prices, counts)
            cost = jnp.where(was, costs[devices:] - 5.0, costs[:devices])
        noise = jnp.concatenate(
            [pltpu.roll(self.ties, (base + i) * 37 % LANES, 1) for i in range(group)], axis=1
        )
        ranked = jnp.floor((jnp.minimum(cost, 4000.0) + noise) * 64.0) * devices + handler_f
        least = jnp.min(ranked, axis=0, keepdims=True)
        chosen = least - jnp.floor(least * (1.0 / devices)) * devices
        for i in range(group):
            table[pl.ds(base + i, 1), :] = chosen[:, i * LANES : (i + 1) * LANES]
        change = jnp.where(handler_f == chosen, 1.0, 0.0)
        if not first:
            change = change - jnp.where(was, 1.0, 0.0)
        return load + dot_rows(change, counts)

    def first_round(self, number, load):
        return self.settle(self.one, self.rows // BESIDE, True, load, number)

    def later_round(self, number, load):
        return self.settle(self.two, self.rows // BESIDE, False, load, number)

    def from_row(self):
        spot = lax.broadcasted_iota(jnp.int32, (self.rows, LANES), 0)
        lane = lax.broadcasted_iota(jnp.int32, (self.rows, LANES), 1)
        return (spot + self.rows - (lane % SLOTS) % self.rows) % self.rows, lane

    def rearrange(self):
        from_row, _ = self.from_row()
        moved = jnp.zeros((self.rows, LANES), jnp.float32)
        for r in range(self.rows):
            moved = jnp.where(from_row == r, self.table[r : r + 1, :], moved)
        self.table[...] = moved

    def finish(self, load, assigned, info, good, tell):
        devices, capacity, rows, keys = self.devices, self.capacity, self.rows, self.keys
        own, sender = self.own()

        def sweep(group, load):
            return lax.fori_loop(
                0, rows // group, lambda i, x: self.settle(self.two, group, False, x, i), load
            )

        def worst(load):
            too_many = jnp.where((sender >= devices) & (load > MOST_KEYS), 1000.0, 0.0)
            return jnp.max(jnp.where(own, too_many, load))

        def again(state):
            count, _, load = state
            load = lax.cond(count == 0, lambda x: sweep(4, x), lambda x: sweep(2, x), load)
            return count + 1, worst(load), load

        _, most, _ = lax.while_loop(
            lambda state: (state[0] < 6) & (state[1] > capacity), again, (0, worst(load), load)
        )
        ok = most <= capacity
        good[0] = ok.astype(jnp.int32)
        tell.start()
        from_row, lane = self.from_row()
        owner = (from_row + rows * (lane // SLOTS)).astype(jnp.float32)
        final = jnp.where(ok, self.table[...], owner)
        assigned[...] = final
        me = device_number()

        def found(device):
            _, _, lane_row, _, row = key_parts(keys_of(keys, device), rows)
            return handlers_of(final, lane_row, row)

        dom_count = lax.axis_size("dom")
        place = lax.axis_index("dom")
        column = lax.broadcasted_iota(jnp.int32, (1, keys.shape[1]), 1)
        extra = jnp.full((1, keys.shape[1]), -1.0, jnp.float32)
        for t, (offset, period) in enumerate(row_zero_uses(dom_count)):
            there = has_use(place, offset, period, dom_count)
            moved = found(jnp.where(there, me + offset, me))
            moved = pltpu.roll(moved, 8 * t, 1) if t else moved
            extra = jnp.where((column >= 8 * t) & (column < 8 * t + 8) & there, moved, extra)
        size = jnp.where(ok, capacity, self.full)
        write_places(info, found(me), extra, ok.astype(jnp.int32), me, devices, size)


def flat_rows(devices, capacity):
    return -(-devices * capacity // LANES)


def table_kernel(*refs, devices, capacity, pieces, balanced, more):
    if balanced:
        keys, assigned, out, handlers, numbers = refs
        me = device_number()
        rows = devices * SLOTS // LANES
        table = assigned[...]
        mine = jnp.where(table == me.astype(jnp.float32), 1.0, 0.0)
        first = lax.broadcasted_iota(jnp.int32, (LANES, LANES), 0)
        second = lax.broadcasted_iota(jnp.int32, (LANES, LANES), 1)
        in_row = dot_plain(mine, jnp.where(first < second, 1.0, 0.0))
        upper = lax.broadcasted_iota(jnp.int32, (rows, rows), 0)
        lower = lax.broadcasted_iota(jnp.int32, (rows, rows), 1)
        above = dot_plain(jnp.where(lower < upper, 1.0, 0.0), mine)
        number = in_row + jnp.sum(above, axis=1, keepdims=True)
        both = jnp.concatenate([table, jnp.where(mine > 0.0, number, 0.0)], axis=0)
        _, _, lane_all, _, row_all = key_parts(all_keys(keys), rows)
        for d in range(devices):
            at = slice(d, d + 1)
            found = dot_plain(both, hot(lane_all[at], LANES))
            pick = hot(row_all[at], rows)
            handlers[at, :] = jnp.sum(pick * found[:rows], axis=0, keepdims=True)
            numbers[at, :] = jnp.sum(pick * found[rows:], axis=0, keepdims=True)
        piece = numbers[...].astype(jnp.int32)
    else:
        keys, out, handlers, numbers = refs
        me = device_number()
        handlers[...] = (all_keys(keys) // SLOTS).astype(jnp.float32)
        piece = all_keys(keys) % SLOTS
    size = piece.shape[1]
    mine = handlers[...] == me.astype(jnp.float32)
    sender = lax.broadcasted_iota(jnp.int32, (devices, size), 0)
    first = lax.broadcasted_iota(jnp.int32, (size, size), 0)
    second = lax.broadcasted_iota(jnp.int32, (size, size), 1)
    earlier = jnp.where(first <= second, 1.0, 0.0)
    column = lax.broadcasted_iota(jnp.int32, (devices, LANES), 1)

    def ranked(hits, ahead):
        count = jnp.where(hits, 1.0, 0.0)
        return dot_plain(count, earlier) + ahead, jnp.sum(count, axis=1, keepdims=True)

    rank, total = ranked(mine, 0.0)
    groups = [(mine, rank, piece)]
    if more:
        dom_count = lax.axis_size("dom")
        mine_more = extra_entries(handlers[...], dom_count, -1.0) == me.astype(jnp.float32)
        rank_more, _ = ranked(mine_more, total)
        groups.append((mine_more, rank_more, extra_entries(piece, dom_count, 0)))
    lines = [jnp.zeros((devices, LANES), jnp.int32) for _ in range(flat_rows(devices, capacity))]
    spot = lax.broadcasted_iota(jnp.int32, (devices, LANES), 0) * capacity
    for r in range(capacity):
        at = jnp.zeros((devices, 1), jnp.int32)
        for hits, ranks, piece_of in groups:
            hit = hits & (sender != me) & (ranks == r + 1.0)
            at = at + jnp.sum(jnp.where(hit, piece_of - pieces, 0), axis=1, keepdims=True)
        for i in range(len(lines)):
            lines[i] = jnp.where(column + LANES * i == spot + r, at, lines[i])
    lines = [jnp.sum(line, axis=0, keepdims=True) for line in lines]
    for hits, _, piece_of in groups:
        stays = hits & (sender == me)
        lines.append(jnp.sum(jnp.where(stays, piece_of - pieces, 0), axis=0, keepdims=True))
    lines += [jnp.zeros((1, LANES), jnp.int32)] * (8 - len(lines))
    out[...] = jnp.concatenate(lines, axis=0) + pieces


def own_sum_kernel(table, own, pieces, *, arrive_rows, extras):
    zero = jnp.zeros((8, LANES), jnp.float32)

    def clear(k, carry):
        for i in range(8):
            pieces[8 * k + i] = zero
        return carry

    lax.fori_loop(0, pieces.shape[0] // 8, clear, 0)

    def add(k, carry):
        for i in range(8):
            piece = table[arrive_rows, 8 * k + i]
            pieces[piece] = pieces[piece] + own[8 * k + i]
        return carry

    lax.fori_loop(0, own.shape[0] // 8, add, 0)
    for i in range(extras):
        piece = table[arrive_rows + 1, i]
        pieces[piece] = pieces[piece] - 0.5 * own[i % 8]


def part_copies(src, dst, sems):
    size = src.shape[0] // sems.shape[0]
    parts = [pl.ds(k * size, size) for k in range(sems.shape[0])]
    return [pltpu.make_async_copy(src.at[p], dst.at[p], sems.at[k]) for k, p in enumerate(parts)]


def sum_kernel(table, arrived, pieces_in, out, pieces, held, sems):
    places = arrived.shape[0]
    for i in range(places):
        piece = table[i // LANES, i % LANES]
        pieces[piece] = pieces[piece] + arrived[i]
    copies = part_copies(held, out, sems)
    size = places // len(copies)
    for k, copy in enumerate(copies):
        for i in range(k * size, (k + 1) * size):
            held[i] = pieces[table[i // LANES, i % LANES]]
        copy.start()
    for copy in copies:
        copy.wait()


def own_back_kernel(table, pieces, out, *, arrive_rows):
    for b in range(out.shape[0]):
        out[b] = pieces[table[arrive_rows, b]]


def unpack_kernel(info, back, own, out, stage, rows, sems):
    halves = []
    for i in range(2):
        for b in range(TILES * i, TILES * (i + 1)):
            stage[pl.ds(8 * b, 8), :] = jnp.where(info[2, b] != 0, own[b], back[info[1, b]])
        for j in range(TILES):
            rows[8 * i : 8 * i + 8, j * LANES : (j + 1) * LANES] = stage[
                pl.ds(j + i * 8 * TILES, 8, stride=TILES), :
            ]
        half = pl.ds(8 * i, 8)
        halves.append(pltpu.make_async_copy(rows.at[half], out.at[half], sems.at[i]))
        halves[i].start()
    for half in halves:
        half.wait()


def f32(*shape):
    return jax.ShapeDtypeStruct(shape, jnp.float32)


def body(concentration, diffusion, velocity, levels, grid_signs, owner_list, slot_list):
    dom_count = lax.axis_size("dom")
    devices = lax.axis_size("grid") * dom_count
    rows = concentration.shape[1]
    conc = concentration[0]
    dif = diffusion[0]
    blocks = owner_list.shape[1]
    capacity = 2 * blocks // devices

    spread = pl.pallas_call(
        spread_kernel,
        out_shape=jax.ShapeDtypeStruct((devices * COPIES, blocks), jnp.int32),
        in_specs=[VM],
        out_specs=VM,
        compiler_params=params(),
        name="spread_keys",
        cost_estimate=pl.CostEstimate(flops=10**10, transcendentals=0, bytes_accessed=0),
    )(owner_list * SLOTS + slot_list)
    spread, conc, dif = lax.optimization_barrier((spread, conc, dif))
    keys = lax.all_to_all(
        spread.reshape(devices, COPIES, blocks),
        ("grid", "dom"),
        split_axis=0,
        concat_axis=0,
        tiled=True,
    ).reshape(devices * COPIES, blocks)

    up = [(i, i + 1) for i in range(dom_count - 1)]
    down = [(i + 1, i) for i in range(dom_count - 1)]
    low_rows, high_rows = pl.pallas_call(
        halo_kernel,
        out_shape=(f32(3, TILES, LANES), f32(5, TILES, LANES)),
        in_specs=[VM, VM],
        out_specs=(VM, VM),
        compiler_params=params(),
        name="halo_rows",
    )(conc, dif)
    low = lax.ppermute(low_rows, "dom", up)
    high = lax.ppermute(high_rows, "dom", down)

    balanced = capacity >= 8 and devices * SLOTS % LANES == 0 and devices <= 64
    info_shape = jax.ShapeDtypeStruct((8, blocks), jnp.int32)
    slots = capacity // 2 if balanced else capacity
    extras = 8 * len(row_zero_uses(dom_count)) if balanced else 0
    row_shapes = (f32(rows * TILES, LANES), f32(TILES, LANES), f32(devices * slots, 8, LANES))
    row_scratch = [
        pltpu.VMEM((TILES + 2 * PAD, 24, LANES), jnp.float32),
        pltpu.VMEM((TILES + 2 * PAD, 24, LANES), jnp.float32),
        pltpu.VMEM((TILES, 24, LANES), jnp.float32),
        pltpu.VMEM((TILES + 1, 16, LANES), jnp.float32),
        pltpu.VMEM((TILES + 64, 16, LANES), jnp.float32),
        pltpu.SMEM((8, blocks), jnp.int32),
        pltpu.SMEM((1,), jnp.int32),
        pltpu.SemaphoreType.DMA((3,)),
    ]
    row_call = functools.partial(
        pl.pallas_call,
        in_specs=[SM, SM, HBM, VM, VM, VM, VM, VM] + [VM] * 3 * balanced,
        compiler_params=params(),
        name="rows",
        cost_estimate=SMALL,
    )
    if balanced:
        key_rows = devices * SLOTS // LANES
        balance = dict(devices=devices, capacity=slots, full=capacity)
        begun = pl.pallas_call(
            functools.partial(first_rounds_kernel, **balance),
            out_shape=(
                f32(key_rows * (devices + 8), LANES),
                f32(key_rows, LANES),
                f32(devices, devices + 8),
            ),
            in_specs=[VM],
            out_specs=(VM, VM, VM),
            scratch_shapes=[pltpu.VMEM((key_rows * (devices + 8), LANES), jnp.float32)],
            compiler_params=params(),
            name="first_rounds",
            cost_estimate=SMALL,
        )(keys)
        low, high, *begun = lax.optimization_barrier((low, high, *begun))
        blocks_in, lead, outgoing, assigned, info, good = row_call(
            functools.partial(
                rows_kernel,
                extras=extras,
                balance=balance,
            ),
            out_shape=row_shapes
            + (f32(key_rows, LANES), info_shape, jax.ShapeDtypeStruct((1,), jnp.int32)),
            out_specs=(VM, VM, VM, VM, VM, HBM),
            scratch_shapes=row_scratch
            + [
                pltpu.VMEM((key_rows, LANES), jnp.float32),
                pltpu.VMEM((devices, devices + 8), jnp.float32),
                pltpu.SMEM((1,), jnp.int32),
            ],
        )(levels, velocity, grid_signs, keys, conc, dif, low, high, *begun)
    else:
        info = pl.pallas_call(
            functools.partial(owner_places_kernel, devices=devices, capacity=capacity),
            out_shape=info_shape,
            in_specs=[VM],
            out_specs=VM,
            compiler_params=params(),
            name="places",
        )(keys)
        blocks_in, lead, outgoing = row_call(
            functools.partial(rows_kernel, extras=extras, balance=None),
            out_shape=row_shapes,
            out_specs=(VM, VM, VM),
            scratch_shapes=row_scratch,
        )(levels, velocity, grid_signs, info, conc, dif, low, high)

    def fixed():
        coarse = None
        for offset, period in row_zero_uses(dom_count):
            pairs = [
                (d, d + offset) for d in range(dom_count) if has_use(d, offset, period, dom_count)
            ]
            part = lax.ppermute(lead, "dom", pairs)
            coarse = part if coarse is None else coarse + part
        return pl.pallas_call(
            fix_kernel,
            out_shape=f32(rows * TILES, LANES),
            in_specs=[SM, VM, VM],
            out_specs=VM,
            scratch_shapes=[
                pltpu.VMEM((TILES + 1, 8, LANES), jnp.float32),
                pltpu.VMEM((TILES + 64, 8, LANES), jnp.float32),
                pltpu.VMEM((8 * TILES, LANES), jnp.float32),
            ],
            compiler_params=params(),
            name="fix_row",
        )(levels, coarse, blocks_in)

    def route(own, outgoing, slots, extras, tables):
        pieces = MOST_KEYS if balanced else SLOTS
        arrive_rows = flat_rows(devices, slots)

        def exchange(x):
            return lax.all_to_all(
                x.reshape(devices, slots * 8, LANES),
                ("grid", "dom"),
                split_axis=0,
                concat_axis=0,
                tiled=True,
            ).reshape(devices * slots, 8, LANES)

        own = own.reshape(blocks, 8, LANES)
        if outgoing is None:
            outgoing = pl.pallas_call(
                scatter_kernel,
                out_shape=f32(devices * slots, 8, LANES),
                in_specs=[SM, VM],
                out_specs=VM,
                compiler_params=params(),
                name="scatter",
            )(info, own)
        arrived = exchange(outgoing)
        table = pl.pallas_call(
            functools.partial(
                table_kernel,
                devices=devices,
                capacity=slots,
                pieces=pieces,
                balanced=balanced,
                more=extras > 0,
            ),
            out_shape=jax.ShapeDtypeStruct((8, LANES), jnp.int32),
            in_specs=[VM] * len(tables),
            out_specs=VM,
            scratch_shapes=[pltpu.VMEM((devices, blocks), jnp.float32)] * 2,
            compiler_params=params(),
            name="piece_table",
        )(*tables)
        all_pieces = f32(pieces + 8, 8, LANES)
        started = pl.pallas_call(
            functools.partial(own_sum_kernel, arrive_rows=arrive_rows, extras=extras),
            out_shape=all_pieces,
            in_specs=[SM, VM],
            out_specs=VM,
            compiler_params=params(),
            name="sum_own",
        )(table, own)
        returned, summed = pl.pallas_call(
            sum_kernel,
            out_shape=(f32(devices * slots, 8, LANES), all_pieces),
            in_specs=[SM, VM, VM],
            out_specs=(HBM, VM),
            input_output_aliases={2: 1},
            scratch_shapes=[
                pltpu.VMEM((devices * slots, 8, LANES), jnp.float32),
                pltpu.SemaphoreType.DMA((4,)),
            ],
            compiler_params=params(),
            name="sum_arrived",
        )(table, arrived, started)
        own_back = pl.pallas_call(
            functools.partial(own_back_kernel, arrive_rows=arrive_rows),
            out_shape=f32(blocks, 8, LANES),
            in_specs=[SM, VM],
            out_specs=VM,
            compiler_params=params(),
            name="own_back",
        )(table, summed)
        return exchange(returned), own_back

    def unpacked(back, own_back):
        return pl.pallas_call(
            unpack_kernel,
            out_shape=f32(rows, TILES * LANES),
            in_specs=[SM, VM, VM],
            out_specs=HBM,
            scratch_shapes=[
                pltpu.VMEM((16 * TILES, LANES), jnp.float32),
                pltpu.VMEM((16, TILES * LANES), jnp.float32),
                pltpu.SemaphoreType.DMA((2,)),
            ],
            compiler_params=params(),
            name="unpack",
        )(info, back, own_back)

    if balanced:
        brought = route(blocks_in, outgoing, slots, extras, (keys, assigned))
        combined = lax.cond(
            good[0] != 0,
            lambda: unpacked(*brought),
            lambda: unpacked(*route(fixed(), None, capacity, 0, (keys, assigned))),
        )
    else:
        combined = unpacked(*route(fixed(), None, capacity, 0, (keys,)))
    return combined[None]


def solution(mesh):
    return jax.shard_map(
        body,
        mesh=mesh,
        in_specs=(
            P("grid", "dom", None),
            P("grid", "dom", None),
            P(),
            P("grid", None),
            P("grid"),
            P(("grid", "dom"), None),
            P(("grid", "dom"), None),
        ),
        out_specs=P("grid", "dom", None),
        check_vma=False,
    )
```
